256 devices in a mesh: ctx: 64 (over z, x, core), dp: 4 (over y).
Axes of the slice: x: 4, y: 4, z: 8, core: 2. Of those that a mesh axis runs over, the one named last changes fastest.
Arguments:
- layer_input: bfloat16 [4, 16384, 4096], P('dp', 'ctx'), may hold values from -6 to 6
- queries: bfloat16 [4, 16384, 512], P('dp', 'ctx'), may hold values from -6 to 6
- keys: bfloat16 [4, 16384, 512], P('dp', 'ctx'), may hold values from -6 to 6
- values: bfloat16 [4, 16384, 1024], P('dp', 'ctx'), may hold values from -6 to 6
- grad_out: bfloat16 [4, 16384, 1024], P('dp', 'ctx'), may hold values from -6 to 6
- doc_pos: int32 [4, 16384], P('dp', 'ctx'), may hold values from 0 to 8319, as said below
- w_input: bfloat16 [4096, 4], replicated, may hold values from -0.09375 to 0.09375
- b_input: float32 [4], replicated, may hold values from -8 to -1
- w_forget: bfloat16 [4096, 4], replicated, may hold values from -0.046875 to 0.046875
- b_forget: float32 [4], replicated, may hold values from 3 to 16
Outputs:
- grad_queries: bfloat16 [4, 16384, 512], P('dp', 'ctx')
- grad_keys: bfloat16 [4, 16384, 512], P('dp', 'ctx')
- grad_values: bfloat16 [4, 16384, 1024], P('dp', 'ctx')
- grad_w_input: float32 [4096, 4], replicated
- grad_w_forget: float32 [4096, 4], replicated
The draws below stay inside these ranges and needn't reach their ends.
Inputs may be any that keep to these rules, and one draw needn't show every extreme that they name: doc_pos[b, 0] = 0 and doc_pos[b, t] is either 0 (a new document starts at t) or doc_pos[b, t-1] + 1; each sequence holds 4 documents, and a document always starts at token 8320.
All inputs are finite; a program needn't handle non-finite values.
Results may differ from the reference program's by a relative error of at most 0.004.
Values sent between devices are 32-bit elements; how exact they have to be, the bound alone decides.
No kernel may reach another device: no remote copies, remote signals or barrier semaphores. Data moves between devices by JAX's collectives and lax.ppermute only.
A program may use at most 128 MiB of HBM per device.

```python
import math
import jax
import jax.numpy as jnp
from jax import lax

D = 4096
HEADS = 4
DK = 128
DV = 256
TOK_DEV = 256
TOKENS = 16384
SEQS = 4


def document_cuts(key):
    key = jax.random.fold_in(key, 11)
    first_cut = TOKENS // 2 + TOK_DEV // 2
    middle = (first_cut + TOKENS) // 2
    second_cut = jax.random.randint(jax.random.fold_in(key, 1), (SEQS, 1), first_cut + 3, middle)
    latest_cut = jax.random.randint(jax.random.fold_in(key, 2), (SEQS, 1), middle + 3, TOKENS)
    return jnp.concatenate([jnp.full((SEQS, 1), first_cut, jnp.int32), second_cut.astype(jnp.int32), latest_cut.astype(jnp.int32)], axis=1)


def gate_columns(key):
    return jax.random.truncated_normal(jax.random.fold_in(key, 5), -6.0, 6.0, (D, HEADS), jnp.float32)


def draw_doc_pos(key, part):
    cuts = document_cuts(key)
    positions = jnp.arange(TOKENS, dtype=jnp.int32)
    is_start = jnp.any(positions[None, :, None] == cuts[:, None, :], axis=-1) | (positions[None, :] == 0)
    starts = jnp.where(is_start, positions[None, :], 0).astype(jnp.int32)
    starts = lax.cummax(starts, axis=1)
    return (positions[None, :] - starts).astype(jnp.int32)


def draw_w_input(key, part):
    columns = gate_columns(key)
    return (columns * D ** (-0.5)).astype(jnp.bfloat16)


def draw_layer_input(key, part):
    key = jax.random.fold_in(key, 41)
    drawn = jax.random.truncated_normal(key, -6.0, 6.0, (SEQS, TOKENS, D), jnp.float32)
    return drawn.astype(jnp.bfloat16)


def draw_keys(key, part):
    key = jax.random.fold_in(key, 53)
    drawn = jax.random.truncated_normal(key, -6.0, 6.0, (SEQS, TOKENS, HEADS * DK), jnp.float32)
    return drawn.astype(jnp.bfloat16)


def draw_b_input(key, part):
    key = jax.random.fold_in(key, 23)
    return jax.random.uniform(key, (HEADS,), jnp.float32, -5.0, -1.0)


def draw_b_forget(key, part):
    key = jax.random.fold_in(key, 37)
    return jax.random.uniform(key, (HEADS,), jnp.float32, math.log(30.0), math.log(4.0 * TOKENS))


def block_scale(key, shape, cuts, smallest, largest):
    gain, own = 1.0, jax.random.fold_in(key, 6)
    for dim, blocks in cuts:
        draws = jnp.exp(jax.random.uniform(jax.random.fold_in(own, dim), (blocks,), jnp.float32, smallest / len(cuts), largest / len(cuts)))
        gain = gain * jnp.repeat(draws, shape[dim] // blocks).reshape([-1 if axis == dim else 1 for axis in range(len(shape))])
    return gain


def bell_draw(rng, dims, scale, most, cuts=(), kind=jnp.bfloat16):
    loudness = block_scale(rng, dims, cuts, -0.22, 0.18) if cuts else 1.0
    values = jax.random.normal(rng, dims, jnp.float32) * scale * loudness
    return jnp.minimum(jnp.maximum(values, -most), most).astype(kind)


def setup_inputs(seed: int = 0) -> dict:
    splits = jax.random.split(jax.random.key(seed), 11)
    layer_input = draw_layer_input(jax.random.fold_in(splits[10], 71), 0)
    queries = bell_draw(splits[1], (SEQS, TOKENS, HEADS * DK), 1.0, 6.0, ((0, 4), (1, 64)))
    keys = draw_keys(jax.random.fold_in(splits[10], 71), 0)
    values = bell_draw(splits[3], (SEQS, TOKENS, HEADS * DV), 1.0, 6.0, ((0, 4), (1, 64)))
    grad_out = bell_draw(splits[4], (SEQS, TOKENS, HEADS * DV), 1.0, 6.0, ((0, 4), (1, 64)))
    doc_pos = draw_doc_pos(jax.random.fold_in(splits[10], 71), 0)
    w_input = draw_w_input(jax.random.fold_in(splits[10], 71), 0)
    b_input = draw_b_input(jax.random.fold_in(splits[10], 71), 0)
    w_forget = bell_draw(splits[8], (D, HEADS), (4 * D) ** -0.5, 0.046875)
    b_forget = draw_b_forget(jax.random.fold_in(splits[10], 71), 0)
    return dict(layer_input=layer_input, queries=queries, keys=keys, values=values, grad_out=grad_out, doc_pos=doc_pos, w_input=w_input, b_input=b_input, w_forget=w_forget, b_forget=b_forget)


very_negative = -1e+30

def inner_product(form, *operands):
    return jnp.einsum(form, *operands, precision=lax.Precision.HIGHEST)

def combine_states(former, latter):
    reset_former, total_former, max_former, matrix_former, vector_former = former
    reset_latter, total_latter, max_latter, matrix_latter, vector_latter = latter
    cut = reset_latter > 0.5
    shifted = max_former + total_latter
    new_max = jnp.where(cut, max_latter, jnp.maximum(shifted, max_latter))
    keep_former = jnp.where(cut, 0.0, jnp.exp(shifted - new_max))
    keep_latter = jnp.exp(max_latter - new_max)
    matrix_new = keep_former[:, None, None] * matrix_former + keep_latter[:, None, None] * matrix_latter
    vector_new = keep_former[:, None] * vector_former + keep_latter[:, None] * vector_latter
    return (jnp.maximum(reset_former, reset_latter), total_former + total_latter, new_max, matrix_new, vector_new)

def local_state(key_row_slab, value_row_slab, in_gate, log_cum, doc_count):
    block_total = log_cum[-1]
    key_valid = doc_count == doc_count[-1]
    key_log = jnp.where(key_valid[:, None], block_total[None] - log_cum + in_gate, very_negative)
    state_max = lax.optimization_barrier(jnp.max(key_log, axis=0))
    key_matrix_weight = jnp.exp(key_log - state_max[None])
    memory_matrix_state = inner_product('nx,nxq,nxd->xqd', key_matrix_weight, key_row_slab, value_row_slab)
    vector_state = inner_product('sh,shk->hk', key_matrix_weight, key_row_slab)
    return (block_total, state_max, memory_matrix_state, vector_state)

def block_output(scaled_query, key_row_slab, value_row_slab, in_gate, log_cum, doc_count, state_max, memory_matrix_state, vector_state):
    rows = log_cum.shape[0]
    positions = jnp.arange(rows)
    pair_mask = (positions[:, None] >= positions[None, :]) & (doc_count[:, None] == doc_count[None, :])
    pair_log = jnp.where(pair_mask[None], log_cum.T[:, :, None] - log_cum.T[:, None, :] + in_gate.T[:, None, :], very_negative)
    query_valid = doc_count == 0
    cross_log = jnp.where(query_valid[:, None], log_cum + state_max[None], very_negative)
    row_max = jnp.maximum(lax.optimization_barrier(jnp.max(pair_log, axis=2)).T, cross_log)
    weights = jnp.exp(pair_log - row_max.T[:, :, None])
    scores = inner_product('thk,shk->hts', scaled_query, key_row_slab)
    coupled_scores = scores * weights
    crossing_scale = jnp.exp(cross_log - row_max)
    sums = lax.optimization_barrier(jnp.sum(coupled_scores, axis=2)).T + crossing_scale * inner_product('thk,hk->th', scaled_query, vector_state)
    numerator = inner_product('cxu,ucp->xcp', coupled_scores, value_row_slab) + crossing_scale[:, :, None] * inner_product('scj,cju->scu', scaled_query, memory_matrix_state)
    denom = jnp.maximum(jnp.abs(sums), jnp.exp(-row_max))
    return numerator / denom[:, :, None]

def sequence_output(layer_rows, doc_row, query_wide, key_wide, value_wide, w_in, w_fg, b_input, b_forget):
    count_blocks = TOKENS // TOK_DEV
    in_gate = jnp.dot(layer_rows, w_in, precision=lax.Precision.HIGHEST) + b_input
    forget_pre = jnp.dot(layer_rows, w_fg, precision=lax.Precision.HIGHEST) + b_forget
    log_forget = jax.nn.log_sigmoid(forget_pre).reshape(count_blocks, TOK_DEV, HEADS)
    log_cum = jnp.cumsum(log_forget, axis=1)
    doc_count = jnp.cumsum((doc_row == 0).astype(jnp.int32).reshape(count_blocks, TOK_DEV), axis=1)
    score_scale = DK ** (-0.5)
    scaled_query = query_wide.reshape(count_blocks, TOK_DEV, HEADS, DK) * score_scale
    key_row_slab = key_wide.reshape(count_blocks, TOK_DEV, HEADS, DK)
    value_row_slab = value_wide.reshape(count_blocks, TOK_DEV, HEADS, DV)
    gate_blocks = in_gate.reshape(count_blocks, TOK_DEV, HEADS)

    def advance(carry, block):
        query_block, key_block, value_block, gate_block, cum_block, count_block = block
        result = block_output(query_block, key_block, value_block, gate_block, cum_block, count_block, carry[2], carry[3], carry[4])
        own = local_state(key_block, value_block, gate_block, cum_block, count_block)
        flag = (count_block[-1:] > 0).astype(jnp.float32)
        return (combine_states(carry, (flag,) + own), result)
    start = (jnp.zeros((1,), jnp.float32), jnp.zeros((HEADS,), jnp.float32), jnp.full((HEADS,), very_negative, jnp.float32), jnp.zeros((HEADS, DK, DV), jnp.float32), jnp.zeros((HEADS, DK), jnp.float32))
    final_state, outputs = lax.scan(jax.checkpoint(advance), start, (scaled_query, key_row_slab, value_row_slab, gate_blocks, log_cum, doc_count))
    return outputs.reshape(TOKENS, HEADS * DV)

def reference(layer_input, queries, keys, values, grad_out, doc_pos, w_input, b_input, w_forget, b_forget):
    w_in_wide = w_input.astype(jnp.float32)
    w_fg_wide = w_forget.astype(jnp.float32)

    def one_sequence(pieces):
        layer_rows, query_rows, key_row_slab, value_row_slab, grad_rows, doc_row = pieces

        def forward(query_wide, key_wide, value_wide, w_in, w_fg):
            return sequence_output(layer_rows, doc_row, query_wide, key_wide, value_wide, w_in, w_fg, b_input, b_forget)
        layer_out, pullback = jax.vjp(forward, query_rows.astype(jnp.float32), key_row_slab.astype(jnp.float32), value_row_slab.astype(jnp.float32), w_in_wide, w_fg_wide)
        return pullback(grad_rows.astype(jnp.float32))
    grads = lax.map(one_sequence, (layer_input, queries, keys, values, grad_out, doc_pos))
    return (grads[0].astype(jnp.bfloat16), grads[1].astype(jnp.bfloat16), grads[2].astype(jnp.bfloat16), lax.optimization_barrier(jnp.sum(grads[3], axis=0)), lax.optimization_barrier(jnp.sum(grads[4], axis=0)))
```

```python
import functools

import jax
import jax.numpy as jnp
from jax import lax
from jax.experimental import pallas as pl
from jax.experimental.pallas import tpu as pltpu
from jax.sharding import PartitionSpec as P

NEG = -1e30
BIG = 1e30
F32 = jnp.float32
BF16 = jnp.bfloat16
VMEM = pl.BlockSpec(memory_space=pltpu.VMEM)
SMEM = pl.BlockSpec(memory_space=pltpu.SMEM)


def dot(a, b, ca, cb):
    return lax.dot_general(a, b, (((ca,), (cb,)), ((), ())), preferred_element_type=F32)


def split(x):
    high = x.astype(BF16)
    return high, (x - high.astype(F32)).astype(BF16)


def dot_left(x, b, ca, cb):
    high, low = split(x)
    return dot(high, b, ca, cb) + dot(low, b, ca, cb)


def dot_right(a, x, ca, cb):
    high, low = split(x)
    return dot(a, high, ca, cb) + dot(a, low, ca, cb)


def dot_exact(a, b):
    return lax.dot_general(
        a, b, (((1,), (0,)), ((), ())), precision=lax.Precision.HIGHEST, preferred_element_type=F32
    )


def iota(shape, dim):
    return lax.broadcasted_iota(jnp.int32, shape, dim)


def column_of(rows):
    r, n = rows.shape
    padded = jnp.concatenate([rows, jnp.zeros((128 - r, n), F32)], axis=0)
    return padded.T


def put(acc, col, h):
    return jnp.where(iota(acc.shape, 1) == h, col, acc)


def gates_kernel(
    heads, x_ref, wi_ref, wf_ref, bi_ref, bf_ref, pos_ref, k_ref, v_ref,
    pay_ref, mem_ref, rows_ref, lc_ref, dc_ref, kl_ref,
):
    n = x_ref.shape[0]
    dk = k_ref.shape[1] // heads
    dv = v_ref.shape[1] // heads
    w8 = jnp.concatenate([wi_ref[...].astype(F32), wf_ref[...].astype(F32)], axis=0).astype(BF16)
    gates = dot(w8, x_ref[...], 1, 1)
    row8 = iota(gates.shape, 0)
    for h in range(heads):
        gates = gates + jnp.where(row8 == h, bi_ref[h], 0.0)
        gates = gates + jnp.where(row8 == h + heads, bf_ref[h], 0.0)
    in_gate, forget_pre = gates[:heads], gates[heads:]
    log_forget = jnp.minimum(forget_pre, 0.0) - jnp.log1p(jnp.exp(-jnp.abs(forget_pre)))
    start = (pos_ref[...] == 0).astype(F32)
    stacked = jnp.concatenate([log_forget, start, jnp.zeros((7 - heads, n), F32)], axis=0)
    upto = (iota((n, n), 0) <= iota((n, n), 1)).astype(F32)
    cum = dot_exact(stacked, upto)
    lc_row, dc_row = cum[:heads], cum[heads : heads + 1]
    rows_ref[...] = jnp.concatenate(
        [in_gate, forget_pre, lc_row, dc_row, jnp.zeros((3, n), F32)], axis=0
    )
    ig = column_of(in_gate)
    lc = column_of(lc_row)
    dc = jnp.broadcast_to(dc_row, (128, n)).T
    lc_ref[...] = lc
    dc_ref[...] = dc
    total, last = lc[n - 1 :], dc[n - 1 :]
    key_log = jnp.where(dc == last, total - lc + ig, NEG)
    kl_ref[...] = key_log
    own_max = jnp.max(key_log, axis=0, keepdims=True)
    weight = jnp.exp(key_log - own_max)
    vectors = []
    for h in range(heads):
        weighted = k_ref[:, dk * h : dk * (h + 1)].astype(F32) * weight[:, h : h + 1]
        vectors.append(jnp.sum(weighted, axis=0, keepdims=True))
        memory = dot_left(weighted, v_ref[:, dv * h : dv * (h + 1)], 0, 0)
        mem_ref[dk // 8 * h : dk // 8 * (h + 1)] = memory.reshape(dk // 8, 8, dv)
    cut = jnp.where(last > 0.5, BIG, 0.0)
    tile = jnp.concatenate(
        vectors
        + [own_max, total - cut, ig[:1] - lc[:1], jnp.where(dc[:1] < 0.5, 1.0, 0.0)],
        axis=0,
    )
    pay_ref[...] = jnp.broadcast_to(tile[None], pay_ref.shape)


def pairs_kernel(
    heads, rows_ref, lc_ref, dc_ref, q_ref, k_ref, v_ref, g_ref,
    wl_ref, pc_ref, gv_ref, rm_ref, ls_ref, lg_ref,
):
    n = q_ref.shape[0]
    dk = k_ref.shape[1] // heads
    dv = v_ref.shape[1] // heads
    lc, dc = lc_ref[...], dc_ref[...]
    mask = (iota((n, n), 0) >= iota((n, n), 1)) & (dc[:, :1] == rows_ref[3 * heads : 3 * heads + 1])
    rm = jnp.zeros((n, 128), F32)
    ls, lg = rm, rm
    for h in range(heads):
        offset = rows_ref[h : h + 1] - rows_ref[2 * heads + h : 2 * heads + h + 1]
        pair_log = jnp.where(mask, lc[:, h : h + 1] + offset, NEG)
        row_max = jnp.max(pair_log, axis=1, keepdims=True)
        weight = jnp.exp(pair_log - row_max)
        ks, vs = slice(dk * h, dk * (h + 1)), slice(dv * h, dv * (h + 1))
        coupled = dot(q_ref[:, ks], k_ref[:, ks], 1, 1) * weight
        grad_pair = dot(g_ref[:, vs], v_ref[:, vs], 1, 1)
        wl_ref[h] = weight
        pc_ref[h] = coupled
        gv_ref[h] = grad_pair
        rm = put(rm, row_max, h)
        ls = put(ls, jnp.sum(coupled, axis=1, keepdims=True), h)
        lg = put(lg, jnp.sum(coupled * grad_pair, axis=1, keepdims=True), h)
    rm_ref[...] = rm
    ls_ref[...] = ls
    lg_ref[...] = lg


def shift_down(x, d, fill):
    return jnp.where(iota(x.shape, 0) < d, fill, pltpu.roll(x, d, 0))


def shift_up(x, d, fill):
    size = x.shape[0]
    return jnp.where(iota(x.shape, 0) >= size - d, fill, pltpu.roll(x, size - d, 0))


def dual_kernel(
    heads, scale, me_ref, ag_ref, mem_ref, lc_ref, dc_ref, rm_ref, ls_ref, q_ref, g_ref,
    pay_ref, coef_ref, later_ref, small_ref, cols_ref,
):
    count = ag_ref.shape[0]
    n = q_ref.shape[0]
    dk = q_ref.shape[1] // heads
    dv = g_ref.shape[1] // heads
    me = me_ref[0]
    own_max, total = ag_ref[:, heads, :], ag_ref[:, heads + 1, :]
    first, valid = ag_ref[:, heads + 2, :], ag_ref[:, heads + 3, :]
    row = iota(own_max.shape, 0)
    lane = iota(own_max.shape, 1)
    steps = [1 << i for i in range((count - 1).bit_length())]
    t, m = total, own_max
    for d in steps:
        m = jnp.maximum(shift_down(m, d, NEG) + t, m)
        t = shift_down(t, d, 0.0) + t
    in_max = shift_down(m, 1, NEG)
    dual_max = jnp.where(valid > 0.5, -jnp.maximum(in_max, first), NEG)
    t, r = total, dual_max
    for d in steps:
        r = jnp.maximum(r, t + shift_up(r, d, NEG))
        t = t + shift_up(t, d, 0.0)
    later_max = shift_up(r, 1, NEG)
    my_head = me // (count // heads)
    coefs = (
        jnp.exp(in_max + total - m),
        jnp.exp(own_max - m),
        jnp.exp(total + later_max - r),
        jnp.exp(dual_max - r),
    )
    for i, c in enumerate(coefs):
        mine = jnp.sum(jnp.where(lane == my_head, c, 0.0), axis=1, keepdims=True)
        coef_ref[i] = jnp.broadcast_to(mine, c.shape)

    def at_me(x):
        return jnp.sum(jnp.where(row == me, x, 0.0), axis=0, keepdims=True)

    in_me, later_me, dual_me, total_me = at_me(in_max), at_me(later_max), at_me(dual_max), at_me(total)
    later_row = iota((count, count), 0) < iota((count, count), 1)
    between = dot_exact(later_row.astype(F32), jnp.where(row < me, total, 0.0))
    weight = jnp.where(row < me, jnp.exp(jnp.minimum(own_max + between - in_me, 0.0)), 0.0)
    earlier_row = iota((count, count), 0) > iota((count, count), 1)
    between = dot_exact(earlier_row.astype(F32), jnp.where(row > me, total, 0.0))
    later_ref[...] = jnp.where(
        row > me, jnp.exp(jnp.minimum(dual_max + between - later_me, 0.0)), 0.0
    )
    vectors = [
        jnp.sum(weight[:, h : h + 1] * ag_ref[:, h, :], axis=0, keepdims=True) for h in range(heads)
    ]
    through = jnp.exp(in_me + total_me + later_me)
    small_ref[...] = jnp.concatenate(
        vectors + [later_me, through, jnp.zeros((6 - heads, 128), F32)], axis=0
    )

    lc, open_query = lc_ref[...], dc_ref[...] < 0.5
    cross_log = jnp.where(open_query, lc + in_me, NEG)
    row_max = jnp.maximum(rm_ref[...], cross_log)
    inside = jnp.exp(rm_ref[...] - row_max)
    cross = jnp.exp(cross_log - row_max)
    qn = jnp.zeros((n, 128), F32)
    for h in range(heads):
        along = q_ref[:, dk * h : dk * (h + 1)].astype(F32) * vectors[h]
        qn = put(qn, jnp.sum(along, axis=1, keepdims=True), h)
    sums = scale * (ls_ref[...] * inside + cross * qn)
    floor = jnp.exp(-row_max)
    size = jnp.abs(sums)
    inverse = 1.0 / jnp.maximum(size, floor)
    active = jnp.where(size > floor, jnp.where(sums > 0.0, 1.0, -1.0), 0.0)
    query_weight = jnp.where(open_query, jnp.exp(jnp.minimum(lc - row_max - dual_me, 0.0)), 0.0)
    cols_ref[0] = inside
    cols_ref[1] = cross
    cols_ref[2] = inverse
    cols_ref[3] = active
    cols_ref[4] = query_weight
    cols_ref[5] = qn
    grad_weight = query_weight * inverse * scale
    pay_ref[:, 0:8, :] = mem_ref[...]
    for h in range(heads):
        weighted = g_ref[:, dv * h : dv * (h + 1)].astype(F32) * grad_weight[:, h : h + 1]
        memory = dot_right(q_ref[:, dk * h : dk * (h + 1)], weighted, 0, 0)
        pay_ref[dk // 8 * h : dk // 8 * (h + 1), 8:16, :] = memory.reshape(dk // 8, 8, dv)


def scan_kernel(got_ref, coef_ref, out_ref):
    count = got_ref.shape[0]
    dv = got_ref.shape[2]
    reps = dv // 128

    def wide(i, j):
        return jnp.concatenate([coef_ref[i, pl.ds(j, 1), :]] * reps, axis=1)

    def forward(j, state):
        out_ref[j, 0:8, :] = state
        return wide(0, j) * state + wide(1, j) * got_ref[j, 0:8, :]

    def backward(i, state):
        j = count - 1 - i
        out_ref[j, 8:16, :] = state
        return wide(2, j) * state + wide(3, j) * got_ref[j, 8:16, :]

    def both(i, states):
        return forward(i, states[0]), backward(i, states[1])

    zero = jnp.zeros((8, dv), F32)
    lax.fori_loop(0, count, both, (zero, zero), unroll=8)


def vector_kernel(
    heads, scale, mem_ref, cols_ref, lg_ref, q_ref, g_ref, pay_ref, gt_ref, gc_ref
):
    n = q_ref.shape[0]
    dk = q_ref.shape[1] // heads
    dv = g_ref.shape[1] // heads
    gc = jnp.zeros((n, 128), F32)
    for h in range(heads):
        memory = mem_ref[dk // 8 * h : dk // 8 * (h + 1), 0:8, :].reshape(dk, dv)
        crossing = dot_right(q_ref[:, dk * h : dk * (h + 1)], memory, 1, 0)
        along = g_ref[:, dv * h : dv * (h + 1)].astype(F32) * crossing
        gc = put(gc, jnp.sum(along, axis=1, keepdims=True), h)
    inverse = cols_ref[2]
    gt = -scale * (lg_ref[...] * cols_ref[0] + cols_ref[1] * gc) * inverse * inverse * cols_ref[3]
    gt_ref[...] = gt
    gc_ref[...] = gc
    weight = cols_ref[4] * gt * scale
    vectors = [
        jnp.sum(
            q_ref[:, dk * h : dk * (h + 1)].astype(F32) * weight[:, h : h + 1], axis=0, keepdims=True
        )
        for h in range(heads)
    ]
    pay_ref[...] = jnp.broadcast_to(jnp.concatenate(vectors, axis=0)[None], pay_ref.shape)


def grads_kernel(
    heads, scale, mem_ref, cols_ref, small_ref, kl_ref, gt_ref, gc_ref, wl_ref, pc_ref, gv_ref,
    q_ref, k_ref, v_ref, g_ref,
    gq_ref, gvalue_ref, gk_ref, row_ref, cc_ref, cold_ref, pass_ref,
):
    n = q_ref.shape[0]
    dk = q_ref.shape[1] // heads
    dv = g_ref.shape[1] // heads
    gt, gc = gt_ref[...], gc_ref[...]
    inside, cross, inverse, qn = cols_ref[0], cols_ref[1], cols_ref[2], cols_ref[5]
    key_scale = jnp.exp(kl_ref[...] + small_ref[heads : heads + 1])
    row_part = scale * cross * (inverse * gc + gt * qn)
    column_cross = jnp.zeros((n, 128), F32)
    through = jnp.zeros((1, 128), F32)
    for h in range(heads):
        ks, vs = slice(dk * h, dk * (h + 1)), slice(dv * h, dv * (h + 1))
        one = slice(h, h + 1)
        q, k, v, g = q_ref[:, ks], k_ref[:, ks], v_ref[:, vs], g_ref[:, vs]
        slab = slice(dk // 8 * h, dk // 8 * (h + 1))
        memory = mem_ref[slab, 0:8, :].reshape(dk, dv)
        following = mem_ref[slab, 8:16, :].reshape(dk, dv)
        follow_high, follow_low = split(following)
        factor = inside[:, one] * (inverse[:, one] * gv_ref[h] + gt[:, one])
        pair_grad = factor * pc_ref[h]
        cold_ref[one, :] = scale * jnp.sum(pair_grad, axis=0, keepdims=True)
        row_part = row_part + put(
            jnp.zeros((n, 128), F32), scale * jnp.sum(pair_grad, axis=1, keepdims=True), h
        )
        score_high, score_low = split(factor * wl_ref[h])
        grad_query = dot(score_high, k, 1, 0) + dot(score_low, k, 1, 0)
        grad_query = grad_query + cross[:, one] * (
            inverse[:, one] * dot_right(g, memory, 1, 1) + gt[:, one] * small_ref[one]
        )
        gq_ref[:, ks] = (scale * grad_query).astype(BF16)
        grad_key = dot(score_high, q, 0, 0) + dot(score_low, q, 0, 0)
        carried = dot(v, follow_high, 1, 1) + dot(v, follow_low, 1, 1)
        gk_ref[:, ks] = scale * grad_key + key_scale[:, one] * carried
        carried = dot(k, follow_high, 1, 0) + dot(k, follow_low, 1, 0)
        along = jnp.sum(v.astype(F32) * carried, axis=1, keepdims=True)
        column_cross = put(column_cross, key_scale[:, one] * along, h)
        coupled = pc_ref[h] * (scale * inside[:, one] * inverse[:, one])
        grad_value = dot_left(coupled, g, 0, 0) + key_scale[:, one] * carried
        gvalue_ref[:, vs] = grad_value.astype(BF16)
        product = jnp.sum(jnp.sum(memory * following, axis=0, keepdims=True), axis=1, keepdims=True)
        through = put(through, product, h)
    row_ref[...] = row_part
    cc_ref[...] = column_cross
    cold_ref[heads:, :] = jnp.zeros((8 - heads, n), F32)
    pass_ref[...] = jnp.broadcast_to(through, pass_ref.shape)


def weights_kernel(
    heads, got_ref, later_ref, small_ref, kl_ref, rows_ref, row_ref, cc_ref, cold_ref, pass_ref,
    gk_ref, k_ref, x_ref, gkey_ref, pay_ref,
):
    n = k_ref.shape[0]
    dk = k_ref.shape[1] // heads
    key_scale = jnp.exp(kl_ref[...] + small_ref[heads : heads + 1])
    later = later_ref[...]
    column_cross = cc_ref[...]
    through = pass_ref[:1]
    for h in range(heads):
        ks, one = slice(dk * h, dk * (h + 1)), slice(h, h + 1)
        vector = jnp.sum(later[:, one] * got_ref[:, h, :], axis=0, keepdims=True)
        k = k_ref[:, ks].astype(F32)
        along = jnp.sum(k * vector, axis=1, keepdims=True)
        column_cross = column_cross + put(jnp.zeros((n, 128), F32), key_scale[:, one] * along, h)
        gkey_ref[:, ks] = (gk_ref[:, ks] + key_scale[:, one] * vector).astype(BF16)
        product = jnp.sum(small_ref[one] * vector, axis=1, keepdims=True)
        through = through + put(jnp.zeros((1, 128), F32), product, h)
    through = through * small_ref[heads + 1 : heads + 2]
    row = row_ref[...].T[:8]
    crossing = column_cross.T[:8]
    passing = jnp.broadcast_to(through, (128, 128)).T[:8, :1]
    inner = cold_ref[...]
    after = iota((n, n), 0) >= iota((n, n), 1)
    suffix = dot_exact(row - inner, after.astype(F32))
    prefix = dot_exact(crossing, 1.0 - after.astype(F32))
    grad_log = suffix + prefix + passing
    grad_forget = grad_log[:heads] / (1.0 + jnp.exp(rows_ref[heads : 2 * heads, :]))
    coefs = jnp.concatenate([(inner + crossing)[:heads], grad_forget], axis=0)
    high = coefs.astype(BF16).astype(F32)
    both = jnp.concatenate([high, coefs - high], axis=0).astype(BF16)
    product = dot(both, x_ref[...], 1, 0)
    result = product[: 2 * heads] + product[2 * heads :]
    tiles = result.shape[1] // 128
    for c in range(tiles):
        pay_ref[c] = result[:heads, 128 * c : 128 * (c + 1)]
        pay_ref[tiles + c] = result[heads:, 128 * c : 128 * (c + 1)]


def sum_kernel(got_ref, out_ref):
    total = jnp.sum(got_ref[...], axis=0, keepdims=True)
    out_ref[...] = jnp.broadcast_to(total, out_ref.shape)


def place_kernel(got_ref, first_ref, second_ref):
    tiles = got_ref.shape[0] // 2
    for c in range(tiles):
        first_ref[:, 128 * c : 128 * (c + 1)] = got_ref[c]
        second_ref[:, 128 * c : 128 * (c + 1)] = got_ref[tiles + c]


def call(body, shapes, *args, scalars=()):
    shapes = [s if isinstance(s, jax.ShapeDtypeStruct) else jax.ShapeDtypeStruct(s, F32) for s in shapes]
    return pl.pallas_call(
        body,
        out_shape=shapes,
        in_specs=[SMEM if i in scalars else VMEM for i in range(len(args))],
        out_specs=[VMEM] * len(shapes),
        compiler_params=pltpu.CompilerParams(vmem_limit_bytes=40 * 1024 * 1024),
    )(*args)


def exchange(x, axis):
    return lax.all_to_all(x, axis, 0, 0)


def local(
    layer_input, queries, keys, values, grad_out, doc_pos, w_input, b_input, w_forget, b_forget
):
    x, q, k, v, g = layer_input[0], queries[0], keys[0], values[0], grad_out[0]
    heads = w_input.shape[1]
    n = q.shape[0]
    dk, dv = q.shape[1] // heads, v.shape[1] // heads
    scale = dk ** (-0.5)
    count = lax.axis_size("ctx")
    me = lax.axis_index("ctx").astype(jnp.int32).reshape(1)
    part = functools.partial
    cols = (n, 128)
    pay, memory, rows, lc, dc, kl = call(
        part(gates_kernel, heads),
        [(count, 8, 128), (count, 8, dv), (16, n), cols, cols, cols],
        x, w_input.T, w_forget.T, b_input, b_forget, doc_pos, k, v,
        scalars=(3, 4),
    )
    got = exchange(pay, "ctx")
    wl, pc, gv, rm, ls, lg = call(
        part(pairs_kernel, heads),
        [(heads, n, n)] * 3 + [cols] * 3,
        rows, lc, dc, q, k, v, g,
    )
    pay, coef, later, small, tokens = call(
        part(dual_kernel, heads, scale),
        [(count, 16, dv), (4, count, 128), (count, 128), (8, 128), (6, n, 128)],
        me, got, memory, lc, dc, rm, ls, q, g,
        scalars=(0,),
    )
    got = exchange(pay, "ctx")
    (pay,) = call(scan_kernel, [(count, 16, dv)], got, coef)
    states = exchange(pay, "ctx")
    pay, gt, gc = call(
        part(vector_kernel, heads, scale), [(count, heads, 128), cols, cols], states, tokens, lg, q, g
    )
    got = exchange(pay, "ctx")
    grad_q, grad_v, gk, row, cc, cold, through = call(
        part(grads_kernel, heads, scale),
        [
            jax.ShapeDtypeStruct(q.shape, BF16), jax.ShapeDtypeStruct(v.shape, BF16),
            k.shape, cols, cols, (8, n), (8, 128),
        ],
        states, tokens, small, kl, gt, gc, wl, pc, gv, q, k, v, g,
    )
    chunks = 2 * x.shape[1] // 128
    grad_k, pay = call(
        part(weights_kernel, heads),
        [jax.ShapeDtypeStruct(k.shape, BF16), (chunks, heads, 128)],
        got, later, small, kl, rows, row, cc, cold, through, gk, k, x,
    )
    got = exchange(pay, "ctx")
    (pay,) = call(sum_kernel, [(lax.axis_size("dp"), heads, 128)], got)
    got = exchange(pay, "dp")
    (pay,) = call(sum_kernel, [(count, heads, 128)], got)
    got = exchange(pay, "ctx")
    first, second = call(place_kernel, [(heads, x.shape[1])] * 2, got)
    return (grad_q[None], grad_k[None], grad_v[None], first.T, second.T)


def solution(mesh):
    split_rows = P("dp", "ctx", None)
    placed = (split_rows,) * 5 + (P("dp", "ctx"),) + (P(),) * 4
    return jax.shard_map(
        local,
        mesh=mesh,
        in_specs=placed,
        out_specs=(split_rows, split_rows, split_rows, P(), P()),
        check_vma=False,
    )
```

```python
import functools

import jax
import jax.numpy as jnp
from jax import lax
from jax.experimental import pallas as pl
from jax.experimental.pallas import tpu as pltpu
from jax.sharding import PartitionSpec as P

NEG = -1e30
BIG = 1e30
F32 = jnp.float32
BF16 = jnp.bfloat16
VMEM = pl.BlockSpec(memory_space=pltpu.VMEM)
SMEM = pl.BlockSpec(memory_space=pltpu.SMEM)


def dot(a, b, ca, cb):
    return lax.dot_general(a, b, (((ca,), (cb,)), ((), ())), preferred_element_type=F32)


def split(x):
    high = x.astype(BF16)
    return high, (x - high.astype(F32)).astype(BF16)


def dot_left(x, b, ca, cb):
    high, low = split(x)
    return dot(high, b, ca, cb) + dot(low, b, ca, cb)


def dot_right(a, x, ca, cb):
    high, low = split(x)
    return dot(a, high, ca, cb) + dot(a, low, ca, cb)


def dot_exact(a, b):
    return lax.dot_general(
        a, b, (((1,), (0,)), ((), ())), precision=lax.Precision.HIGHEST, preferred_element_type=F32
    )


def iota(shape, dim):
    return lax.broadcasted_iota(jnp.int32, shape, dim)


def column_of(rows):
    r, n = rows.shape
    padded = jnp.concatenate([rows, jnp.zeros((128 - r, n), F32)], axis=0)
    return padded.T


def put(acc, col, h):
    return jnp.where(iota(acc.shape, 1) == h, col, acc)


def pick(row, lane):
    return jnp.sum(jnp.where(iota(row.shape, 1) == lane, row, 0.0), axis=1, keepdims=True)


def gates_kernel(
    heads, me_ref, x_ref, wi_ref, wf_ref, bi_ref, bf_ref, pos_ref, k_ref, v_ref,
    give_ref, mem_ref, tile_ref, rows_ref, lc_ref, dc_ref, kl_ref,
):
    core = me_ref[0] % 2
    n = x_ref.shape[0]
    dk = k_ref.shape[1] // heads
    dv = v_ref.shape[1] // heads
    w8 = jnp.concatenate([wi_ref[...].astype(F32), wf_ref[...].astype(F32)], axis=0).astype(BF16)
    gates = dot(w8, x_ref[...], 1, 1)
    row8 = iota(gates.shape, 0)
    for h in range(heads):
        gates = gates + jnp.where(row8 == h, bi_ref[h], 0.0)
        gates = gates + jnp.where(row8 == h + heads, bf_ref[h], 0.0)
    in_gate, forget_pre = gates[:heads], gates[heads:]
    log_forget = jnp.minimum(forget_pre, 0.0) - jnp.log1p(jnp.exp(-jnp.abs(forget_pre)))
    start = (pos_ref[...] == 0).astype(F32)
    stacked = jnp.concatenate([log_forget, start, jnp.zeros((7 - heads, n), F32)], axis=0)
    upto = (iota((n, n), 0) <= iota((n, n), 1)).astype(F32)
    cum = dot_exact(stacked, upto)
    lc_row, dc_row = cum[:heads], cum[heads : heads + 1]
    rows_ref[...] = jnp.concatenate(
        [in_gate, forget_pre, lc_row, dc_row, jnp.zeros((3, n), F32)], axis=0
    )
    ig = column_of(in_gate)
    lc = column_of(lc_row)
    dc = jnp.broadcast_to(dc_row, (128, n)).T
    lc_ref[...] = lc
    dc_ref[...] = dc
    total, last = lc[n - 1 :], dc[n - 1 :]
    key_log = jnp.where(dc == last, total - lc + ig, NEG)
    kl_ref[...] = key_log
    own_max = jnp.max(key_log, axis=0, keepdims=True)
    weight = jnp.exp(key_log - own_max)
    vectors = []
    for h in range(heads):
        weighted = k_ref[:, dk * h : dk * (h + 1)].astype(F32) * weight[:, h : h + 1]
        vectors.append(jnp.sum(weighted, axis=0, keepdims=True))
        memory = dot_left(weighted, v_ref[:, dv * h : dv * (h + 1)], 0, 0)
        mem_ref[dk // 8 * h : dk // 8 * (h + 1)] = memory.reshape(dk // 8, 8, dv)
    cut = jnp.where(last > 0.5, BIG, 0.0)
    tile = jnp.concatenate(
        vectors
        + [own_max, total - cut, ig[:1] - lc[:1], jnp.where(dc[:1] < 0.5, 1.0, 0.0)],
        axis=0,
    )
    tile_ref[...] = tile
    half = mem_ref.shape[0] // 2
    give_ref[:half] = mem_ref[pl.ds((1 - core) * half, half)]
    give_ref[half] = jnp.concatenate([tile, jnp.zeros((8, dv - 128), F32)], axis=1)


def first_kernel(heads, me_ref, mem_ref, tile_ref, got_ref, out_ref):
    core = me_ref[0] % 2
    half, dv = out_ref.shape[0], mem_ref.shape[2]
    mine, other = tile_ref[...], got_ref[half, :, :128]
    even = jnp.where(core == 0, mine, other)
    odd = jnp.where(core == 0, other, mine)
    chip_max = jnp.maximum(even[4:5] + odd[5:6], odd[4:5])
    keep = jnp.exp(even[4:5] + odd[5:6] - chip_max)
    add = jnp.exp(odd[4:5] - chip_max)
    vectors = [
        keep[:, h : h + 1] * even[h : h + 1] + add[:, h : h + 1] * odd[h : h + 1]
        for h in range(heads)
    ]
    both = jnp.where(iota(even.shape, 1) < heads, even, pltpu.roll(odd, heads, 1))
    tile = jnp.concatenate(vectors + [both[heads:]], axis=0)
    out_ref[:, :, dv:] = jnp.broadcast_to(tile[None], (half, 8, 128))
    weight_mine = jnp.where(core == 0, keep, add)
    weight_other = jnp.where(core == 0, add, keep)
    per_head = half // (heads // 2)
    for i in range(heads // 2):
        at = core * (heads // 2) + i
        slab = slice(i * per_head, (i + 1) * per_head)
        own = mem_ref[pl.ds(core * half + i * per_head, per_head)]
        out_ref[slab, :, :dv] = pick(weight_mine, at) * own + pick(weight_other, at) * got_ref[slab]


def pairs_kernel(
    heads, rows_ref, lc_ref, dc_ref, q_ref, k_ref, v_ref, g_ref,
    wl_ref, pc_ref, gv_ref, rm_ref, ls_ref, lg_ref,
):
    n = q_ref.shape[0]
    dk = k_ref.shape[1] // heads
    dv = v_ref.shape[1] // heads
    lc, dc = lc_ref[...], dc_ref[...]
    mask = (iota((n, n), 0) >= iota((n, n), 1)) & (dc[:, :1] == rows_ref[3 * heads : 3 * heads + 1])
    rm = jnp.zeros((n, 128), F32)
    ls, lg = rm, rm
    for h in range(heads):
        offset = rows_ref[h : h + 1] - rows_ref[2 * heads + h : 2 * heads + h + 1]
        pair_log = jnp.where(mask, lc[:, h : h + 1] + offset, NEG)
        row_max = jnp.max(pair_log, axis=1, keepdims=True)
        weight = jnp.exp(pair_log - row_max)
        ks, vs = slice(dk * h, dk * (h + 1)), slice(dv * h, dv * (h + 1))
        coupled = dot(q_ref[:, ks], k_ref[:, ks], 1, 1) * weight
        grad_pair = dot(g_ref[:, vs], v_ref[:, vs], 1, 1)
        wl_ref[h] = weight
        pc_ref[h] = coupled
        gv_ref[h] = grad_pair
        rm = put(rm, row_max, h)
        ls = put(ls, jnp.sum(coupled, axis=1, keepdims=True), h)
        lg = put(lg, jnp.sum(coupled * grad_pair, axis=1, keepdims=True), h)
    rm_ref[...] = rm
    ls_ref[...] = ls
    lg_ref[...] = lg


def shift_down(x, d, fill):
    return jnp.where(iota(x.shape, 0) < d, fill, pltpu.roll(x, d, 0))


def shift_up(x, d, fill):
    size = x.shape[0]
    return jnp.where(iota(x.shape, 0) >= size - d, fill, pltpu.roll(x, size - d, 0))


def dual_kernel(
    heads, scale, me_ref, got_ref, tile_ref, pair_ref, lc_ref, dc_ref, rm_ref, ls_ref, q_ref, g_ref,
    give_ref, dual_ref, coef_ref, later_ref, small_ref, cols_ref,
):
    count = got_ref.shape[0]
    n = q_ref.shape[0]
    dk = q_ref.shape[1] // heads
    dv = g_ref.shape[1] // heads
    me = me_ref[0]
    core, chip = me % 2, me // 2
    max_even, total_even = got_ref[:, heads, dv:], got_ref[:, heads + 1, dv:]
    first_even, valid_even = got_ref[:, heads + 2, dv:], got_ref[:, heads + 3, dv:]
    max_odd, total_odd, first_odd, valid_odd = (
        pltpu.roll(x, 128 - heads, 1) for x in (max_even, total_even, first_even, valid_even)
    )
    row = iota(max_even.shape, 0)
    lane = iota(max_even.shape, 1)
    steps = [1 << i for i in range((count - 1).bit_length())]
    chip_max = jnp.maximum(max_even + total_odd, max_odd)
    total = total_even + total_odd
    t, m = total, chip_max
    for d in steps:
        m = jnp.maximum(shift_down(m, d, NEG) + t, m)
        t = shift_down(t, d, 0.0) + t
    in_even = shift_down(m, 1, NEG)
    in_odd = jnp.maximum(in_even + total_even, max_even)
    dual_even = jnp.where(valid_even > 0.5, -jnp.maximum(in_even, first_even), NEG)
    dual_odd = jnp.where(valid_odd > 0.5, -jnp.maximum(in_odd, first_odd), NEG)
    chip_dual = jnp.maximum(dual_even, total_even + dual_odd)
    t, r = total, chip_dual
    for d in steps:
        r = jnp.maximum(r, t + shift_up(r, d, NEG))
        t = t + shift_up(t, d, 0.0)
    later_odd = shift_up(r, 1, NEG)
    later_even = jnp.maximum(dual_odd, total_odd + later_odd)
    my_head = (heads // 2) * core + chip // (2 * count // heads)
    coefs = (
        jnp.exp(in_even + total - m),
        jnp.exp(chip_max - m),
        jnp.exp(total + later_odd - r),
        jnp.exp(chip_dual - r),
    )
    for i, c in enumerate(coefs):
        mine = jnp.sum(jnp.where(lane == my_head, c, 0.0), axis=1, keepdims=True)
        coef_ref[i] = jnp.broadcast_to(mine, c.shape)

    def here(x):
        return jnp.sum(jnp.where(row == chip, x, 0.0), axis=0, keepdims=True)

    def mine_of(even, odd):
        return here(jnp.where(core == 0, even, odd))

    in_me, later_me = mine_of(in_even, in_odd), mine_of(later_even, later_odd)
    dual_me, total_me = mine_of(dual_even, dual_odd), mine_of(total_even, total_odd)
    keep = here(jnp.exp(in_even + total_even - in_odd))
    add = here(jnp.exp(max_even - in_odd))
    later_row = iota((count, count), 0) < iota((count, count), 1)
    between = dot_exact(later_row.astype(F32), jnp.where(row < chip, total, 0.0))
    weight = jnp.where(
        row < chip, jnp.exp(jnp.minimum(chip_max + between - here(in_even), 0.0)), 0.0
    )
    earlier_row = iota((count, count), 0) > iota((count, count), 1)
    between = dot_exact(earlier_row.astype(F32), jnp.where(row > chip, total, 0.0))
    source = jnp.where(core == 0, dual_even, total_even + dual_odd)
    later_ref[...] = jnp.where(
        row > chip, jnp.exp(jnp.minimum(source + between - here(later_odd), 0.0)), 0.0
    )
    even_tile = jnp.where(core == 0, tile_ref[...], pair_ref[0, :, :128])
    vectors = []
    for h in range(heads):
        one = slice(h, h + 1)
        vector = jnp.sum(weight[:, one] * got_ref[:, h, dv:], axis=0, keepdims=True)
        second = keep[:, one] * vector + add[:, one] * even_tile[one]
        vectors.append(jnp.where(core == 0, vector, second))
    small_ref[...] = jnp.concatenate(
        vectors
        + [
            later_me,
            jnp.exp(in_me + total_me + later_me),
            keep,
            add,
            here(jnp.exp(total_odd + later_odd - later_even)),
            here(jnp.exp(dual_odd - later_even)),
            here(jnp.exp(dual_even - chip_dual)),
            here(jnp.exp(total_even + dual_odd - chip_dual)),
            jnp.zeros((8 - heads, 128), F32),
        ],
        axis=0,
    )

    lc, open_query = lc_ref[...], dc_ref[...] < 0.5
    cross_log = jnp.where(open_query, lc + in_me, NEG)
    row_max = jnp.maximum(rm_ref[...], cross_log)
    inside = jnp.exp(rm_ref[...] - row_max)
    cross = jnp.exp(cross_log - row_max)
    qn = jnp.zeros((n, 128), F32)
    for h in range(heads):
        along = q_ref[:, dk * h : dk * (h + 1)].astype(F32) * vectors[h]
        qn = put(qn, jnp.sum(along, axis=1, keepdims=True), h)
    sums = scale * (ls_ref[...] * inside + cross * qn)
    floor = jnp.exp(-row_max)
    size = jnp.abs(sums)
    inverse = 1.0 / jnp.maximum(size, floor)
    active = jnp.where(size > floor, jnp.where(sums > 0.0, 1.0, -1.0), 0.0)
    query_weight = jnp.where(open_query, jnp.exp(jnp.minimum(lc - row_max - dual_me, 0.0)), 0.0)
    cols_ref[0] = inside
    cols_ref[1] = cross
    cols_ref[2] = inverse
    cols_ref[3] = active
    cols_ref[4] = query_weight
    cols_ref[5] = qn
    grad_weight = query_weight * inverse * scale
    for h in range(heads):
        weighted = g_ref[:, dv * h : dv * (h + 1)].astype(F32) * grad_weight[:, h : h + 1]
        memory = dot_right(q_ref[:, dk * h : dk * (h + 1)], weighted, 0, 0)
        dual_ref[dk // 8 * h : dk // 8 * (h + 1)] = memory.reshape(dk // 8, 8, dv)
    half = give_ref.shape[0]
    give_ref[...] = dual_ref[pl.ds((1 - core) * half, half)]


def wide(coef_ref, i, j, reps):
    return jnp.concatenate([coef_ref[i, pl.ds(j, 1), :]] * reps, axis=1)


def second_kernel(heads, me_ref, got_ref, coef_ref, small_ref, dual_ref, pair_ref, out_ref):
    core = me_ref[0] % 2
    count, dv = got_ref.shape[0], dual_ref.shape[2]
    reps = dv // 128

    def forward(j, state):
        out_ref[j, :, :dv] = state
        step = wide(coef_ref, 1, j, reps) * got_ref[j, :, :dv]
        return wide(coef_ref, 0, j, reps) * state + step

    lax.fori_loop(0, count, forward, jnp.zeros((8, dv), F32), unroll=8)
    even, odd = small_ref[10:11], small_ref[11:12]
    weight_mine = jnp.where(core == 0, even, odd)
    weight_other = jnp.where(core == 0, odd, even)
    per_head = count // (heads // 2)
    for i in range(heads // 2):
        at = core * (heads // 2) + i
        slab = slice(i * per_head, (i + 1) * per_head)
        own = dual_ref[pl.ds(core * count + i * per_head, per_head)]
        out_ref[slab, :, dv:] = pick(weight_mine, at) * own + pick(weight_other, at) * pair_ref[slab]


def halves_kernel(heads, me_ref, got_ref, mem_ref, pair_ref, small_ref, give_ref, mine_ref):
    core = me_ref[0] % 2
    count, dv = give_ref.shape[0], mem_ref.shape[2]
    per_head = count // (heads // 2)

    def fill(even_ref, odd_ref, even_own):
        for i in range(heads // 2):
            at = core * (heads // 2) + i
            slab = slice(i * per_head, (i + 1) * per_head)
            before = got_ref[slab, :, :dv]
            even_ref[slab] = before
            odd_ref[slab] = pick(small_ref[6:7], at) * before + pick(small_ref[7:8], at) * even_own(slab)

    @pl.when(core == 0)
    def _():
        fill(mine_ref, give_ref, lambda slab: mem_ref[slab])

    @pl.when(core == 1)
    def _():
        fill(give_ref, mine_ref, lambda slab: pair_ref[slab])


def vector_kernel(
    heads, scale, me_ref, mine_ref, pair_ref, got_ref, coef_ref, cols_ref, lg_ref, q_ref, g_ref,
    out_ref, mem_ref, tile_ref, gt_ref, gc_ref,
):
    core = me_ref[0] % 2
    n = q_ref.shape[0]
    dk = q_ref.shape[1] // heads
    dv = g_ref.shape[1] // heads
    count = got_ref.shape[0]
    reps = dv // 128
    mem_ref[pl.ds(core * count, count)] = mine_ref[...]
    mem_ref[pl.ds((1 - core) * count, count)] = pair_ref[...]
    gc = jnp.zeros((n, 128), F32)
    for h in range(heads):
        memory = mem_ref[dk // 8 * h : dk // 8 * (h + 1)].reshape(dk, dv)
        crossing = dot_right(q_ref[:, dk * h : dk * (h + 1)], memory, 1, 0)
        along = g_ref[:, dv * h : dv * (h + 1)].astype(F32) * crossing
        gc = put(gc, jnp.sum(along, axis=1, keepdims=True), h)
    inverse = cols_ref[2]
    gt = -scale * (lg_ref[...] * cols_ref[0] + cols_ref[1] * gc) * inverse * inverse * cols_ref[3]
    gt_ref[...] = gt
    gc_ref[...] = gc
    weight = cols_ref[4] * gt * scale
    vectors = [
        jnp.sum(
            q_ref[:, dk * h : dk * (h + 1)].astype(F32) * weight[:, h : h + 1], axis=0, keepdims=True
        )
        for h in range(heads)
    ]
    tile = jnp.concatenate(vectors + [jnp.zeros((8 - heads, 128), F32)], axis=0)
    tile_ref[...] = tile
    out_ref[:, :, dv:] = jnp.broadcast_to(tile[None], (count, 8, 128))

    def backward(i, state):
        j = count - 1 - i
        out_ref[j, :, :dv] = state
        step = wide(coef_ref, 3, j, reps) * got_ref[j, :, dv:]
        return wide(coef_ref, 2, j, reps) * state + step

    lax.fori_loop(0, count, backward, jnp.zeros((8, dv), F32), unroll=8)


def inner_kernel(
    heads, scale, mem_ref, cols_ref, small_ref, gt_ref, gc_ref, wl_ref, pc_ref, gv_ref,
    q_ref, k_ref, g_ref,
    gq_ref, gvalue_ref, gk_ref, row_ref, cold_ref,
):
    n = q_ref.shape[0]
    dk = q_ref.shape[1] // heads
    dv = g_ref.shape[1] // heads
    gt, gc = gt_ref[...], gc_ref[...]
    inside, cross, inverse, qn = cols_ref[0], cols_ref[1], cols_ref[2], cols_ref[5]
    row_part = scale * cross * (inverse * gc + gt * qn)
    for h in range(heads):
        ks, vs = slice(dk * h, dk * (h + 1)), slice(dv * h, dv * (h + 1))
        one = slice(h, h + 1)
        q, k, g = q_ref[:, ks], k_ref[:, ks], g_ref[:, vs]
        memory = mem_ref[dk // 8 * h : dk // 8 * (h + 1)].reshape(dk, dv)
        factor = inside[:, one] * (inverse[:, one] * gv_ref[h] + gt[:, one])
        pair_grad = factor * pc_ref[h]
        cold_ref[one, :] = scale * jnp.sum(pair_grad, axis=0, keepdims=True)
        row_part = row_part + put(
            jnp.zeros((n, 128), F32), scale * jnp.sum(pair_grad, axis=1, keepdims=True), h
        )
        score_high, score_low = split(factor * wl_ref[h])
        grad_query = dot(score_high, k, 1, 0) + dot(score_low, k, 1, 0)
        grad_query = grad_query + cross[:, one] * (
            inverse[:, one] * dot_right(g, memory, 1, 1) + gt[:, one] * small_ref[one]
        )
        gq_ref[:, ks] = (scale * grad_query).astype(BF16)
        gk_ref[:, ks] = scale * (dot(score_high, q, 0, 0) + dot(score_low, q, 0, 0))
        coupled = pc_ref[h] * (scale * inside[:, one] * inverse[:, one])
        gvalue_ref[:, vs] = dot_left(coupled, g, 0, 0)
    row_ref[...] = row_part
    cold_ref[heads:, :] = jnp.zeros((8 - heads, n), F32)


def after_kernel(
    heads, me_ref, got_ref, later_ref, small_ref, dual_ref, pair_ref, tile_ref,
    give_ref, mine_ref, sum_ref,
):
    core = me_ref[0] % 2
    count, dv = mine_ref.shape[0], dual_ref.shape[2]
    per_head = count // (heads // 2)
    vectors = [
        jnp.sum(later_ref[:, h : h + 1] * got_ref[:, h, dv:], axis=0, keepdims=True)
        for h in range(heads)
    ]
    tile = jnp.concatenate(vectors + [tile_ref[:heads]], axis=0)
    sum_ref[...] = tile
    give_ref[count] = jnp.concatenate([tile, jnp.zeros((8, dv - 128), F32)], axis=1)

    def fill(even_ref, odd_ref, odd_own):
        for i in range(heads // 2):
            at = core * (heads // 2) + i
            slab = slice(i * per_head, (i + 1) * per_head)
            after = got_ref[slab, :, :dv]
            odd_ref[slab] = after
            even_ref[slab] = pick(small_ref[8:9], at) * after + pick(small_ref[9:10], at) * odd_own(i)

    @pl.when(core == 0)
    def _():
        fill(mine_ref, give_ref, lambda i: pair_ref[i * per_head : (i + 1) * per_head])

    @pl.when(core == 1)
    def _():
        fill(give_ref, mine_ref, lambda i: dual_ref[count + i * per_head : count + (i + 1) * per_head])


def weights_kernel(
    heads, me_ref, mine_ref, pair_ref, sum_ref, mem_ref, small_ref, kl_ref, rows_ref, row_ref, cold_ref,
    k_ref, v_ref, x_ref,
    after_ref, vector_ref, carried_ref, pay_ref,
):
    core = me_ref[0] % 2
    n = k_ref.shape[0]
    dk = k_ref.shape[1] // heads
    dv = v_ref.shape[1] // heads
    count = mine_ref.shape[0]
    after_ref[pl.ds(core * count, count)] = mine_ref[...]
    after_ref[pl.ds((1 - core) * count, count)] = pair_ref[:count]
    mine, other = sum_ref[...], pair_ref[count, :, :128]
    key_scale = jnp.exp(kl_ref[...] + small_ref[heads : heads + 1])
    column_cross = jnp.zeros((n, 128), F32)
    through = jnp.zeros((1, 128), F32)
    vectors = []
    for h in range(heads):
        ks, vs, one = slice(dk * h, dk * (h + 1)), slice(dv * h, dv * (h + 1)), slice(h, h + 1)
        slab = slice(dk // 8 * h, dk // 8 * (h + 1))
        odd = mine[one] + other[one]
        even = small_ref[8:9, one] * odd + small_ref[9:10, one] * other[heads + h : heads + h + 1]
        vector = jnp.where(core == 0, even, odd)
        vectors.append(vector)
        following = after_ref[slab].reshape(dk, dv)
        carried = dot_right(k_ref[:, ks], following, 1, 0)
        carried_ref[:, vs] = carried
        along = jnp.sum(v_ref[:, vs].astype(F32) * carried, axis=1, keepdims=True)
        along = along + jnp.sum(k_ref[:, ks].astype(F32) * vector, axis=1, keepdims=True)
        column_cross = put(column_cross, key_scale[:, one] * along, h)
        product = jnp.sum(mem_ref[slab].reshape(dk, dv) * following, axis=0, keepdims=True)
        product = jnp.sum(product, axis=1, keepdims=True)
        product = product + jnp.sum(small_ref[one] * vector, axis=1, keepdims=True)
        through = put(through, product, h)
    vector_ref[...] = jnp.concatenate(vectors + [jnp.zeros((8 - heads, 128), F32)], axis=0)
    through = through * small_ref[heads + 1 : heads + 2]
    row = row_ref[...].T[:8]
    crossing = column_cross.T[:8]
    passing = jnp.broadcast_to(through, (128, 128)).T[:8, :1]
    inner = cold_ref[...]
    after = iota((n, n), 0) >= iota((n, n), 1)
    suffix = dot_exact(row - inner, after.astype(F32))
    prefix = dot_exact(crossing, 1.0 - after.astype(F32))
    grad_log = suffix + prefix + passing
    grad_forget = grad_log[:heads] / (1.0 + jnp.exp(rows_ref[heads : 2 * heads, :]))
    coefs = jnp.concatenate([(inner + crossing)[:heads], grad_forget], axis=0)
    high = coefs.astype(BF16).astype(F32)
    both = jnp.concatenate([high, coefs - high], axis=0).astype(BF16)
    product = dot(both, x_ref[...], 1, 0)
    result = product[: 2 * heads] + product[2 * heads :]
    tiles = result.shape[1] // 128
    for c in range(tiles):
        pay_ref[c] = result[:heads, 128 * c : 128 * (c + 1)]
        pay_ref[tiles + c] = result[heads:, 128 * c : 128 * (c + 1)]


def finish_kernel(
    heads, after_ref, vector_ref, carried_ref, small_ref, kl_ref, gk_ref, gvalue_ref, v_ref,
    gkey_ref, out_ref,
):
    dk = gk_ref.shape[1] // heads
    dv = v_ref.shape[1] // heads
    key_scale = jnp.exp(kl_ref[...] + small_ref[heads : heads + 1])
    for h in range(heads):
        ks, vs, one = slice(dk * h, dk * (h + 1)), slice(dv * h, dv * (h + 1)), slice(h, h + 1)
        following = after_ref[dk // 8 * h : dk // 8 * (h + 1)].reshape(dk, dv)
        carried = dot_right(v_ref[:, vs], following, 1, 1) + vector_ref[one]
        gkey_ref[:, ks] = (gk_ref[:, ks] + key_scale[:, one] * carried).astype(BF16)
        out_ref[:, vs] = (gvalue_ref[:, vs] + key_scale[:, one] * carried_ref[:, vs]).astype(BF16)


def sum_kernel(got_ref, out_ref):
    total = jnp.sum(got_ref[...], axis=0, keepdims=True)
    out_ref[...] = jnp.broadcast_to(total, out_ref.shape)


def place_kernel(got_ref, first_ref, second_ref):
    tiles = got_ref.shape[0] // 2
    for c in range(tiles):
        first_ref[:, 128 * c : 128 * (c + 1)] = got_ref[c]
        second_ref[:, 128 * c : 128 * (c + 1)] = got_ref[tiles + c]


def call(body, shapes, *args, scalars=()):
    shapes = [s if isinstance(s, jax.ShapeDtypeStruct) else jax.ShapeDtypeStruct(s, F32) for s in shapes]
    return pl.pallas_call(
        body,
        out_shape=shapes,
        in_specs=[SMEM if i in scalars else VMEM for i in range(len(args))],
        out_specs=[VMEM] * len(shapes),
    )(*args)


def exchange(x, axis, groups=None):
    return lax.all_to_all(x, axis, 0, 0, axis_index_groups=groups)


def local(
    layer_input, queries, keys, values, grad_out, doc_pos, w_input, b_input, w_forget, b_forget
):
    x, q, k, v, g = layer_input[0], queries[0], keys[0], values[0], grad_out[0]
    heads = w_input.shape[1]
    n = q.shape[0]
    dk, dv = q.shape[1] // heads, v.shape[1] // heads
    scale = dk ** (-0.5)
    devices = lax.axis_size("ctx")
    count = devices // 2
    me = lax.axis_index("ctx").astype(jnp.int32).reshape(1)
    part = functools.partial
    cols = (n, 128)
    slabs = heads * dk // 8
    cores = [[2 * i + c for i in range(count)] for c in range(2)]

    def to_pair(a):
        return lax.ppermute(a, "ctx", [(i, i ^ 1) for i in range(devices)])

    give, memory, tile, rows, lc, dc, kl = call(
        part(gates_kernel, heads),
        [(slabs // 2 + 1, 8, dv), (slabs, 8, dv), (8, 128), (16, n), cols, cols, cols],
        me, x, w_input.T, w_forget.T, b_input, b_forget, doc_pos, k, v,
        scalars=(0, 4, 5),
    )
    pair_memory = to_pair(give)
    (pay,) = call(
        part(first_kernel, heads), [(count, 8, dv + 128)], me, memory, tile, pair_memory, scalars=(0,)
    )
    first = exchange(pay, "ctx", cores)
    wl, pc, gv, rm, ls, lg = call(
        part(pairs_kernel, heads),
        [(heads, n, n)] * 3 + [cols] * 3,
        rows, lc, dc, q, k, v, g,
    )
    give, dual, coef, later, small, tokens = call(
        part(dual_kernel, heads, scale),
        [(count, 8, dv), (slabs, 8, dv), (4, count, 128), (count, 128), (16, 128), (6, n, 128)],
        me, first, tile, pair_memory[slabs // 2 :], lc, dc, rm, ls, q, g,
        scalars=(0,),
    )
    pair_dual = to_pair(give)
    (pay,) = call(
        part(second_kernel, heads),
        [(count, 8, 2 * dv)],
        me, first, coef, small, dual, pair_dual,
        scalars=(0,),
    )
    second = exchange(pay, "ctx", cores)
    give, mine = call(
        part(halves_kernel, heads),
        [(count, 8, dv)] * 2,
        me, second, memory, pair_memory, small,
        scalars=(0,),
    )
    pair = to_pair(give)
    pay, states, tile, gt, gc = call(
        part(vector_kernel, heads, scale),
        [(count, 8, dv + 128), (slabs, 8, dv), (8, 128), cols, cols],
        me, mine, pair, second, coef, tokens, lg, q, g,
        scalars=(0,),
    )
    third = exchange(pay, "ctx", cores)
    grad_q, gvalue, gk, row, cold = call(
        part(inner_kernel, heads, scale),
        [jax.ShapeDtypeStruct(q.shape, BF16), v.shape, k.shape, cols, (8, n)],
        states, tokens, small, gt, gc, wl, pc, gv, q, k, g,
    )
    give, mine, tile = call(
        part(after_kernel, heads),
        [(count + 1, 8, dv), (count, 8, dv), (8, 128)],
        me, third, later, small, dual, pair_dual, tile,
        scalars=(0,),
    )
    pair = to_pair(give)
    chunks = 2 * x.shape[1] // 128
    following, vector, carried, pay = call(
        part(weights_kernel, heads),
        [(slabs, 8, dv), (8, 128), v.shape, (chunks, heads, 128)],
        me, mine, pair, tile, states, small, kl, rows, row, cold, k, v, x,
        scalars=(0,),
    )
    got = exchange(pay, "ctx")
    grad_k, grad_v = call(
        part(finish_kernel, heads),
        [jax.ShapeDtypeStruct(k.shape, BF16), jax.ShapeDtypeStruct(v.shape, BF16)],
        following, vector, carried, small, kl, gk, gvalue, v,
    )
    (pay,) = call(sum_kernel, [(lax.axis_size("dp"), heads, 128)], got)
    got = exchange(pay, "dp")
    (pay,) = call(sum_kernel, [(devices, heads, 128)], got)
    got = exchange(pay, "ctx")
    first, second = call(place_kernel, [(heads, x.shape[1])] * 2, got)
    return (grad_q[None], grad_k[None], grad_v[None], first.T, second.T)


def solution(mesh):
    split_rows = P("dp", "ctx", None)
    placed = (split_rows,) * 5 + (P("dp", "ctx"),) + (P(),) * 4
    return jax.shard_map(
        local,
        mesh=mesh,
        in_specs=placed,
        out_specs=(split_rows, split_rows, split_rows, P(), P()),
        check_vma=False,
    )
```

```python
import functools

import jax
import jax.numpy as jnp
from jax import lax
from jax.experimental import pallas as pl
from jax.experimental.pallas import tpu as pltpu
from jax.sharding import PartitionSpec as P

NEG = -1e30
BIG = 1e30
F32 = jnp.float32
BF16 = jnp.bfloat16


def dot(a, b, ca, cb):
    return lax.dot_general(a, b, (((ca,), (cb,)), ((), ())), preferred_element_type=F32)


def split(x):
    high = x.astype(BF16)
    return high, (x - high.astype(F32)).astype(BF16)


def dot_left(x, b, ca, cb):
    high, low = split(x)
    return dot(high, b, ca, cb) + dot(low, b, ca, cb)


def dot_right(a, x, ca, cb):
    high, low = split(x)
    return dot(a, high, ca, cb) + dot(a, low, ca, cb)


def dot_exact(a, b):
    return lax.dot_general(
        a, b, (((1,), (0,)), ((), ())), precision=lax.Precision.HIGHEST, preferred_element_type=F32
    )


def iota(shape, dim):
    return lax.broadcasted_iota(jnp.int32, shape, dim)


def column_of(rows):
    r, n = rows.shape
    padded = jnp.concatenate([rows, jnp.zeros((128 - r, n), F32)], axis=0)
    return padded.T


def put(acc, col, h):
    return jnp.where(iota(acc.shape, 1) == h, col, acc)


def pick(row, lane):
    return jnp.sum(jnp.where(iota(row.shape, 1) == lane, row, 0.0), axis=1, keepdims=True)


def gates_kernel(
    heads, me_ref, x_ref, wi_ref, wf_ref, bi_ref, bf_ref, pos_ref, k_ref, v_ref,
    give_ref, mem_ref, tile_ref, rows_ref, cols_ref,
):
    core = me_ref[0] % 2
    n = x_ref.shape[0]
    dk = k_ref.shape[1] // heads
    dv = v_ref.shape[1] // heads
    w8 = jnp.concatenate([wi_ref[...].astype(F32), wf_ref[...].astype(F32)], axis=0).astype(BF16)
    gates = dot(w8, x_ref[...], 1, 1)
    row8 = iota(gates.shape, 0)
    for h in range(heads):
        gates = gates + jnp.where(row8 == h, bi_ref[h], 0.0)
        gates = gates + jnp.where(row8 == h + heads, bf_ref[h], 0.0)
    in_gate, forget_pre = gates[:heads], gates[heads:]
    log_forget = jnp.minimum(forget_pre, 0.0) - jnp.log1p(jnp.exp(-jnp.abs(forget_pre)))
    start = (pos_ref[...] == 0).astype(F32)
    stacked = jnp.concatenate([log_forget, start, jnp.zeros((7 - heads, n), F32)], axis=0)
    upto = (iota((n, n), 0) <= iota((n, n), 1)).astype(F32)
    cum = dot_exact(stacked, upto)
    lc_row, dc_row = cum[:heads], cum[heads : heads + 1]
    rows_ref[...] = jnp.concatenate(
        [in_gate, forget_pre, lc_row, dc_row, jnp.zeros((3, n), F32)], axis=0
    )
    ig = column_of(in_gate)
    lc = column_of(lc_row)
    dc = jnp.broadcast_to(dc_row, (128, n)).T
    total, last = lc[n - 1 :], dc[n - 1 :]
    key_log = jnp.where(dc == last, total - lc + ig, NEG)
    cols_ref[...] = pack([lc, key_log, dc], heads)
    rows_ref.send()
    cols_ref.send()
    own_max = jnp.max(key_log, axis=0, keepdims=True)
    weight = jnp.exp(key_log - own_max)
    vectors = []
    for h in range(heads):
        weighted = k_ref[:, dk * h : dk * (h + 1)].astype(F32) * weight[:, h : h + 1]
        vectors.append(jnp.sum(weighted, axis=0, keepdims=True))
        memory = dot_left(weighted, v_ref[:, dv * h : dv * (h + 1)], 0, 0)
        mem_ref[dk // 8 * h : dk // 8 * (h + 1)] = memory.reshape(dk // 8, 8, dv)
    cut = jnp.where(last > 0.5, BIG, 0.0)
    tile = jnp.concatenate(
        vectors
        + [own_max, total - cut, ig[:1] - lc[:1], jnp.where(dc[:1] < 0.5, 1.0, 0.0)],
        axis=0,
    )
    tile_ref[...] = tile
    half = mem_ref.shape[0] // 2
    give_ref[:half] = mem_ref[pl.ds((1 - core) * half, half)]
    give_ref[half] = jnp.concatenate([tile, jnp.zeros((8, dv - 128), F32)], axis=1)


def first_kernel(heads, me_ref, mem_ref, tile_ref, got_ref, out_ref, even_ref, even_tile_ref):
    core = me_ref[0] % 2
    half, dv = out_ref.shape[0], mem_ref.shape[2]
    mine, other = tile_ref[...], got_ref[half, :, :128]
    even = jnp.where(core == 0, mine, other)
    odd = jnp.where(core == 0, other, mine)
    chip_max = jnp.maximum(even[4:5] + odd[5:6], odd[4:5])
    keep = jnp.exp(even[4:5] + odd[5:6] - chip_max)
    add = jnp.exp(odd[4:5] - chip_max)
    vectors = [
        keep[:, h : h + 1] * even[h : h + 1] + add[:, h : h + 1] * odd[h : h + 1]
        for h in range(heads)
    ]
    both = jnp.where(iota(even.shape, 1) < heads, even, pltpu.roll(odd, heads, 1))
    tile = jnp.concatenate(vectors + [both[heads:]], axis=0)
    out_ref[:, :, dv:] = jnp.broadcast_to(tile[None], (half, 8, 128))
    weight_mine = jnp.where(core == 0, keep, add)
    weight_other = jnp.where(core == 0, add, keep)
    per_head = half // (heads // 2)
    for i in range(heads // 2):
        at = core * (heads // 2) + i
        slab = slice(i * per_head, (i + 1) * per_head)
        own = mem_ref[pl.ds(core * half + i * per_head, per_head)]
        other = got_ref[slab]
        out_ref[slab, :, :dv] = pick(weight_mine, at) * own + pick(weight_other, at) * other
        even_ref[slab] = jnp.where(core == 0, own, other)
    even_tile_ref[...] = even


def pairs_kernel(
    heads, rows_ref, cols_ref, q_ref, k_ref, v_ref, g_ref,
    wl_ref, pc_ref, gv_ref, sums_ref,
):
    n = q_ref.shape[0]
    dk = k_ref.shape[1] // heads
    dv = v_ref.shape[1] // heads
    lc = cols_ref[...]
    dc = lc[:, 2 * heads : 2 * heads + 1]
    mask = (iota((n, n), 0) >= iota((n, n), 1)) & (dc == rows_ref[3 * heads : 3 * heads + 1])
    rm = jnp.zeros((n, 128), F32)
    ls, lg = rm, rm
    for h in range(heads):
        offset = rows_ref[h : h + 1] - rows_ref[2 * heads + h : 2 * heads + h + 1]
        pair_log = jnp.where(mask, lc[:, h : h + 1] + offset, NEG)
        row_max = jnp.max(pair_log, axis=1, keepdims=True)
        weight = jnp.exp(pair_log - row_max)
        ks, vs = slice(dk * h, dk * (h + 1)), slice(dv * h, dv * (h + 1))
        coupled = dot(q_ref[:, ks], k_ref[:, ks], 1, 1) * weight
        grad_pair = dot(g_ref[:, vs], v_ref[:, vs], 1, 1)
        wl_ref[h] = weight
        pc_ref[h] = coupled
        gv_ref[h] = grad_pair
        rm = put(rm, row_max, h)
        ls = put(ls, jnp.sum(coupled, axis=1, keepdims=True), h)
        lg = put(lg, jnp.sum(coupled * grad_pair, axis=1, keepdims=True), h)
    sums_ref[...] = pack([rm, ls, lg], heads)


def shift_down(x, d, fill):
    return jnp.where(iota(x.shape, 0) < d, fill, pltpu.roll(x, d, 0))


def shift_up(x, d, fill):
    size = x.shape[0]
    return jnp.where(iota(x.shape, 0) >= size - d, fill, pltpu.roll(x, size - d, 0))


def dual_kernel(
    heads, scale, me_ref, got_ref, tile_ref, cols_ref, sums_ref, q_ref, g_ref,
    give_ref, dual_ref, coef_ref, now_ref, coef_later_ref, later_ref, small_ref, tokens_ref,
):
    count = got_ref.shape[0]
    n = q_ref.shape[0]
    dk = q_ref.shape[1] // heads
    dv = g_ref.shape[1] // heads
    me = me_ref[0]
    core, chip = me % 2, me // 2
    max_even, total_even = got_ref[:, heads, dv:], got_ref[:, heads + 1, dv:]
    first_even, valid_even = got_ref[:, heads + 2, dv:], got_ref[:, heads + 3, dv:]
    max_odd, total_odd, first_odd, valid_odd = (
        pltpu.roll(x, 128 - heads, 1) for x in (max_even, total_even, first_even, valid_even)
    )
    row = iota(max_even.shape, 0)
    lane = iota(max_even.shape, 1)
    steps = [1 << i for i in range((count - 1).bit_length())]
    chip_max = jnp.maximum(max_even + total_odd, max_odd)
    total = total_even + total_odd
    t, m = total, chip_max
    for d in steps:
        m = jnp.maximum(shift_down(m, d, NEG) + t, m)
        t = shift_down(t, d, 0.0) + t
    in_even = shift_down(m, 1, NEG)
    in_odd = jnp.maximum(in_even + total_even, max_even)
    dual_even = jnp.where(valid_even > 0.5, -jnp.maximum(in_even, first_even), NEG)
    dual_odd = jnp.where(valid_odd > 0.5, -jnp.maximum(in_odd, first_odd), NEG)
    chip_dual = jnp.maximum(dual_even, total_even + dual_odd)
    t, r = total, chip_dual
    for d in steps:
        r = jnp.maximum(r, t + shift_up(r, d, NEG))
        t = t + shift_up(t, d, 0.0)
    later_odd = shift_up(r, 1, NEG)
    later_even = jnp.maximum(dual_odd, total_odd + later_odd)
    my_head = (heads // 2) * core + chip // (2 * count // heads)
    coefs = (
        jnp.exp(in_even + total - m),
        jnp.exp(chip_max - m),
        jnp.exp(total + later_odd - r),
        jnp.exp(chip_dual - r),
    )
    for i, c in enumerate(coefs):
        mine = jnp.sum(jnp.where(lane == my_head, c, 0.0), axis=1, keepdims=True)
        (coef_ref if i < 2 else coef_later_ref)[i % 2] = jnp.broadcast_to(mine, c.shape)
    coef_later_ref.send()

    def here(x):
        return jnp.sum(jnp.where(row == chip, x, 0.0), axis=0, keepdims=True)

    def mine_of(even, odd):
        return here(jnp.where(core == 0, even, odd))

    in_me, later_me = mine_of(in_even, in_odd), mine_of(later_even, later_odd)
    dual_me, total_me = mine_of(dual_even, dual_odd), mine_of(total_even, total_odd)
    keep = here(jnp.exp(in_even + total_even - in_odd))
    add = here(jnp.exp(max_even - in_odd))
    later_row = iota((count, count), 0) < iota((count, count), 1)
    between = dot_exact(later_row.astype(F32), jnp.where(row < chip, total, 0.0))
    weight = jnp.where(
        row < chip, jnp.exp(jnp.minimum(chip_max + between - here(in_even), 0.0)), 0.0
    )
    earlier_row = iota((count, count), 0) > iota((count, count), 1)
    between = dot_exact(earlier_row.astype(F32), jnp.where(row > chip, total, 0.0))
    source = jnp.where(core == 0, dual_even, total_even + dual_odd)
    later_ref[...] = jnp.where(
        row > chip, jnp.exp(jnp.minimum(source + between - here(later_odd), 0.0)), 0.0
    )
    later_ref.send()
    even_tile = tile_ref[...]
    vectors = []
    for h in range(heads):
        one = slice(h, h + 1)
        vector = jnp.sum(weight[:, one] * got_ref[:, h, dv:], axis=0, keepdims=True)
        second = keep[:, one] * vector + add[:, one] * even_tile[one]
        vectors.append(jnp.where(core == 0, vector, second))
    small = jnp.concatenate(
        vectors
        + [
            later_me,
            jnp.exp(in_me + total_me + later_me),
            keep,
            add,
            here(jnp.exp(total_odd + later_odd - later_even)),
            here(jnp.exp(dual_odd - later_even)),
            here(jnp.exp(dual_even - chip_dual)),
            here(jnp.exp(total_even + dual_odd - chip_dual)),
            jnp.zeros((8 - heads, 128), F32),
        ],
        axis=0,
    )

    small_ref[...] = small
    small_ref.send()
    now_ref[...] = small
    lc = cols_ref[...]
    open_query = lc[:, 2 * heads : 2 * heads + 1] < 0.5
    sums = sums_ref[...]
    cross_log = jnp.where(open_query, lc + in_me, NEG)
    row_max = jnp.maximum(sums, cross_log)
    inside = jnp.exp(sums - row_max)
    cross = jnp.exp(cross_log - row_max)
    qn = jnp.zeros((n, 128), F32)
    for h in range(heads):
        along = q_ref[:, dk * h : dk * (h + 1)].astype(F32) * vectors[h]
        qn = put(qn, jnp.sum(along, axis=1, keepdims=True), h)
    sums = scale * (unpack(sums, 1, heads) * inside + cross * qn)
    floor = jnp.exp(-row_max)
    size = jnp.abs(sums)
    inverse = 1.0 / jnp.maximum(size, floor)
    active = jnp.where(size > floor, jnp.where(sums > 0.0, 1.0, -1.0), 0.0)
    query_weight = jnp.where(open_query, jnp.exp(jnp.minimum(lc - row_max - dual_me, 0.0)), 0.0)
    tokens_ref[...] = pack([inside, cross, inverse, active, query_weight, qn], heads)
    tokens_ref.send()
    grad_weight = query_weight * inverse * scale
    half = give_ref.shape[0]
    per_head = dk // 8
    for h in range(heads):
        weighted = g_ref[:, dv * h : dv * (h + 1)].astype(F32) * grad_weight[:, h : h + 1]
        memory = dot_right(q_ref[:, dk * h : dk * (h + 1)], weighted, 0, 0).reshape(per_head, 8, dv)
        slab = slice(per_head * h % half, per_head * h % half + per_head)

        @pl.when(core == h // (heads // 2))
        def _():
            dual_ref[slab] = memory

        @pl.when(core != h // (heads // 2))
        def _():
            give_ref[slab] = memory


def wide(coef_ref, i, j, reps):
    return jnp.concatenate([coef_ref[i, pl.ds(j, 1), :]] * reps, axis=1)


def second_kernel(
    heads, me_ref, got_ref, coef_ref, small_ref, dual_ref, pair_ref, out_ref, odd_ref
):
    core = me_ref[0] % 2
    count, dv = got_ref.shape[0], dual_ref.shape[2]
    reps = dv // 128

    def forward(j, state):
        out_ref[j, :, :dv] = state
        step = wide(coef_ref, 1, j, reps) * got_ref[j, :, :dv]
        return wide(coef_ref, 0, j, reps) * state + step

    even, odd = small_ref[10:11], small_ref[11:12]
    weight_mine = jnp.where(core == 0, even, odd)
    weight_other = jnp.where(core == 0, odd, even)
    per_head = count // (heads // 2)
    for i in range(heads // 2):
        at = core * (heads // 2) + i
        slab = slice(i * per_head, (i + 1) * per_head)
        own, other = dual_ref[slab], pair_ref[slab]
        out_ref[slab, :, dv:] = pick(weight_mine, at) * own + pick(weight_other, at) * other
        odd_ref[slab] = jnp.where(core == 0, other, own)
    odd_ref.send()
    lax.fori_loop(0, count, forward, jnp.zeros((8, dv), F32), unroll=8)


def halves_kernel(heads, me_ref, got_ref, even_ref, small_ref, give_ref, mine_ref):
    core = me_ref[0] % 2
    count, dv = give_ref.shape[0], give_ref.shape[2]
    per_head = count // (heads // 2)
    even, small = even_ref.ready(), small_ref[...]

    def fill(to_even_ref, to_odd_ref):
        for i in range(heads // 2):
            at = core * (heads // 2) + i
            slab = slice(i * per_head, (i + 1) * per_head)
            before = got_ref[slab, :, :dv]
            to_even_ref[slab] = before
            to_odd_ref[slab] = pick(small[6:7], at) * before + pick(small[7:8], at) * even[slab]

    @pl.when(core == 0)
    def _():
        fill(mine_ref, give_ref)

    @pl.when(core == 1)
    def _():
        fill(give_ref, mine_ref)


def vector_kernel(
    heads, scale, me_ref, mine_ref, pair_ref, got_ref, coef_ref, cols_ref, sums_ref, q_ref, g_ref,
    out_ref, mem_ref, tile_ref, gt_ref,
):
    core = me_ref[0] % 2
    n = q_ref.shape[0]
    dk = q_ref.shape[1] // heads
    dv = g_ref.shape[1] // heads
    count = got_ref.shape[0]
    reps = dv // 128
    mem_ref[pl.ds(core * count, count)] = mine_ref[...]
    mem_ref[pl.ds((1 - core) * count, count)] = pair_ref[...]
    mem_ref.send()
    gc = jnp.zeros((n, 128), F32)
    for h in range(heads):
        memory = mem_ref[dk // 8 * h : dk // 8 * (h + 1)].reshape(dk, dv)
        crossing = dot_right(q_ref[:, dk * h : dk * (h + 1)], memory, 1, 0)
        along = g_ref[:, dv * h : dv * (h + 1)].astype(F32) * crossing
        gc = put(gc, jnp.sum(along, axis=1, keepdims=True), h)
    tokens = cols_ref[...]
    inside, cross, inverse, active, query_weight = (unpack(tokens, i, heads) for i in range(5))
    gt = -scale * (unpack(sums_ref[...], 2, heads) * inside + cross * gc) * inverse * inverse * active
    gt_ref[...] = pack([gt, gc], heads)
    gt_ref.send()
    weight = query_weight * gt * scale
    vectors = [
        jnp.sum(
            q_ref[:, dk * h : dk * (h + 1)].astype(F32) * weight[:, h : h + 1], axis=0, keepdims=True
        )
        for h in range(heads)
    ]
    tile = jnp.concatenate(vectors + [jnp.zeros((8 - heads, 128), F32)], axis=0)
    tile_ref[...] = tile
    tile_ref.send()
    out_ref[:, :, dv:] = jnp.broadcast_to(tile[None], (count, 8, 128))

    coef = coef_ref.ready()

    def backward(i, state):
        j = count - 1 - i
        out_ref[j, :, :dv] = state
        step = wide(coef, 1, j, reps) * got_ref[j, :, dv:]
        return wide(coef, 0, j, reps) * state + step

    lax.fori_loop(0, count, backward, jnp.zeros((8, dv), F32), unroll=8)


def inner_kernel(
    heads, scale, mem_ref, cols_ref, small_ref, gt_ref, wl_ref, pc_ref, gv_ref,
    q_ref, k_ref, g_ref,
    gq_ref, gvalue_ref, gk_ref, row_ref, cold_ref,
):
    n = q_ref.shape[0]
    dk = q_ref.shape[1] // heads
    dv = g_ref.shape[1] // heads
    gt, tokens = gt_ref[...], cols_ref[...]
    gc = unpack(gt, 1, heads)
    inside, cross, inverse, qn = (unpack(tokens, i, heads) for i in (0, 1, 2, 5))
    row_part = scale * cross * (inverse * gc + gt * qn)
    for h in range(heads):
        ks, vs = slice(dk * h, dk * (h + 1)), slice(dv * h, dv * (h + 1))
        one = slice(h, h + 1)
        q, k, g = q_ref[:, ks], k_ref[:, ks], g_ref[:, vs]
        memory = mem_ref[dk // 8 * h : dk // 8 * (h + 1)].reshape(dk, dv)
        factor = inside[:, one] * (inverse[:, one] * gv_ref[h] + gt[:, one])
        pair_grad = factor * pc_ref[h]
        cold_ref[one, :] = scale * jnp.sum(pair_grad, axis=0, keepdims=True)
        row_part = row_part + put(
            jnp.zeros((n, 128), F32), scale * jnp.sum(pair_grad, axis=1, keepdims=True), h
        )
        score_high, score_low = split(factor * wl_ref[h])
        grad_query = dot(score_high, k, 1, 0) + dot(score_low, k, 1, 0)
        grad_query = grad_query + cross[:, one] * (
            inverse[:, one] * dot_right(g, memory, 1, 1) + gt[:, one] * small_ref[one]
        )
        gq_ref[:, ks] = (scale * grad_query).astype(BF16)
        gk_ref[:, ks] = scale * (dot(score_high, q, 0, 0) + dot(score_low, q, 0, 0))
        coupled = pc_ref[h] * (scale * inside[:, one] * inverse[:, one])
        gvalue_ref[:, vs] = dot_left(coupled, g, 0, 0)
    row_ref[...] = row_part
    cold_ref[heads:, :] = jnp.zeros((8 - heads, n), F32)


def after_kernel(
    heads, me_ref, got_ref, later_ref, small_ref, odd_ref, tile_ref, unused_ref,
    give_ref, mine_ref, sum_ref,
):
    core = me_ref[0] % 2
    count, dv = mine_ref.shape[0], mine_ref.shape[2]
    per_head = count // (heads // 2)
    vectors = [
        jnp.sum(later_ref[:, h : h + 1] * got_ref[:, h, dv:], axis=0, keepdims=True)
        for h in range(heads)
    ]
    tile = jnp.concatenate(vectors + [tile_ref[:heads]], axis=0)
    sum_ref[...] = tile
    give_ref[count] = jnp.concatenate([tile, jnp.zeros((8, dv - 128), F32)], axis=1)
    odd, small = odd_ref.ready(), small_ref[...]

    def fill(to_even_ref, to_odd_ref):
        for i in range(heads // 2):
            at = core * (heads // 2) + i
            slab = slice(i * per_head, (i + 1) * per_head)
            after = got_ref[slab, :, :dv]
            to_odd_ref[slab] = after
            to_even_ref[slab] = pick(small[8:9], at) * after + pick(small[9:10], at) * odd[slab]

    @pl.when(core == 0)
    def _():
        fill(mine_ref, give_ref)

    @pl.when(core == 1)
    def _():
        fill(give_ref, mine_ref)


def weights_kernel(
    heads, me_ref, mine_ref, pair_ref, sum_ref, small_ref, cols_ref, k_ref, v_ref, mem_ref, row_ref,
    cold_ref, rows_ref, x_ref,
    after_ref, vector_ref, pay_ref,
):
    core = me_ref[0] % 2
    n = k_ref.shape[0]
    dk = k_ref.shape[1] // heads
    dv = v_ref.shape[1] // heads
    count = mine_ref.shape[0]
    after_ref[pl.ds(core * count, count)] = mine_ref[...]
    after_ref[pl.ds((1 - core) * count, count)] = pair_ref[:count]
    after_ref.send()
    mine, other = sum_ref[...], pair_ref[count, :, :128]
    key_scale = jnp.exp(unpack(cols_ref[...], 1, heads) + small_ref[heads : heads + 1])
    column_cross = jnp.zeros((n, 128), F32)
    through = jnp.zeros((1, 128), F32)
    vectors = []
    for h in range(heads):
        ks, vs, one = slice(dk * h, dk * (h + 1)), slice(dv * h, dv * (h + 1)), slice(h, h + 1)
        slab = slice(dk // 8 * h, dk // 8 * (h + 1))
        odd = mine[one] + other[one]
        even = small_ref[8:9, one] * odd + small_ref[9:10, one] * other[heads + h : heads + h + 1]
        vector = jnp.where(core == 0, even, odd)
        vectors.append(vector)
        following = after_ref[slab].reshape(dk, dv)
        carried = dot_right(k_ref[:, ks], following, 1, 0)
        along = jnp.sum(v_ref[:, vs].astype(F32) * carried, axis=1, keepdims=True)
        along = along + jnp.sum(k_ref[:, ks].astype(F32) * vector, axis=1, keepdims=True)
        column_cross = put(column_cross, key_scale[:, one] * along, h)
        product = jnp.sum(mem_ref[slab].reshape(dk, dv) * following, axis=0, keepdims=True)
        product = jnp.sum(product, axis=1, keepdims=True)
        product = product + jnp.sum(small_ref[one] * vector, axis=1, keepdims=True)
        through = put(through, product, h)
    vector_ref[...] = jnp.concatenate(vectors + [jnp.zeros((8 - heads, 128), F32)], axis=0)
    vector_ref.send()
    through = through * small_ref[heads + 1 : heads + 2]
    row = row_ref[...].T[:8]
    crossing = column_cross.T[:8]
    passing = jnp.broadcast_to(through, (128, 128)).T[:8, :1]
    inner = cold_ref[...]
    after = iota((n, n), 0) >= iota((n, n), 1)
    suffix = dot_exact(row - inner, after.astype(F32))
    prefix = dot_exact(crossing, 1.0 - after.astype(F32))
    grad_log = suffix + prefix + passing
    grad_forget = grad_log[:heads] / (1.0 + jnp.exp(rows_ref[heads : 2 * heads, :]))
    coefs = jnp.concatenate([(inner + crossing)[:heads], grad_forget], axis=0)
    high = coefs.astype(BF16).astype(F32)
    both = jnp.concatenate([high, coefs - high], axis=0).astype(BF16)
    product = dot(both, x_ref[...], 1, 0)
    result = product[: 2 * heads] + product[2 * heads :]
    tiles = result.shape[1] // 128
    for c in range(tiles):
        pay_ref[c] = result[:heads, 128 * c : 128 * (c + 1)]
        pay_ref[tiles + c] = result[heads:, 128 * c : 128 * (c + 1)]


def finish_kernel(
    heads, after_ref, vector_ref, small_ref, cols_ref, gk_ref, gvalue_ref, k_ref, v_ref,
    gkey_ref, out_ref,
):
    dk = gk_ref.shape[1] // heads
    dv = v_ref.shape[1] // heads
    key_scale = jnp.exp(unpack(cols_ref[...], 1, heads) + small_ref[heads : heads + 1])
    for h in range(heads):
        ks, vs, one = slice(dk * h, dk * (h + 1)), slice(dv * h, dv * (h + 1)), slice(h, h + 1)
        following = after_ref[dk // 8 * h : dk // 8 * (h + 1)].reshape(dk, dv)
        high, low = split(following)
        carried = dot(v_ref[:, vs], high, 1, 1) + dot(v_ref[:, vs], low, 1, 1) + vector_ref[one]
        gkey_ref[:, ks] = (gk_ref[:, ks] + key_scale[:, one] * carried).astype(BF16)
        carried = dot(k_ref[:, ks], high, 1, 0) + dot(k_ref[:, ks], low, 1, 0)
        out_ref[:, vs] = (gvalue_ref[:, vs] + key_scale[:, one] * carried).astype(BF16)


def sum_kernel(got_ref, out_ref):
    total = jnp.sum(got_ref[...], axis=0, keepdims=True)
    out_ref[...] = jnp.broadcast_to(total, out_ref.shape)


def place_kernel(got_ref, first_ref, second_ref):
    tiles = got_ref.shape[0] // 2
    for c in range(tiles):
        first_ref[:, 128 * c : 128 * (c + 1)] = got_ref[c]
        second_ref[:, 128 * c : 128 * (c + 1)] = got_ref[tiles + c]


class Fetched:
    def __init__(self, copy, ref):
        self.copy, self.ref, self.waited = copy, ref, False

    def ready(self):
        if not self.waited:
            self.copy.wait()
            self.waited = True
        return self.ref

    @property
    def shape(self):
        return self.ref.shape

    def __getitem__(self, at):
        return self.ready()[at]


class Stored:
    def __init__(self, copy, ref):
        self.copy, self.ref, self.sent = copy, ref, False

    @property
    def shape(self):
        return self.ref.shape

    def send(self):
        if not self.sent:
            self.copy.start()
            self.sent = True

    def __getitem__(self, at):
        return self.ref[at]

    def __setitem__(self, at, value):
        self.ref[at] = value


def call(body, outs, ins, limit=24):
    outs = [(k, o if isinstance(o, jax.ShapeDtypeStruct) else jax.ShapeDtypeStruct(o, F32)) for k, o in outs]
    spaces = {"s": pltpu.SMEM, "v": pltpu.VMEM, "h": pltpu.HBM, "m": pltpu.HBM, "a": pltpu.HBM}
    scratch = [
        (pltpu.SMEM if k == "m" else pltpu.VMEM)(a.shape, a.dtype) for k, a in ins + outs if k in "hm"
    ]
    scratch.append(pltpu.SemaphoreType.DMA((max(len(scratch), 1),)))

    def kernel(*refs):
        given, rest = refs[: len(ins)], refs[len(ins) :]
        results, buffers, sems = rest[: len(outs)], rest[len(outs) : -1], rest[-1]
        taken, made, used = [], [], 0
        for (kind, _), ref in zip(ins, given):
            if kind in "hm":
                copy = pltpu.make_async_copy(ref, buffers[used], sems.at[used])
                copy.start()
                ref = Fetched(copy, buffers[used])
                used += 1
            taken.append(ref)
        for (kind, _), ref in zip(outs, results):
            if kind == "h":
                copy = pltpu.make_async_copy(buffers[used], ref, sems.at[used])
                ref = Stored(copy, buffers[used])
                used += 1
            made.append(ref)
        body(*taken, *made)
        for ref in taken:
            if isinstance(ref, Fetched):
                ref.ready()
        for ref in made:
            if isinstance(ref, Stored):
                ref.send()
        for ref in made:
            if isinstance(ref, Stored):
                ref.copy.wait()

    return pl.pallas_call(
        kernel,
        out_shape=[pltpu.HBM(o.shape, o.dtype) if k == "h" else o for k, o in outs],
        in_specs=[pl.BlockSpec(memory_space=spaces[k]) for k, _ in ins],
        out_specs=[pl.BlockSpec(memory_space=spaces[k]) for k, _ in outs],
        scratch_shapes=scratch,
        compiler_params=pltpu.CompilerParams(vmem_limit_bytes=limit * 1024 * 1024),
    )(*[pltpu.with_memory_space_constraint(a, pltpu.HBM) if k in "hma" else a for k, a in ins])


def pack(items, heads):
    total = None
    for i, x in enumerate(items):
        x = jnp.where(iota(x.shape, 1) < heads, x, 0.0)
        x = pltpu.roll(x, heads * i, 1) if i else x
        total = x if total is None else total + x
    return total


def unpack(x, i, heads):
    return pltpu.roll(x, 128 - heads * i, 1) if i else x


def exchange(x, axis, groups=None):
    return lax.all_to_all(x, axis, 0, 0, axis_index_groups=groups)


def local(
    layer_input, queries, keys, values, grad_out, doc_pos, w_input, b_input, w_forget, b_forget
):
    x, q, k, v, g = layer_input[0], queries[0], keys[0], values[0], grad_out[0]
    heads = w_input.shape[1]
    n = q.shape[0]
    dk, dv = q.shape[1] // heads, v.shape[1] // heads
    scale = dk ** (-0.5)
    devices = lax.axis_size("ctx")
    count = devices // 2
    me = lax.axis_index("ctx").astype(jnp.int32).reshape(1)
    part = functools.partial
    cols = (n, 128)
    slabs = heads * dk // 8
    cores = [[2 * i + c for i in range(count)] for c in range(2)]

    def to_pair(a):
        return lax.ppermute(a, "ctx", [(i, i ^ 1) for i in range(devices)])

    low = jax.ShapeDtypeStruct

    def given(kinds, *arrays):
        return list(zip(kinds, arrays, strict=True))

    give, memory, tile, rows, token_cols = call(
        part(gates_kernel, heads),
        given("vvvhh", (slabs // 2 + 1, 8, dv), (slabs, 8, dv), (8, 128), (16, n), cols),
        given("shhhmmhhh", me, x, w_input.T, w_forget.T, b_input, b_forget, doc_pos, k, v),
    )
    pair = to_pair(give)
    pay, even_memory, even_tile = call(
        part(first_kernel, heads),
        given("vhh", (count, 8, dv + 128), (count, 8, dv), (8, 128)),
        given("svvv", me, memory, tile, pair),
    )
    first = exchange(pay, "ctx", cores)
    wl, pc, gv, sums = call(
        part(pairs_kernel, heads),
        given("hhhh", *[(heads, n, n)] * 3, cols),
        given("hhhhhh", rows, token_cols, q, k, v, g),
    )
    give, dual, coef, now, coef_later, later, small, tokens = call(
        part(dual_kernel, heads, scale),
        given(
            "vvvvhhhh", (count, 8, dv), (count, 8, dv), (2, count, 128), (16, 128),
            (2, count, 128), (count, 128), (16, 128), cols,
        ),
        given("svhhhhh", me, first, even_tile, token_cols, sums, q, g),
    )
    pair = to_pair(give)
    pay, odd_dual = call(
        part(second_kernel, heads),
        given("vh", (count, 8, 2 * dv), (count, 8, dv)),
        given("svvvvv", me, first, coef, now, dual, pair),
    )
    second = exchange(pay, "ctx", cores)
    give, mine = call(
        part(halves_kernel, heads),
        given("vv", (count, 8, dv), (count, 8, dv)),
        given("svhh", me, second, even_memory, small),
    )
    pair = to_pair(give)
    pay, states, tile, gt = call(
        part(vector_kernel, heads, scale),
        given("vhhh", (count, 8, dv + 128), (slabs, 8, dv), (8, 128), cols),
        given("svvvhhhhh", me, mine, pair, second, coef_later, tokens, sums, q, g),
    )
    third = exchange(pay, "ctx", cores)
    grad_q, gvalue, gk, row, cold = call(
        part(inner_kernel, heads, scale),
        given("hhhhh", low(q.shape, BF16), v.shape, k.shape, cols, (8, n)),
        given("hhhhhhhhhh", states, tokens, small, gt, wl, pc, gv, q, k, g),
    )
    give, mine, sums = call(
        part(after_kernel, heads),
        given("vvv", (count + 1, 8, dv), (count, 8, dv), (8, 128)),
        given("svhhhha", me, third, later, small, odd_dual, tile, gk),
    )
    pair = to_pair(give)
    chunks = 2 * x.shape[1] // 128
    following, vector, pay = call(
        part(weights_kernel, heads),
        given("hhv", (slabs, 8, dv), (8, 128), (chunks, heads, 128)),
        given(
            "svvvhhhhhhhhh", me, mine, pair, sums, small, token_cols, k, v, states, row, cold, rows, x
        ),
    )
    got = exchange(pay, "ctx")
    grad_k, grad_v = call(
        part(finish_kernel, heads),
        given("hh", low(k.shape, BF16), low(v.shape, BF16)),
        given("hhhhhhhh", following, vector, small, token_cols, gk, gvalue, k, v),
    )
    (pay,) = call(sum_kernel, given("v", (lax.axis_size("dp"), heads, 128)), given("v", got))
    got = exchange(pay, "dp")
    (pay,) = call(sum_kernel, given("v", (devices, heads, 128)), given("v", got))
    got = exchange(pay, "ctx")
    first, second = call(
        place_kernel, given("vv", (heads, x.shape[1]), (heads, x.shape[1])), given("v", got)
    )
    return (grad_q[None], grad_k[None], grad_v[None], first.T, second.T)


def solution(mesh):
    split_rows = P("dp", "ctx", None)
    placed = (split_rows,) * 5 + (P("dp", "ctx"),) + (P(),) * 4
    return jax.shard_map(
        local,
        mesh=mesh,
        in_specs=placed,
        out_specs=(split_rows, split_rows, split_rows, P(), P()),
        check_vma=False,
    )
```

```python
import functools

import jax
import jax.numpy as jnp
from jax import lax
from jax.experimental import pallas as pl
from jax.experimental.pallas import tpu as pltpu
from jax.sharding import PartitionSpec as P

NEG = -1e30
BIG = 1e30
F32 = jnp.float32
BF16 = jnp.bfloat16


def dot(a, b, ca, cb):
    return lax.dot_general(a, b, (((ca,), (cb,)), ((), ())), preferred_element_type=F32)


def split(x):
    high = x.astype(BF16)
    return high, (x - high.astype(F32)).astype(BF16)


def dot_left(x, b, ca, cb):
    high, low = split(x)
    return dot(high, b, ca, cb) + dot(low, b, ca, cb)


def dot_right(a, x, ca, cb):
    high, low = split(x)
    return dot(a, high, ca, cb) + dot(a, low, ca, cb)


def thirds(x):
    high = x.astype(BF16).astype(F32)
    middle = (x - high).astype(BF16).astype(F32)
    return [high, middle, x - high - middle]


def times_ones(x, ones):
    parts = dot(jnp.concatenate(thirds(x), axis=0).astype(BF16), ones.astype(F32).astype(BF16), 1, 0)
    return parts[:8] + parts[8:16] + parts[16:24]


def ones_times(ones, x):
    parts = dot(ones.astype(F32).astype(BF16), jnp.concatenate(thirds(x), axis=1).astype(BF16), 1, 0)
    return parts[:, :128] + parts[:, 128:256] + parts[:, 256:]


def iota(shape, dim):
    return lax.broadcasted_iota(jnp.int32, shape, dim)


def column_of(rows):
    r, n = rows.shape
    padded = jnp.concatenate([rows, jnp.zeros((128 - r, n), F32)], axis=0)
    return padded.T


def put(acc, col, h):
    return jnp.where(iota(acc.shape, 1) == h, col, acc)


def down(row, heads):
    return jnp.concatenate([pick(row, h) for h in range(heads)], axis=0)


def across(column):
    row = jnp.zeros((1, 128), F32)
    for h in range(column.shape[0]):
        row = put(row, column[h : h + 1], h)
    return row


def padded(rows):
    return jnp.concatenate([rows, jnp.zeros((8 - rows.shape[0], rows.shape[1]), F32)], axis=0)


def rows_times(rows, b):
    parts = dot(jnp.concatenate(thirds(padded(rows)), axis=0).astype(BF16), b, 1, 0)
    return parts[:8] + parts[8:16] + parts[16:24]


def pick(row, lane):
    return jnp.sum(jnp.where(iota(row.shape, 1) == lane, row, 0.0), axis=1, keepdims=True)


def gates_kernel(
    heads, me_ref, wi_ref, wf_ref, bi_ref, bf_ref, pos_ref, k_ref, x_ref, v_ref,
    give_ref, mem_ref, tile_ref, rows_ref,
):
    core = me_ref[0] % 2
    n = x_ref.shape[0]
    dk = k_ref.shape[1] // heads
    dv = v_ref.shape[1] // heads
    weights = [wi_ref[...].astype(F32), wf_ref[...].astype(F32)]
    weights.append(jnp.zeros((16 - 2 * heads, weights[0].shape[1]), F32))
    weights = jnp.concatenate(weights, axis=0).astype(BF16)
    k = k_ref[...]
    turned = k.T
    gates = dot(x_ref[...], weights, 1, 1)
    gates = jnp.concatenate([gates, jnp.zeros((n, 112), F32)], axis=1).T[: 2 * heads]
    row8 = iota(gates.shape, 0)
    for h in range(heads):
        gates = gates + jnp.where(row8 == h, bi_ref[h], 0.0)
        gates = gates + jnp.where(row8 == h + heads, bf_ref[h], 0.0)
    in_gate, forget_pre = gates[:heads], gates[heads:]
    log_forget = jnp.minimum(forget_pre, 0.0) - jnp.log1p(jnp.exp(-jnp.abs(forget_pre)))
    start = (pos_ref[...] == 0).astype(F32)
    stacked = jnp.concatenate([log_forget, start, jnp.zeros((7 - heads, n), F32)], axis=0)
    cum = times_ones(stacked, iota((n, n), 0) <= iota((n, n), 1))
    lc, dc = cum[:heads], cum[heads : heads + 1]
    total, last = lc[:, n - 1 :], dc[:, n - 1 :]
    key_log = jnp.where(dc == last, total - lc + in_gate, NEG)
    rows_ref[...] = jnp.concatenate(
        [in_gate, forget_pre, lc, key_log, dc, jnp.zeros((7, n), F32)], axis=0
    )
    rows_ref.send()
    own_max = jnp.max(key_log, axis=1, keepdims=True)
    weight = jnp.exp(key_log - own_max)
    sums = rows_times(weight, k)
    column = column_of(weight)
    for h in range(heads):
        weighted = v_ref[:, dv * h : dv * (h + 1)].astype(F32) * column[:, h : h + 1]
        memory = dot_right(turned[dk * h : dk * (h + 1)], weighted, 1, 0)
        mem_ref[dk // 8 * h : dk // 8 * (h + 1)] = memory.reshape(dk // 8, 8, dv)
    cut = jnp.where(last > 0.5, BIG, 0.0)
    tile = jnp.concatenate(
        [sums[h : h + 1, dk * h : dk * (h + 1)] for h in range(heads)]
        + [across(own_max), across(total - cut), across(in_gate[:, :1] - lc[:, :1])]
        + [jnp.broadcast_to(jnp.where(dc[:, :1] < 0.5, 1.0, 0.0), (1, 128))],
        axis=0,
    )
    tile_ref[...] = tile
    half = mem_ref.shape[0] // 2
    give_ref[:half] = mem_ref[pl.ds((1 - core) * half, half)]
    give_ref[half] = jnp.concatenate([tile, jnp.zeros((8, dv - 128), F32)], axis=1)


def first_kernel(heads, me_ref, mem_ref, tile_ref, got_ref, out_ref):
    core = me_ref[0] % 2
    half, dv = out_ref.shape[0], mem_ref.shape[2]
    mine, other = tile_ref[...], got_ref[half, :, :128]
    even = jnp.where(core == 0, mine, other)
    odd = jnp.where(core == 0, other, mine)
    chip_max = jnp.maximum(even[4:5] + odd[5:6], odd[4:5])
    keep = jnp.exp(even[4:5] + odd[5:6] - chip_max)
    add = jnp.exp(odd[4:5] - chip_max)
    vectors = [
        keep[:, h : h + 1] * even[h : h + 1] + add[:, h : h + 1] * odd[h : h + 1]
        for h in range(heads)
    ]
    both = jnp.where(iota(even.shape, 1) < heads, even, pltpu.roll(odd, heads, 1))
    tile = jnp.concatenate(vectors + [both[heads:]], axis=0)
    out_ref[:, :, dv:] = jnp.broadcast_to(tile[None], (half, 8, 128))
    weight_mine = jnp.where(core == 0, keep, add)
    weight_other = jnp.where(core == 0, add, keep)
    per_head = half // (heads // 2)
    for i in range(heads // 2):
        at = core * (heads // 2) + i
        slab = slice(i * per_head, (i + 1) * per_head)
        own = mem_ref[pl.ds(core * half + i * per_head, per_head)]
        out_ref[slab, :, :dv] = pick(weight_mine, at) * own + pick(weight_other, at) * got_ref[slab]


def pairs_kernel(
    heads, me_ref, mem_ref, tile_ref, got_ref, rows_ref, q_ref, k_ref, v_ref, g_ref,
    even_ref, even_tile_ref, turned_ref, wl_ref, pc_ref, gv_ref, sums_ref,
):
    core = me_ref[0] % 2
    half = even_ref.shape[0]
    even_ref[...] = jnp.where(core == 0, mem_ref[pl.ds(core * half, half)], got_ref[:half])
    even_ref.send()
    even_tile_ref[...] = jnp.where(core == 0, tile_ref[...], got_ref[half, :, :128])
    n = q_ref.shape[0]
    dk = k_ref.shape[1] // heads
    dv = v_ref.shape[1] // heads
    rows = rows_ref[...]
    lc = column_of(rows)
    place = 4 * heads
    mask = (iota((n, n), 0) >= iota((n, n), 1)) & (lc[:, place : place + 1] == rows[place : place + 1])
    turned_ref[...] = q_ref[...].T
    sums = jnp.zeros((n, 128), F32)
    for h in range(heads):
        offset = rows[h : h + 1] - rows[2 * heads + h : 2 * heads + h + 1]
        pair_log = jnp.where(mask, lc[:, 2 * heads + h : 2 * heads + h + 1] + offset, NEG)
        row_max = jnp.max(pair_log, axis=1, keepdims=True)
        weight = jnp.exp(pair_log - row_max)
        ks, vs = slice(dk * h, dk * (h + 1)), slice(dv * h, dv * (h + 1))
        coupled = dot(q_ref[:, ks], k_ref[:, ks], 1, 1) * weight
        grad_pair = dot(g_ref[:, vs], v_ref[:, vs], 1, 1)
        wl_ref[h] = weight
        pc_ref[h] = coupled
        gv_ref[h] = grad_pair
        sums = put(sums, row_max, h)
        sums = put(sums, jnp.sum(coupled, axis=1, keepdims=True), heads + h)
        sums = put(sums, jnp.sum(coupled * grad_pair, axis=1, keepdims=True), 2 * heads + h)
    sums_ref[...] = sums.T[: sums_ref.shape[0]]


def shift_down(x, d, fill):
    return jnp.where(iota(x.shape, 0) < d, fill, pltpu.roll(x, d, 0))


def shift_up(x, d, fill):
    size = x.shape[0]
    return jnp.where(iota(x.shape, 0) >= size - d, fill, pltpu.roll(x, size - d, 0))


def dual_kernel(
    heads, scale, me_ref, got_ref, tile_ref, rows_ref, sums_ref, turned_ref, g_ref,
    give_ref, dual_ref, coef_ref, now_ref, coef_later_ref, later_ref, small_ref, tokens_ref,
):
    count = got_ref.shape[0]
    n = g_ref.shape[0]
    dk = turned_ref.shape[0] // heads
    dv = g_ref.shape[1] // heads
    me = me_ref[0]
    core, chip = me % 2, me // 2
    max_even, total_even = got_ref[:, heads, dv:], got_ref[:, heads + 1, dv:]
    first_even, valid_even = got_ref[:, heads + 2, dv:], got_ref[:, heads + 3, dv:]
    max_odd, total_odd, first_odd, valid_odd = (
        pltpu.roll(x, 128 - heads, 1) for x in (max_even, total_even, first_even, valid_even)
    )
    row = iota(max_even.shape, 0)
    lane = iota(max_even.shape, 1)
    steps = [1 << i for i in range((count - 1).bit_length())]
    chip_max = jnp.maximum(max_even + total_odd, max_odd)
    total = total_even + total_odd
    t, m = total, chip_max
    for d in steps:
        m = jnp.maximum(shift_down(m, d, NEG) + t, m)
        t = shift_down(t, d, 0.0) + t
    in_even = shift_down(m, 1, NEG)
    in_odd = jnp.maximum(in_even + total_even, max_even)
    dual_even = jnp.where(valid_even > 0.5, -jnp.maximum(in_even, first_even), NEG)
    dual_odd = jnp.where(valid_odd > 0.5, -jnp.maximum(in_odd, first_odd), NEG)
    chip_dual = jnp.maximum(dual_even, total_even + dual_odd)
    t, r = total, chip_dual
    for d in steps:
        r = jnp.maximum(r, t + shift_up(r, d, NEG))
        t = t + shift_up(t, d, 0.0)
    later_odd = shift_up(r, 1, NEG)
    later_even = jnp.maximum(dual_odd, total_odd + later_odd)
    my_head = (heads // 2) * core + chip // (2 * count // heads)
    coefs = (
        jnp.exp(in_even + total - m),
        jnp.exp(chip_max - m),
        jnp.exp(total + later_odd - r),
        jnp.exp(chip_dual - r),
    )
    for i, c in enumerate(coefs):
        mine = jnp.sum(jnp.where(lane == my_head, c, 0.0), axis=1, keepdims=True)
        (coef_ref if i < 2 else coef_later_ref)[i % 2] = jnp.broadcast_to(mine, c.shape)

    def here(x):
        return jnp.sum(jnp.where(row == chip, x, 0.0), axis=0, keepdims=True)

    def mine_of(even, odd):
        return here(jnp.where(core == 0, even, odd))

    in_me, later_me = mine_of(in_even, in_odd), mine_of(later_even, later_odd)
    dual_me, total_me = mine_of(dual_even, dual_odd), mine_of(total_even, total_odd)
    keep = here(jnp.exp(in_even + total_even - in_odd))
    add = here(jnp.exp(max_even - in_odd))
    later_row = iota((count, count), 0) < iota((count, count), 1)
    between = ones_times(later_row, jnp.where(row < chip, total, 0.0))
    weight = jnp.where(
        row < chip, jnp.exp(jnp.minimum(chip_max + between - here(in_even), 0.0)), 0.0
    )
    earlier_row = iota((count, count), 0) > iota((count, count), 1)
    between = ones_times(earlier_row, jnp.where(row > chip, total, 0.0))
    source = jnp.where(core == 0, dual_even, total_even + dual_odd)
    later_ref[...] = jnp.where(
        row > chip, jnp.exp(jnp.minimum(source + between - here(later_odd), 0.0)), 0.0
    )
    even_tile = tile_ref[...]
    vectors = []
    for h in range(heads):
        one = slice(h, h + 1)
        vector = jnp.sum(weight[:, one] * got_ref[:, h, dv:], axis=0, keepdims=True)
        second = keep[:, one] * vector + add[:, one] * even_tile[one]
        vectors.append(jnp.where(core == 0, vector, second))
    small = jnp.concatenate(
        vectors
        + [
            later_me,
            jnp.exp(in_me + total_me + later_me),
            keep,
            add,
            here(jnp.exp(total_odd + later_odd - later_even)),
            here(jnp.exp(dual_odd - later_even)),
            here(jnp.exp(dual_even - chip_dual)),
            here(jnp.exp(total_even + dual_odd - chip_dual)),
            jnp.zeros((8 - heads, 128), F32),
        ],
        axis=0,
    )

    small_ref[...] = small
    small_ref.send()
    now_ref[...] = small
    lc = rows_ref[2 * heads : 3 * heads]
    open_query = rows_ref[4 * heads : 4 * heads + 1] < 0.5
    inner_max = sums_ref[:heads]
    cross_log = jnp.where(open_query, lc + down(in_me, heads), NEG)
    row_max = jnp.maximum(inner_max, cross_log)
    inside = jnp.exp(inner_max - row_max)
    cross = jnp.exp(cross_log - row_max)
    qn = [
        rows_times(small[:heads], turned_ref[dk * h : dk * (h + 1)])[h : h + 1] for h in range(heads)
    ]
    qn = jnp.concatenate(qn, axis=0)
    sums = scale * (sums_ref[heads : 2 * heads] * inside + cross * qn)
    floor = jnp.exp(-row_max)
    size = jnp.abs(sums)
    inverse = 1.0 / jnp.maximum(size, floor)
    active = jnp.where(size > floor, jnp.where(sums > 0.0, 1.0, -1.0), 0.0)
    query_weight = jnp.exp(jnp.minimum(lc - row_max - down(dual_me, heads), 0.0))
    query_weight = jnp.where(open_query, query_weight, 0.0)
    tokens_ref[...] = jnp.concatenate([inside, cross, inverse, active, query_weight, qn], axis=0)
    tokens_ref.send()
    grad_weight = column_of(query_weight * inverse * scale)
    half = give_ref.shape[0]
    per_head = dk // 8
    for h in range(heads):
        weighted = g_ref[:, dv * h : dv * (h + 1)].astype(F32) * grad_weight[:, h : h + 1]
        memory = dot_right(turned_ref[dk * h : dk * (h + 1)], weighted, 1, 0).reshape(per_head, 8, dv)
        slab = slice(per_head * h % half, per_head * h % half + per_head)

        @pl.when(core == h // (heads // 2))
        def _():
            dual_ref[slab] = memory

        @pl.when(core != h // (heads // 2))
        def _():
            give_ref[slab] = memory


def wide(coef_ref, i, j, reps):
    return jnp.concatenate([coef_ref[i, pl.ds(j, 1), :]] * reps, axis=1)


def second_kernel(
    heads, me_ref, got_ref, coef_ref, small_ref, dual_ref, pair_ref, out_ref
):
    core = me_ref[0] % 2
    count, dv = got_ref.shape[0], dual_ref.shape[2]
    reps = dv // 128

    def forward(j, state):
        out_ref[j, :, :dv] = state
        step = wide(coef_ref, 1, j, reps) * got_ref[j, :, :dv]
        return wide(coef_ref, 0, j, reps) * state + step

    even, odd = small_ref[10:11], small_ref[11:12]
    weight_mine = jnp.where(core == 0, even, odd)
    weight_other = jnp.where(core == 0, odd, even)
    per_head = count // (heads // 2)
    for i in range(heads // 2):
        at = core * (heads // 2) + i
        slab = slice(i * per_head, (i + 1) * per_head)
        step = pick(weight_other, at) * pair_ref[slab]
        out_ref[slab, :, dv:] = pick(weight_mine, at) * dual_ref[slab] + step
    lax.fori_loop(0, count, forward, jnp.zeros((8, dv), F32), unroll=8)


def odd_kernel(me_ref, dual_ref, pair_ref, odd_ref):
    odd_ref[...] = jnp.where(me_ref[0] % 2 == 0, pair_ref[...], dual_ref[...])


def halves_kernel(heads, me_ref, got_ref, even_ref, small_ref, unused_ref, give_ref, mine_ref):
    core = me_ref[0] % 2
    count, dv = give_ref.shape[0], give_ref.shape[2]
    per_head = count // (heads // 2)
    even, small = even_ref, small_ref[...]

    def fill(to_even_ref, to_odd_ref):
        for i in range(heads // 2):
            at = core * (heads // 2) + i
            slab = slice(i * per_head, (i + 1) * per_head)
            before = got_ref[slab, :, :dv]
            to_even_ref[slab] = before
            to_odd_ref[slab] = pick(small[6:7], at) * before + pick(small[7:8], at) * even[slab]

    @pl.when(core == 0)
    def _():
        fill(mine_ref, give_ref)

    @pl.when(core == 1)
    def _():
        fill(give_ref, mine_ref)


def vector_kernel(
    heads, scale, me_ref, mine_ref, pair_ref, got_ref, coef_ref, tokens_ref, sums_ref, q_ref, g_ref,
    out_ref, mem_ref, tile_ref, gt_ref,
):
    core = me_ref[0] % 2
    n = q_ref.shape[0]
    dk = q_ref.shape[1] // heads
    dv = g_ref.shape[1] // heads
    count = got_ref.shape[0]
    reps = dv // 128
    mem_ref[pl.ds(core * count, count)] = mine_ref[...]
    mem_ref[pl.ds((1 - core) * count, count)] = pair_ref[...]
    mem_ref.send()
    coef = coef_ref

    def backward(i, state):
        j = count - 1 - i
        for i in range(2):
            for c in range(reps):
                out_ref[j, i * reps + c] = state[4 * i : 4 * (i + 1), 128 * c : 128 * (c + 1)]
        step = wide(coef, 1, j, reps) * got_ref[j, :, dv:]
        return wide(coef, 0, j, reps) * state + step

    lax.fori_loop(0, count, backward, jnp.zeros((8, dv), F32), unroll=8)
    gc = jnp.zeros((n, 128), F32)
    for h in range(heads):
        memory = mem_ref[dk // 8 * h : dk // 8 * (h + 1)].reshape(dk, dv)
        crossing = dot_right(q_ref[:, dk * h : dk * (h + 1)], memory, 1, 0)
        along = g_ref[:, dv * h : dv * (h + 1)].astype(F32) * crossing
        gc = put(gc, jnp.sum(along, axis=1, keepdims=True), h)
    inside, cross, inverse, active, query_weight = (
        tokens_ref[heads * i : heads * (i + 1)] for i in range(5)
    )
    gc = gc.T[:heads]
    gt = sums_ref[2 * heads : 3 * heads] * inside + cross * gc
    gt = -scale * gt * inverse * inverse * active
    gt_ref[...] = jnp.concatenate([gt, gc], axis=0)
    gt_ref.send()
    vectors = rows_times(query_weight * gt * scale, q_ref[...])
    vectors = [vectors[h : h + 1, dk * h : dk * (h + 1)] for h in range(heads)]
    tile = jnp.concatenate(vectors + [jnp.zeros((8 - heads, 128), F32)], axis=0)
    tile_ref[...] = tile
    out_ref[:, 2 * reps] = jnp.broadcast_to(tile[None, :4], (count, 4, 128))


def inner_kernel(
    heads, scale, mem_ref, tokens_ref, small_ref, gt_ref, wl_ref, pc_ref, gv_ref,
    q_ref, k_ref, g_ref,
    gq_ref, gvalue_ref, gk_ref, row_ref, cold_ref,
):
    n = q_ref.shape[0]
    dk = q_ref.shape[1] // heads
    dv = g_ref.shape[1] // heads
    tokens = column_of(jnp.concatenate([tokens_ref[...], gt_ref[...]], axis=0))
    inside, cross, inverse, qn, gt, gc = (unpack(tokens, i, heads) for i in (0, 1, 2, 5, 6, 7))
    row_part = scale * cross * (inverse * gc + gt * qn)
    for h in range(heads):
        ks, vs = slice(dk * h, dk * (h + 1)), slice(dv * h, dv * (h + 1))
        one = slice(h, h + 1)
        q, k, g = q_ref[:, ks], k_ref[:, ks], g_ref[:, vs]
        memory = mem_ref[dk // 8 * h : dk // 8 * (h + 1)].reshape(dk, dv)
        factor = inside[:, one] * (inverse[:, one] * gv_ref[h] + gt[:, one])
        pair_grad = factor * pc_ref[h]
        cold_ref[one, :] = scale * jnp.sum(pair_grad, axis=0, keepdims=True)
        row_part = row_part + put(
            jnp.zeros((n, 128), F32), scale * jnp.sum(pair_grad, axis=1, keepdims=True), h
        )
        score_high, score_low = split(factor * wl_ref[h])
        grad_query = dot(score_high, k, 1, 0) + dot(score_low, k, 1, 0)
        grad_query = grad_query + cross[:, one] * (
            inverse[:, one] * dot_right(g, memory, 1, 1) + gt[:, one] * small_ref[one]
        )
        gq_ref[:, ks] = (scale * grad_query).astype(BF16)
        gk_ref[:, ks] = scale * (dot(score_high, q, 0, 0) + dot(score_low, q, 0, 0))
        coupled = pc_ref[h] * (scale * inside[:, one] * inverse[:, one])
        gvalue_ref[:, vs] = dot_left(coupled, g, 0, 0)
    row_ref[...] = row_part.T[:8]
    cold_ref[heads:, :] = jnp.zeros((8 - heads, n), F32)


def after_kernel(
    heads, me_ref, got_ref, later_ref, small_ref, odd_ref, tile_ref, unused_ref,
    give_ref, mine_ref, sum_ref,
):
    core = me_ref[0] % 2
    count, dv = mine_ref.shape[0], mine_ref.shape[2]
    reps = dv // 128
    per_head = count // (heads // 2)
    vectors = [
        jnp.sum(later_ref[:, h : h + 1] * got_ref[:, 2 * reps, h, :], axis=0, keepdims=True)
        for h in range(heads)
    ]
    tile = jnp.concatenate(vectors + [tile_ref[:heads]], axis=0)
    sum_ref[...] = tile
    give_ref[count] = jnp.concatenate([tile, jnp.zeros((8, dv - 128), F32)], axis=1)
    odd, small = odd_ref.ready(), small_ref[...]

    def fill(to_even_ref, to_odd_ref):
        for i in range(heads // 2):
            at = core * (heads // 2) + i
            slab = slice(i * per_head, (i + 1) * per_head)
            after = [
                jnp.concatenate([got_ref[slab, i * reps + c] for c in range(reps)], axis=2)
                for i in range(2)
            ]
            after = jnp.concatenate(after, axis=1)
            to_odd_ref[slab] = after
            to_even_ref[slab] = pick(small[8:9], at) * after + pick(small[9:10], at) * odd[slab]

    @pl.when(core == 0)
    def _():
        fill(mine_ref, give_ref)

    @pl.when(core == 1)
    def _():
        fill(give_ref, mine_ref)


def weights_kernel(
    heads, me_ref, mine_ref, pair_ref, sum_ref, small_ref, k_ref, v_ref, mem_ref, rows_ref, row_ref,
    cold_ref, x_ref,
    after_ref, vector_ref, pay_ref,
):
    core = me_ref[0] % 2
    n = k_ref.shape[0]
    dk = k_ref.shape[1] // heads
    dv = v_ref.shape[1] // heads
    count = mine_ref.shape[0]
    after_ref[pl.ds(core * count, count)] = mine_ref[...]
    after_ref[pl.ds((1 - core) * count, count)] = pair_ref[:count]
    after_ref.send()
    mine, other = sum_ref[...], pair_ref[count, :, :128]
    column_cross = jnp.zeros((n, 128), F32)
    through = []
    vectors = []
    for h in range(heads):
        ks, vs, one = slice(dk * h, dk * (h + 1)), slice(dv * h, dv * (h + 1)), slice(h, h + 1)
        slab = slice(dk // 8 * h, dk // 8 * (h + 1))
        odd = mine[one] + other[one]
        even = small_ref[8:9, one] * odd + small_ref[9:10, one] * other[heads + h : heads + h + 1]
        vector = jnp.where(core == 0, even, odd)
        vectors.append(vector)
        following = after_ref[slab].reshape(dk, dv)
        carried = dot_right(k_ref[:, ks], following, 1, 0)
        along = jnp.sum(v_ref[:, vs].astype(F32) * carried, axis=1, keepdims=True)
        along = along + jnp.sum(k_ref[:, ks].astype(F32) * vector, axis=1, keepdims=True)
        column_cross = put(column_cross, along, h)
        product = jnp.sum(mem_ref[slab].reshape(dk, dv) * following, axis=0, keepdims=True)
        product = jnp.sum(product, axis=1, keepdims=True)
        product = product + jnp.sum(small_ref[one] * vector, axis=1, keepdims=True)
        through.append(product)
    vector_ref[...] = jnp.concatenate(vectors + [jnp.zeros((8 - heads, 128), F32)], axis=0)
    vector_ref.send()
    passing = padded(jnp.concatenate(through, axis=0) * down(small_ref[heads + 1 : heads + 2], heads))
    key_scale = jnp.exp(rows_ref[3 * heads : 4 * heads] + down(small_ref[heads : heads + 1], heads))
    crossing = padded(column_cross.T[:heads] * key_scale)
    row, inner = row_ref[...], cold_ref[...]
    after = iota((n, n), 0) >= iota((n, n), 1)
    suffix = times_ones(row - inner, after)
    prefix = times_ones(crossing, jnp.logical_not(after))
    grad_log = suffix + prefix + passing
    grad_forget = grad_log[:heads] / (1.0 + jnp.exp(rows_ref[heads : 2 * heads, :]))
    coefs = jnp.concatenate([(inner + crossing)[:heads], grad_forget], axis=0)
    high = coefs.astype(BF16).astype(F32)
    both = jnp.concatenate([high, coefs - high], axis=0).astype(BF16)
    product = dot(both, x_ref[...], 1, 0)
    result = product[: 2 * heads] + product[2 * heads :]
    tiles, _, width = pay_ref.shape
    for c in range(tiles):
        pay_ref[c] = result[:, width * c : width * (c + 1)]


def finish_kernel(
    heads, after_ref, vector_ref, small_ref, rows_ref, gk_ref, gvalue_ref, k_ref, v_ref,
    gkey_ref, out_ref,
):
    dk = gk_ref.shape[1] // heads
    dv = v_ref.shape[1] // heads
    key_scale = jnp.exp(unpack(column_of(rows_ref[...]), 3, heads) + small_ref[heads : heads + 1])
    for h in range(heads):
        ks, vs, one = slice(dk * h, dk * (h + 1)), slice(dv * h, dv * (h + 1)), slice(h, h + 1)
        following = after_ref[dk // 8 * h : dk // 8 * (h + 1)].reshape(dk, dv)
        high, low = split(following)
        carried = dot(v_ref[:, vs], high, 1, 1) + dot(v_ref[:, vs], low, 1, 1) + vector_ref[one]
        gkey_ref[:, ks] = (gk_ref[:, ks] + key_scale[:, one] * carried).astype(BF16)
        carried = dot(k_ref[:, ks], high, 1, 0) + dot(k_ref[:, ks], low, 1, 0)
        out_ref[:, vs] = (gvalue_ref[:, vs] + key_scale[:, one] * carried).astype(BF16)


def sum_kernel(got_ref, *refs):
    out_ref = refs[-1]
    total = jnp.sum(got_ref[...], axis=0, keepdims=True)
    out_ref[...] = jnp.broadcast_to(total, out_ref.shape)


def place_kernel(got_ref, first_ref, second_ref):
    heads = first_ref.shape[0]
    tiles, _, width = got_ref.shape
    for c in range(tiles):
        first_ref[:, width * c : width * (c + 1)] = got_ref[c, :heads]
        second_ref[:, width * c : width * (c + 1)] = got_ref[c, heads:]


class Fetched:
    def __init__(self, copy, ref):
        self.copy, self.ref, self.waited = copy, ref, False

    def ready(self):
        if not self.waited:
            self.copy.wait()
            self.waited = True
        return self.ref

    @property
    def shape(self):
        return self.ref.shape

    def __getitem__(self, at):
        return self.ready()[at]


class Stored:
    def __init__(self, copy, ref):
        self.copy, self.ref, self.sent = copy, ref, False

    @property
    def shape(self):
        return self.ref.shape

    def send(self):
        if not self.sent:
            self.copy.start()
            self.sent = True

    def __getitem__(self, at):
        return self.ref[at]

    def __setitem__(self, at, value):
        self.ref[at] = value


def call(body, outs, ins, limit=24):
    outs = [(k, o if isinstance(o, jax.ShapeDtypeStruct) else jax.ShapeDtypeStruct(o, F32)) for k, o in outs]
    spaces = {"s": pltpu.SMEM, "v": pltpu.VMEM, "h": pltpu.HBM, "m": pltpu.HBM, "a": pltpu.HBM}
    scratch = [
        (pltpu.SMEM if k == "m" else pltpu.VMEM)(a.shape, a.dtype) for k, a in ins + outs if k in "hm"
    ]
    scratch.append(pltpu.SemaphoreType.DMA((max(len(scratch), 1),)))

    def kernel(*refs):
        given, rest = refs[: len(ins)], refs[len(ins) :]
        results, buffers, sems = rest[: len(outs)], rest[len(outs) : -1], rest[-1]
        taken, made, used = [], [], 0
        for (kind, _), ref in zip(ins, given):
            if kind in "hm":
                copy = pltpu.make_async_copy(ref, buffers[used], sems.at[used])
                copy.start()
                ref = Fetched(copy, buffers[used])
                used += 1
            taken.append(ref)
        for (kind, _), ref in zip(outs, results):
            if kind == "h":
                copy = pltpu.make_async_copy(buffers[used], ref, sems.at[used])
                ref = Stored(copy, buffers[used])
                used += 1
            made.append(ref)
        body(*taken, *made)
        for ref in taken:
            if isinstance(ref, Fetched):
                ref.ready()
        for ref in made:
            if isinstance(ref, Stored):
                ref.send()
        for ref in made:
            if isinstance(ref, Stored):
                ref.copy.wait()

    return pl.pallas_call(
        kernel,
        out_shape=[pltpu.HBM(o.shape, o.dtype) if k == "h" else o for k, o in outs],
        in_specs=[pl.BlockSpec(memory_space=spaces[k]) for k, _ in ins],
        out_specs=[pl.BlockSpec(memory_space=spaces[k]) for k, _ in outs],
        scratch_shapes=scratch,
        compiler_params=pltpu.CompilerParams(vmem_limit_bytes=limit * 1024 * 1024),
    )(*[pltpu.with_memory_space_constraint(a, pltpu.HBM) if k in "hma" else a for k, a in ins])


def unpack(x, i, heads):
    return pltpu.roll(x, 128 - heads * i, 1) if i else x


def exchange(x, axis, groups=None):
    return lax.all_to_all(x, axis, 0, 0, axis_index_groups=groups)


def local(
    layer_input, queries, keys, values, grad_out, doc_pos, w_input, b_input, w_forget, b_forget
):
    x, q, k, v, g = layer_input[0], queries[0], keys[0], values[0], grad_out[0]
    heads = w_input.shape[1]
    n = q.shape[0]
    dk, dv = q.shape[1] // heads, v.shape[1] // heads
    scale = dk ** (-0.5)
    devices = lax.axis_size("ctx")
    count = devices // 2
    me = lax.axis_index("ctx").astype(jnp.int32).reshape(1)
    part = functools.partial
    slabs = heads * dk // 8
    cores = [[2 * i + c for i in range(count)] for c in range(2)]

    def to_pair(a):
        return lax.ppermute(a, "ctx", [(i, i ^ 1) for i in range(devices)])

    low = jax.ShapeDtypeStruct

    def given(kinds, *arrays):
        return list(zip(kinds, arrays, strict=True))

    give, memory, tile, rows = call(
        part(gates_kernel, heads),
        given("vvvh", (slabs // 2 + 1, 8, dv), (slabs, 8, dv), (8, 128), (24, n)),
        given("shhmmhhhh", me, w_input.T, w_forget.T, b_input, b_forget, doc_pos, k, x, v),
    )
    pair = to_pair(give)
    (pay,) = call(
        part(first_kernel, heads),
        given("v", (count, 8, dv + 128)),
        given("svvv", me, memory, tile, pair),
    )
    first = exchange(pay, "ctx", cores)
    even_memory, even_tile, turned, wl, pc, gv, sums = call(
        part(pairs_kernel, heads),
        given(
            "hvvhhhv", (count, 8, dv), (8, 128), low((heads * dk, n), BF16), *[(heads, n, n)] * 3, (16, n)
        ),
        given("svvvhhhhh", me, memory, tile, pair, rows, q, k, v, g),
    )
    give, dual, coef, now, coef_later, later, small, tokens = call(
        part(dual_kernel, heads, scale),
        given(
            "vvvvvvhh", (count, 8, dv), (count, 8, dv), (2, count, 128), (16, 128),
            (2, count, 128), (count, 128), (16, 128), (24, n),
        ),
        given("svvhvvh", me, first, even_tile, rows, sums, turned, g),
    )
    pair = to_pair(give)
    (pay,) = call(
        part(second_kernel, heads),
        given("v", (count, 8, 2 * dv)),
        given("svvvvv", me, first, coef, now, dual, pair),
    )
    second = exchange(pay, "ctx", cores)
    (odd_dual,) = call(odd_kernel, given("h", (count, 8, dv)), given("svv", me, dual, pair))
    give, mine = call(
        part(halves_kernel, heads),
        given("vv", (count, 8, dv), (count, 8, dv)),
        given("svvva", me, second, even_memory, now, odd_dual),
    )
    pair = to_pair(give)
    pay, states, tile, gt = call(
        part(vector_kernel, heads, scale),
        given("vhvh", (count, 2 * dv // 128 + 1, 4, 128), (slabs, 8, dv), (8, 128), (8, n)),
        given("svvvvvvvv", me, mine, pair, second, coef_later, tokens, sums, q, g),
    )
    third = exchange(pay, "ctx", cores)
    grad_q, gvalue, gk, row, cold = call(
        part(inner_kernel, heads, scale),
        given("hhhhh", low(q.shape, BF16), v.shape, k.shape, (8, n), (8, n)),
        given("hhhhhhhhhh", states, tokens, small, gt, wl, pc, gv, q, k, g),
    )
    give, mine, sums = call(
        part(after_kernel, heads),
        given("vvv", (count + 1, 8, dv), (count, 8, dv), (8, 128)),
        given("svvvhva", me, third, later, now, odd_dual, tile, gk),
    )
    pair = to_pair(give)
    batch, across_x = lax.axis_size("dp"), 4
    tiles = batch * across_x
    at = [[[(z * across_x + i) * 2 + c for i in range(across_x)] for c in range(2)] for z in range(count // across_x)]
    planes = [[i * batch + d for i in row for d in range(batch)] for z in at for row in z]
    lines = [[row[i] for z in at for row in z] for i in range(across_x)]
    chunk = (8, x.shape[1] // tiles)
    following, vector, pay = call(
        part(weights_kernel, heads),
        given("hhv", (slabs, 8, dv), (8, 128), (tiles, *chunk)),
        given(
            "svvvvvvhhhhv", me, mine, pair, sums, now, k, v, states, rows, row, cold, x
        ),
    )
    got = exchange(pay, ("ctx", "dp"), planes)
    grad_k, grad_v = call(
        part(finish_kernel, heads),
        given("hh", low(k.shape, BF16), low(v.shape, BF16)),
        given("hhhhhhhh", following, vector, small, rows, gk, gvalue, k, v),
    )
    (pay,) = call(sum_kernel, given("v", (len(lines[0]), *chunk)), given("va", got, grad_k))
    got = exchange(pay, "ctx", lines)
    (pay,) = call(sum_kernel, given("v", (tiles, *chunk)), given("v", got))
    got = exchange(pay, ("ctx", "dp"), planes)
    first, second = call(
        place_kernel, given("vv", (heads, x.shape[1]), (heads, x.shape[1])), given("v", got)
    )
    return (grad_q[None], grad_k[None], grad_v[None], first.T, second.T)


def solution(mesh):
    split_rows = P("dp", "ctx", None)
    placed = (split_rows,) * 5 + (P("dp", "ctx"),) + (P(),) * 4
    return jax.shard_map(
        local,
        mesh=mesh,
        in_specs=placed,
        out_specs=(split_rows, split_rows, split_rows, P(), P()),
        check_vma=False,
    )
```

```python
import functools

import jax
import jax.numpy as jnp
from jax import lax
from jax.experimental import pallas as pl
from jax.experimental.pallas import tpu as pltpu
from jax.sharding import PartitionSpec as P

NEG = -1e30
BIG = 1e30
F32 = jnp.float32
BF16 = jnp.bfloat16


def dot(a, b, ca, cb):
    return lax.dot_general(a, b, (((ca,), (cb,)), ((), ())), preferred_element_type=F32)


def split(x):
    high = x.astype(BF16)
    return high, (x - high.astype(F32)).astype(BF16)


def dot_left(x, b, ca, cb):
    high, low = split(x)
    return dot(high, b, ca, cb) + dot(low, b, ca, cb)


def dot_right(a, x, ca, cb):
    high, low = split(x)
    return dot(a, high, ca, cb) + dot(a, low, ca, cb)


def thirds(x):
    high = x.astype(BF16).astype(F32)
    middle = (x - high).astype(BF16).astype(F32)
    return [high, middle, x - high - middle]


def times_ones(x, ones):
    parts = dot(jnp.concatenate(thirds(x), axis=0).astype(BF16), ones.astype(F32).astype(BF16), 1, 0)
    return parts[:8] + parts[8:16] + parts[16:24]


def ones_times(ones, x):
    parts = dot(ones.astype(F32).astype(BF16), jnp.concatenate(thirds(x), axis=1).astype(BF16), 1, 0)
    return parts[:, :128] + parts[:, 128:256] + parts[:, 256:]


def iota(shape, dim):
    return lax.broadcasted_iota(jnp.int32, shape, dim)


def column_of(rows):
    r, n = rows.shape
    padded = jnp.concatenate([rows, jnp.zeros((128 - r, n), F32)], axis=0)
    return padded.T


def put(acc, col, h):
    return jnp.where(iota(acc.shape, 1) == h, col, acc)


def down(row, heads):
    return jnp.concatenate([pick(row, h) for h in range(heads)], axis=0)


def across(column):
    row = jnp.zeros((1, 128), F32)
    for h in range(column.shape[0]):
        row = put(row, column[h : h + 1], h)
    return row


def padded(rows):
    return jnp.concatenate([rows, jnp.zeros((8 - rows.shape[0], rows.shape[1]), F32)], axis=0)


def rows_times(rows, b):
    parts = dot(jnp.concatenate(thirds(padded(rows)), axis=0).astype(BF16), b, 1, 0)
    return parts[:8] + parts[8:16] + parts[16:24]


def pick(row, lane):
    return jnp.sum(jnp.where(iota(row.shape, 1) == lane, row, 0.0), axis=1, keepdims=True)


def outer_products(side, heads, turned_ref, rows_ref, columns, out_ref):
    half = heads // 2
    dk, dv = turned_ref.shape[0] // heads, rows_ref.shape[1] // heads
    columns = jnp.where(side == 0, columns, pltpu.roll(columns, 128 - half, 1))
    for i in range(half):
        at = pl.multiple_of((side * half + i) * dv, dv)
        weighted = rows_ref[:, pl.ds(at, dv)].astype(F32) * columns[:, i : i + 1]
        at = pl.multiple_of((side * half + i) * dk, dk)
        product = dot_right(turned_ref[pl.ds(at, dk), :], weighted, 1, 0)
        out_ref[dk // 8 * i : dk // 8 * (i + 1)] = product.reshape(dk // 8, 8, dv)


def products_kernel(heads, me_ref, turned_ref, rows_ref, column_ref, out_ref):
    outer_products(me_ref[0] % 2, heads, turned_ref, rows_ref, column_ref[...], out_ref)


def gates_kernel(
    heads, me_ref, wi_ref, wf_ref, bi_ref, bf_ref, pos_ref, k_ref, x_ref, v_ref,
    give_ref, turned_ref, column_ref, tile_ref, rows_ref,
):
    core = me_ref[0] % 2
    n = x_ref.shape[0]
    dk = k_ref.shape[1] // heads
    dv = v_ref.shape[1] // heads
    weights = [wi_ref[...].astype(F32), wf_ref[...].astype(F32)]
    weights.append(jnp.zeros((16 - 2 * heads, weights[0].shape[1]), F32))
    weights = jnp.concatenate(weights, axis=0).astype(BF16)
    k = k_ref[...]
    turned = k.T
    gates = dot(x_ref[...], weights, 1, 1)
    gates = jnp.concatenate([gates, jnp.zeros((n, 112), F32)], axis=1).T[: 2 * heads]
    row8 = iota(gates.shape, 0)
    for h in range(heads):
        gates = gates + jnp.where(row8 == h, bi_ref[h], 0.0)
        gates = gates + jnp.where(row8 == h + heads, bf_ref[h], 0.0)
    in_gate, forget_pre = gates[:heads], gates[heads:]
    log_forget = jnp.minimum(forget_pre, 0.0) - jnp.log1p(jnp.exp(-jnp.abs(forget_pre)))
    start = (pos_ref[...] == 0).astype(F32)
    stacked = jnp.concatenate([log_forget, start, jnp.zeros((7 - heads, n), F32)], axis=0)
    cum = times_ones(stacked, iota((n, n), 0) <= iota((n, n), 1))
    lc, dc = cum[:heads], cum[heads : heads + 1]
    total, last = lc[:, n - 1 :], dc[:, n - 1 :]
    key_log = jnp.where(dc == last, total - lc + in_gate, NEG)
    rows_ref[...] = jnp.concatenate(
        [in_gate, forget_pre, lc, key_log, dc, jnp.zeros((7, n), F32)], axis=0
    )
    rows_ref.send()
    own_max = jnp.max(key_log, axis=1, keepdims=True)
    weight = jnp.exp(key_log - own_max)
    sums = rows_times(weight, k)
    column = column_of(weight)
    column_ref[...] = column
    turned_ref[...] = turned
    half = give_ref.shape[0] - 1
    outer_products(1 - core, heads, turned_ref, v_ref, column, give_ref)
    cut = jnp.where(last > 0.5, BIG, 0.0)
    tile = jnp.concatenate(
        [sums[h : h + 1, dk * h : dk * (h + 1)] for h in range(heads)]
        + [across(own_max), across(total - cut), across(in_gate[:, :1] - lc[:, :1])]
        + [jnp.broadcast_to(jnp.where(dc[:, :1] < 0.5, 1.0, 0.0), (1, 128))],
        axis=0,
    )
    tile_ref[...] = tile
    give_ref[half] = jnp.concatenate([tile, jnp.zeros((8, dv - 128), F32)], axis=1)


def first_kernel(heads, me_ref, mem_ref, tile_ref, got_ref, out_ref):
    core = me_ref[0] % 2
    half, dv = out_ref.shape[0], mem_ref.shape[2]
    mine, other = tile_ref[...], got_ref[half, :, :128]
    even = jnp.where(core == 0, mine, other)
    odd = jnp.where(core == 0, other, mine)
    chip_max = jnp.maximum(even[4:5] + odd[5:6], odd[4:5])
    keep = jnp.exp(even[4:5] + odd[5:6] - chip_max)
    add = jnp.exp(odd[4:5] - chip_max)
    vectors = [
        keep[:, h : h + 1] * even[h : h + 1] + add[:, h : h + 1] * odd[h : h + 1]
        for h in range(heads)
    ]
    both = jnp.where(iota(even.shape, 1) < heads, even, pltpu.roll(odd, heads, 1))
    tile = jnp.concatenate(vectors + [both[heads:]], axis=0)
    out_ref[:, :, dv:] = jnp.broadcast_to(tile[None], (half, 8, 128))
    weight_mine = jnp.where(core == 0, keep, add)
    weight_other = jnp.where(core == 0, add, keep)
    per_head = half // (heads // 2)
    for i in range(heads // 2):
        at = core * (heads // 2) + i
        slab = slice(i * per_head, (i + 1) * per_head)
        own = mem_ref[slab]
        out_ref[slab, :, :dv] = pick(weight_mine, at) * own + pick(weight_other, at) * got_ref[slab]


def pairs_kernel(
    heads, me_ref, mem_ref, tile_ref, got_ref, rows_ref, q_ref, k_ref, v_ref, g_ref,
    even_ref, even_tile_ref, turned_ref, wl_ref, pc_ref, gv_ref, sums_ref,
):
    core = me_ref[0] % 2
    half = even_ref.shape[0]
    even_ref[...] = jnp.where(core == 0, mem_ref[...], got_ref[:half])
    even_ref.send()
    even_tile_ref[...] = jnp.where(core == 0, tile_ref[...], got_ref[half, :, :128])
    n = q_ref.shape[0]
    dk = k_ref.shape[1] // heads
    dv = v_ref.shape[1] // heads
    rows = rows_ref[...]
    lc = column_of(rows)
    place = 4 * heads
    mask = (iota((n, n), 0) >= iota((n, n), 1)) & (lc[:, place : place + 1] == rows[place : place + 1])
    turned_ref[...] = q_ref[...].T
    sums = jnp.zeros((n, 128), F32)
    for h in range(heads):
        offset = rows[h : h + 1] - rows[2 * heads + h : 2 * heads + h + 1]
        pair_log = jnp.where(mask, lc[:, 2 * heads + h : 2 * heads + h + 1] + offset, NEG)
        row_max = jnp.max(pair_log, axis=1, keepdims=True)
        weight = jnp.exp(pair_log - row_max)
        ks, vs = slice(dk * h, dk * (h + 1)), slice(dv * h, dv * (h + 1))
        coupled = dot(q_ref[:, ks], k_ref[:, ks], 1, 1) * weight
        grad_pair = dot(g_ref[:, vs], v_ref[:, vs], 1, 1)
        wl_ref[h] = weight
        pc_ref[h] = coupled
        gv_ref[h] = grad_pair
        sums = put(sums, row_max, h)
        sums = put(sums, jnp.sum(coupled, axis=1, keepdims=True), heads + h)
        sums = put(sums, jnp.sum(coupled * grad_pair, axis=1, keepdims=True), 2 * heads + h)
    sums_ref[...] = sums.T[: sums_ref.shape[0]]


def shift_down(x, d, fill):
    return jnp.where(iota(x.shape, 0) < d, fill, pltpu.roll(x, d, 0))


def shift_up(x, d, fill):
    size = x.shape[0]
    return jnp.where(iota(x.shape, 0) >= size - d, fill, pltpu.roll(x, size - d, 0))


def dual_kernel(
    heads, scale, me_ref, got_ref, tile_ref, rows_ref, sums_ref, turned_ref, g_ref,
    give_ref, column_ref, coef_ref, now_ref, coef_later_ref, later_ref, small_ref, tokens_ref,
):
    count = got_ref.shape[0]
    n = g_ref.shape[0]
    dk = turned_ref.shape[0] // heads
    dv = g_ref.shape[1] // heads
    me = me_ref[0]
    core, chip = me % 2, me // 2
    max_even, total_even = got_ref[:, heads, dv:], got_ref[:, heads + 1, dv:]
    first_even, valid_even = got_ref[:, heads + 2, dv:], got_ref[:, heads + 3, dv:]
    max_odd, total_odd, first_odd, valid_odd = (
        pltpu.roll(x, 128 - heads, 1) for x in (max_even, total_even, first_even, valid_even)
    )
    row = iota(max_even.shape, 0)
    lane = iota(max_even.shape, 1)
    steps = [1 << i for i in range((count - 1).bit_length())]
    chip_max = jnp.maximum(max_even + total_odd, max_odd)
    total = total_even + total_odd
    t, m = total, chip_max
    for d in steps:
        m = jnp.maximum(shift_down(m, d, NEG) + t, m)
        t = shift_down(t, d, 0.0) + t
    in_even = shift_down(m, 1, NEG)
    in_odd = jnp.maximum(in_even + total_even, max_even)
    dual_even = jnp.where(valid_even > 0.5, -jnp.maximum(in_even, first_even), NEG)
    dual_odd = jnp.where(valid_odd > 0.5, -jnp.maximum(in_odd, first_odd), NEG)
    chip_dual = jnp.maximum(dual_even, total_even + dual_odd)
    t, r = total, chip_dual
    for d in steps:
        r = jnp.maximum(r, t + shift_up(r, d, NEG))
        t = t + shift_up(t, d, 0.0)
    later_odd = shift_up(r, 1, NEG)
    later_even = jnp.maximum(dual_odd, total_odd + later_odd)
    my_head = (heads // 2) * core + chip // (2 * count // heads)
    coefs = (
        jnp.exp(in_even + total - m),
        jnp.exp(chip_max - m),
        jnp.exp(total + later_odd - r),
        jnp.exp(chip_dual - r),
    )
    for i, c in enumerate(coefs):
        mine = jnp.sum(jnp.where(lane == my_head, c, 0.0), axis=1, keepdims=True)
        (coef_ref if i < 2 else coef_later_ref)[i % 2] = jnp.broadcast_to(mine, c.shape)

    def here(x):
        return jnp.sum(jnp.where(row == chip, x, 0.0), axis=0, keepdims=True)

    def mine_of(even, odd):
        return here(jnp.where(core == 0, even, odd))

    in_me, later_me = mine_of(in_even, in_odd), mine_of(later_even, later_odd)
    dual_me, total_me = mine_of(dual_even, dual_odd), mine_of(total_even, total_odd)
    keep = here(jnp.exp(in_even + total_even - in_odd))
    add = here(jnp.exp(max_even - in_odd))
    later_row = iota((count, count), 0) < iota((count, count), 1)
    between = ones_times(later_row, jnp.where(row < chip, total, 0.0))
    weight = jnp.where(
        row < chip, jnp.exp(jnp.minimum(chip_max + between - here(in_even), 0.0)), 0.0
    )
    earlier_row = iota((count, count), 0) > iota((count, count), 1)
    between = ones_times(earlier_row, jnp.where(row > chip, total, 0.0))
    source = jnp.where(core == 0, dual_even, total_even + dual_odd)
    later_ref[...] = jnp.where(
        row > chip, jnp.exp(jnp.minimum(source + between - here(later_odd), 0.0)), 0.0
    )
    even_tile = tile_ref[...]
    vectors = []
    for h in range(heads):
        one = slice(h, h + 1)
        vector = jnp.sum(weight[:, one] * got_ref[:, h, dv:], axis=0, keepdims=True)
        second = keep[:, one] * vector + add[:, one] * even_tile[one]
        vectors.append(jnp.where(core == 0, vector, second))
    small = jnp.concatenate(
        vectors
        + [
            later_me,
            jnp.exp(in_me + total_me + later_me),
            keep,
            add,
            here(jnp.exp(total_odd + later_odd - later_even)),
            here(jnp.exp(dual_odd - later_even)),
            here(jnp.exp(dual_even - chip_dual)),
            here(jnp.exp(total_even + dual_odd - chip_dual)),
            jnp.zeros((8 - heads, 128), F32),
        ],
        axis=0,
    )

    small_ref[...] = small
    small_ref.send()
    now_ref[...] = small
    lc = rows_ref[2 * heads : 3 * heads]
    open_query = rows_ref[4 * heads : 4 * heads + 1] < 0.5
    inner_max = sums_ref[:heads]
    cross_log = jnp.where(open_query, lc + down(in_me, heads), NEG)
    row_max = jnp.maximum(inner_max, cross_log)
    inside = jnp.exp(inner_max - row_max)
    cross = jnp.exp(cross_log - row_max)
    qn = [
        rows_times(small[:heads], turned_ref[dk * h : dk * (h + 1)])[h : h + 1] for h in range(heads)
    ]
    qn = jnp.concatenate(qn, axis=0)
    sums = scale * (sums_ref[heads : 2 * heads] * inside + cross * qn)
    floor = jnp.exp(-row_max)
    size = jnp.abs(sums)
    inverse = 1.0 / jnp.maximum(size, floor)
    active = jnp.where(size > floor, jnp.where(sums > 0.0, 1.0, -1.0), 0.0)
    query_weight = jnp.exp(jnp.minimum(lc - row_max - down(dual_me, heads), 0.0))
    query_weight = jnp.where(open_query, query_weight, 0.0)
    tokens_ref[...] = jnp.concatenate([inside, cross, inverse, active, query_weight, qn], axis=0)
    tokens_ref.send()
    grad_weight = column_of(query_weight * inverse * scale)
    column_ref[...] = grad_weight
    outer_products(1 - core, heads, turned_ref, g_ref, grad_weight, give_ref)


def wide(coef_ref, i, j, reps):
    return jnp.concatenate([coef_ref[i, pl.ds(j, 1), :]] * reps, axis=1)


def before_kernel(got_ref, coef_ref, out_ref):
    count, _, dv = out_ref.shape
    reps = dv // 128

    def forward(j, state):
        out_ref[j] = state
        step = wide(coef_ref, 1, j, reps) * got_ref[j, :, :dv]
        return wide(coef_ref, 0, j, reps) * state + step

    lax.fori_loop(0, count, forward, jnp.zeros((8, dv), F32), unroll=8)


def second_kernel(heads, me_ref, before_ref, small_ref, dual_ref, pair_ref, out_ref, odd_ref):
    core = me_ref[0] % 2
    count, _, dv = dual_ref.shape
    odd_ref[...] = jnp.where(core == 0, pair_ref[...], dual_ref[...])
    odd_ref.send()
    out_ref[:, :, :dv] = before_ref[...]
    even, odd = small_ref[10:11], small_ref[11:12]
    weight_mine = jnp.where(core == 0, even, odd)
    weight_other = jnp.where(core == 0, odd, even)
    per_head = count // (heads // 2)
    for i in range(heads // 2):
        at = core * (heads // 2) + i
        slab = slice(i * per_head, (i + 1) * per_head)
        step = pick(weight_other, at) * pair_ref[slab]
        out_ref[slab, :, dv:] = pick(weight_mine, at) * dual_ref[slab] + step


def halves_kernel(heads, me_ref, got_ref, even_ref, small_ref, give_ref, mine_ref):
    core = me_ref[0] % 2
    count, dv = give_ref.shape[0], give_ref.shape[2]
    per_head = count // (heads // 2)
    even, small = even_ref, small_ref[...]

    def fill(to_even_ref, to_odd_ref):
        for i in range(heads // 2):
            at = core * (heads // 2) + i
            slab = slice(i * per_head, (i + 1) * per_head)
            before = got_ref[slab, :, :dv]
            to_even_ref[slab] = before
            to_odd_ref[slab] = pick(small[6:7], at) * before + pick(small[7:8], at) * even[slab]

    @pl.when(core == 0)
    def _():
        fill(mine_ref, give_ref)

    @pl.when(core == 1)
    def _():
        fill(give_ref, mine_ref)


def crossings(side, heads, memory_ref, q_ref, g_ref):
    half = heads // 2
    n, dk, dv = q_ref.shape[0], q_ref.shape[1] // heads, g_ref.shape[1] // heads
    result = jnp.zeros((n, 128), F32)
    for i in range(half):
        memory = memory_ref[dk // 8 * i : dk // 8 * (i + 1)].reshape(dk, dv)
        at = pl.multiple_of((side * half + i) * dk, dk)
        crossing = dot_right(q_ref[:, pl.ds(at, dk)], memory, 1, 0)
        at = pl.multiple_of((side * half + i) * dv, dv)
        along = g_ref[:, pl.ds(at, dv)].astype(F32) * crossing
        result = put(result, jnp.sum(along, axis=1, keepdims=True), i)
    return result


def merged(core, heads, mine, other):
    half = heads // 2
    first = jnp.where(core == 0, mine, other)
    return first + pltpu.roll(jnp.where(core == 0, other, mine), half, 1)


def mine_kernel(heads, me_ref, mine_ref, got_ref, coef_ref, q_ref, g_ref, out_ref, gc_ref):
    count, dv = mine_ref.shape[0], mine_ref.shape[2]
    reps = dv // 128

    def backward(i, state):
        j = count - 1 - i
        for i in range(2):
            for c in range(reps):
                out_ref[j, i * reps + c] = state[4 * i : 4 * (i + 1), 128 * c : 128 * (c + 1)]
        step = wide(coef_ref, 1, j, reps) * got_ref[j, :, dv:]
        return wide(coef_ref, 0, j, reps) * state + step

    lax.fori_loop(0, count, backward, jnp.zeros((8, dv), F32), unroll=8)
    gc_ref[...] = crossings(me_ref[0] % 2, heads, mine_ref, q_ref, g_ref)


def vector_kernel(
    heads, scale, me_ref, mine_ref, pair_ref, after_ref, crossing_ref, tokens_ref, sums_ref, q_ref, g_ref,
    out_ref, tile_ref, gt_ref,
):
    core = me_ref[0] % 2
    dk = q_ref.shape[1] // heads
    count, pieces = mine_ref.shape[0], after_ref.shape[1]
    out_ref[:, :pieces] = after_ref[...]
    gc = merged(core, heads, crossing_ref[...], crossings(1 - core, heads, pair_ref, q_ref, g_ref))
    inside, cross, inverse, active, query_weight = (
        tokens_ref[heads * i : heads * (i + 1)] for i in range(5)
    )
    gc = gc.T[:heads]
    gt = sums_ref[2 * heads : 3 * heads] * inside + cross * gc
    gt = -scale * gt * inverse * inverse * active
    gt_ref[...] = jnp.concatenate([gt, gc], axis=0)
    vectors = rows_times(query_weight * gt * scale, q_ref[...])
    vectors = [vectors[h : h + 1, dk * h : dk * (h + 1)] for h in range(heads)]
    tile = jnp.concatenate(vectors + [jnp.zeros((8 - heads, 128), F32)], axis=0)
    tile_ref[...] = tile
    out_ref[:, pieces] = jnp.broadcast_to(tile[None, :4], (count, 4, 128))


def inner_kernel(
    heads, scale, me_ref, mine_ref, pair_ref, gt_ref, tokens_ref, small_ref, wl_ref, pc_ref, gv_ref,
    q_ref, k_ref, g_ref,
    mem_ref, gq_ref, gvalue_ref, gk_ref, row_ref, cold_ref,
):
    core, count = me_ref[0] % 2, mine_ref.shape[0]
    mem_ref[pl.ds(core * count, count)] = mine_ref[...]
    mem_ref[pl.ds((1 - core) * count, count)] = pair_ref[...]
    mem_ref.send()
    n = q_ref.shape[0]
    dk = q_ref.shape[1] // heads
    dv = g_ref.shape[1] // heads
    tokens = column_of(jnp.concatenate([tokens_ref[...], gt_ref[...]], axis=0))
    inside, cross, inverse, qn, gt, gc = (unpack(tokens, i, heads) for i in (0, 1, 2, 5, 6, 7))
    row_part = scale * cross * (inverse * gc + gt * qn)
    for h in range(heads):
        ks, vs = slice(dk * h, dk * (h + 1)), slice(dv * h, dv * (h + 1))
        one = slice(h, h + 1)
        q, k, g = q_ref[:, ks], k_ref[:, ks], g_ref[:, vs]
        memory = mem_ref[dk // 8 * h : dk // 8 * (h + 1)].reshape(dk, dv)
        factor = inside[:, one] * (inverse[:, one] * gv_ref[h] + gt[:, one])
        pair_grad = factor * pc_ref[h]
        cold_ref[one, :] = scale * jnp.sum(pair_grad, axis=0, keepdims=True)
        row_part = row_part + put(
            jnp.zeros((n, 128), F32), scale * jnp.sum(pair_grad, axis=1, keepdims=True), h
        )
        score_high, score_low = split(factor * wl_ref[h])
        grad_query = dot(score_high, k, 1, 0) + dot(score_low, k, 1, 0)
        grad_query = grad_query + cross[:, one] * (
            inverse[:, one] * dot_right(g, memory, 1, 1) + gt[:, one] * small_ref[one]
        )
        gq_ref[:, ks] = (scale * grad_query).astype(BF16)
        gk_ref[:, ks] = scale * (dot(score_high, q, 0, 0) + dot(score_low, q, 0, 0))
        coupled = pc_ref[h] * (scale * inside[:, one] * inverse[:, one])
        gvalue_ref[:, vs] = dot_left(coupled, g, 0, 0)
    row_ref[...] = row_part.T[:8]
    cold_ref[heads:, :] = jnp.zeros((8 - heads, n), F32)


def after_kernel(
    heads, me_ref, got_ref, later_ref, small_ref, odd_ref, tile_ref, unused_ref,
    give_ref, mine_ref, sum_ref,
):
    core = me_ref[0] % 2
    count, dv = mine_ref.shape[0], mine_ref.shape[2]
    reps = dv // 128
    per_head = count // (heads // 2)
    vectors = [
        jnp.sum(later_ref[:, h : h + 1] * got_ref[:, 2 * reps, h, :], axis=0, keepdims=True)
        for h in range(heads)
    ]
    tile = jnp.concatenate(vectors + [tile_ref[:heads]], axis=0)
    sum_ref[...] = tile
    give_ref[count] = jnp.concatenate([tile, jnp.zeros((8, dv - 128), F32)], axis=1)
    odd, small = odd_ref.ready(), small_ref[...]

    def fill(to_even_ref, to_odd_ref):
        for i in range(heads // 2):
            at = core * (heads // 2) + i
            slab = slice(i * per_head, (i + 1) * per_head)
            after = [
                jnp.concatenate([got_ref[slab, i * reps + c] for c in range(reps)], axis=2)
                for i in range(2)
            ]
            after = jnp.concatenate(after, axis=1)
            to_odd_ref[slab] = after
            to_even_ref[slab] = pick(small[8:9], at) * after + pick(small[9:10], at) * odd[slab]

    @pl.when(core == 0)
    def _():
        fill(mine_ref, give_ref)

    @pl.when(core == 1)
    def _():
        fill(give_ref, mine_ref)


def alongs(side, heads, after_ref, k_ref, v_ref):
    half = heads // 2
    n, dk, dv = k_ref.shape[0], k_ref.shape[1] // heads, v_ref.shape[1] // heads
    result = jnp.zeros((n, 128), F32)
    for i in range(half):
        following = after_ref[dk // 8 * i : dk // 8 * (i + 1)].reshape(dk, dv)
        at = pl.multiple_of((side * half + i) * dk, dk)
        carried = dot_right(k_ref[:, pl.ds(at, dk)], following, 1, 0)
        at = pl.multiple_of((side * half + i) * dv, dv)
        along = v_ref[:, pl.ds(at, dv)].astype(F32) * carried
        result = put(result, jnp.sum(along, axis=1, keepdims=True), i)
    return result


def along_kernel(heads, me_ref, mine_ref, k_ref, v_ref, out_ref):
    out_ref[...] = alongs(me_ref[0] % 2, heads, mine_ref, k_ref, v_ref)


def weights_kernel(
    heads, me_ref, mine_ref, pair_ref, sum_ref, along_ref, small_ref, k_ref, v_ref, mem_ref, rows_ref,
    row_ref, cold_ref, x_ref,
    after_ref, vector_ref, pay_ref,
):
    core = me_ref[0] % 2
    n = k_ref.shape[0]
    dk = k_ref.shape[1] // heads
    dv = v_ref.shape[1] // heads
    count = mine_ref.shape[0]
    after_ref[pl.ds(core * count, count)] = mine_ref[...]
    after_ref[pl.ds((1 - core) * count, count)] = pair_ref[:count]
    after_ref.send()
    mine, other = sum_ref[...], pair_ref[count, :, :128]
    column_cross = merged(
        core, heads, along_ref[...], alongs(1 - core, heads, pair_ref, k_ref, v_ref)
    )
    through = []
    vectors = []
    for h in range(heads):
        ks, one = slice(dk * h, dk * (h + 1)), slice(h, h + 1)
        slab = slice(dk // 8 * h, dk // 8 * (h + 1))
        odd = mine[one] + other[one]
        even = small_ref[8:9, one] * odd + small_ref[9:10, one] * other[heads + h : heads + h + 1]
        vector = jnp.where(core == 0, even, odd)
        vectors.append(vector)
        along = jnp.sum(k_ref[:, ks].astype(F32) * vector, axis=1, keepdims=True)
        column_cross = column_cross + put(jnp.zeros((n, 128), F32), along, h)
        following = after_ref[slab].reshape(dk, dv)
        product = jnp.sum(mem_ref[slab].reshape(dk, dv) * following, axis=0, keepdims=True)
        product = jnp.sum(product, axis=1, keepdims=True)
        product = product + jnp.sum(small_ref[one] * vector, axis=1, keepdims=True)
        through.append(product)
    vector_ref[...] = jnp.concatenate(vectors + [jnp.zeros((8 - heads, 128), F32)], axis=0)
    vector_ref.send()
    passing = padded(jnp.concatenate(through, axis=0) * down(small_ref[heads + 1 : heads + 2], heads))
    key_scale = jnp.exp(rows_ref[3 * heads : 4 * heads] + down(small_ref[heads : heads + 1], heads))
    crossing = padded(column_cross.T[:heads] * key_scale)
    row, inner = row_ref[...], cold_ref[...]
    after = iota((n, n), 0) >= iota((n, n), 1)
    suffix = times_ones(row - inner, after)
    prefix = times_ones(crossing, jnp.logical_not(after))
    grad_log = suffix + prefix + passing
    grad_forget = grad_log[:heads] / (1.0 + jnp.exp(rows_ref[heads : 2 * heads, :]))
    coefs = jnp.concatenate([(inner + crossing)[:heads], grad_forget], axis=0)
    high = coefs.astype(BF16).astype(F32)
    both = jnp.concatenate([high, coefs - high], axis=0).astype(BF16)
    product = dot(both, x_ref[...], 1, 0)
    result = product[: 2 * heads] + product[2 * heads :]
    tiles, _, width = pay_ref.shape
    for c in range(tiles):
        pay_ref[c] = result[:, width * c : width * (c + 1)]


def finish_kernel(
    heads, after_ref, vector_ref, small_ref, rows_ref, gk_ref, gvalue_ref, k_ref, v_ref,
    gkey_ref, out_ref,
):
    dk = gk_ref.shape[1] // heads
    dv = v_ref.shape[1] // heads
    key_scale = jnp.exp(unpack(column_of(rows_ref[...]), 3, heads) + small_ref[heads : heads + 1])
    for h in range(heads):
        ks, vs, one = slice(dk * h, dk * (h + 1)), slice(dv * h, dv * (h + 1)), slice(h, h + 1)
        following = after_ref[dk // 8 * h : dk // 8 * (h + 1)].reshape(dk, dv)
        high, low = split(following)
        carried = dot(v_ref[:, vs], high, 1, 1) + dot(v_ref[:, vs], low, 1, 1) + vector_ref[one]
        gkey_ref[:, ks] = (gk_ref[:, ks] + key_scale[:, one] * carried).astype(BF16)
        carried = dot(k_ref[:, ks], high, 1, 0) + dot(k_ref[:, ks], low, 1, 0)
        out_ref[:, vs] = (gvalue_ref[:, vs] + key_scale[:, one] * carried).astype(BF16)


def sum_kernel(got_ref, *refs):
    out_ref = refs[-1]
    total = jnp.sum(got_ref[...], axis=0, keepdims=True)
    out_ref[...] = jnp.broadcast_to(total, out_ref.shape)


def place_kernel(got_ref, first_ref, second_ref):
    heads = first_ref.shape[0]
    tiles, _, width = got_ref.shape
    for c in range(tiles):
        first_ref[:, width * c : width * (c + 1)] = got_ref[c, :heads]
        second_ref[:, width * c : width * (c + 1)] = got_ref[c, heads:]


class Fetched:
    def __init__(self, copy, ref):
        self.copy, self.ref, self.waited = copy, ref, False

    def ready(self):
        if not self.waited:
            self.copy.wait()
            self.waited = True
        return self.ref

    @property
    def shape(self):
        return self.ref.shape

    def __getitem__(self, at):
        return self.ready()[at]


class Stored:
    def __init__(self, copy, ref):
        self.copy, self.ref, self.sent = copy, ref, False

    @property
    def shape(self):
        return self.ref.shape

    def send(self):
        if not self.sent:
            self.copy.start()
            self.sent = True

    def __getitem__(self, at):
        return self.ref[at]

    def __setitem__(self, at, value):
        self.ref[at] = value


def call(body, outs, ins, limit=24):
    outs = [(k, o if isinstance(o, jax.ShapeDtypeStruct) else jax.ShapeDtypeStruct(o, F32)) for k, o in outs]
    spaces = {"s": pltpu.SMEM, "v": pltpu.VMEM, "h": pltpu.HBM, "m": pltpu.HBM, "a": pltpu.HBM}
    scratch = [
        (pltpu.SMEM if k == "m" else pltpu.VMEM)(a.shape, a.dtype) for k, a in ins + outs if k in "hm"
    ]
    scratch.append(pltpu.SemaphoreType.DMA((max(len(scratch), 1),)))

    def kernel(*refs):
        given, rest = refs[: len(ins)], refs[len(ins) :]
        results, buffers, sems = rest[: len(outs)], rest[len(outs) : -1], rest[-1]
        taken, made, used = [], [], 0
        for (kind, _), ref in zip(ins, given):
            if kind in "hm":
                copy = pltpu.make_async_copy(ref, buffers[used], sems.at[used])
                copy.start()
                ref = Fetched(copy, buffers[used])
                used += 1
            taken.append(ref)
        for (kind, _), ref in zip(outs, results):
            if kind == "h":
                copy = pltpu.make_async_copy(buffers[used], ref, sems.at[used])
                ref = Stored(copy, buffers[used])
                used += 1
            made.append(ref)
        body(*taken, *made)
        for ref in taken:
            if isinstance(ref, Fetched):
                ref.ready()
        for ref in made:
            if isinstance(ref, Stored):
                ref.send()
        for ref in made:
            if isinstance(ref, Stored):
                ref.copy.wait()

    return pl.pallas_call(
        kernel,
        out_shape=[pltpu.HBM(o.shape, o.dtype) if k == "h" else o for k, o in outs],
        in_specs=[pl.BlockSpec(memory_space=spaces[k]) for k, _ in ins],
        out_specs=[pl.BlockSpec(memory_space=spaces[k]) for k, _ in outs],
        scratch_shapes=scratch,
        compiler_params=pltpu.CompilerParams(vmem_limit_bytes=limit * 1024 * 1024),
    )(*[pltpu.with_memory_space_constraint(a, pltpu.HBM) if k in "hma" else a for k, a in ins])


def unpack(x, i, heads):
    return pltpu.roll(x, 128 - heads * i, 1) if i else x


def exchange(x, axis, groups=None):
    return lax.all_to_all(x, axis, 0, 0, axis_index_groups=groups)


def local(
    layer_input, queries, keys, values, grad_out, doc_pos, w_input, b_input, w_forget, b_forget
):
    x, q, k, v, g = layer_input[0], queries[0], keys[0], values[0], grad_out[0]
    heads = w_input.shape[1]
    n = q.shape[0]
    dk, dv = q.shape[1] // heads, v.shape[1] // heads
    scale = dk ** (-0.5)
    devices = lax.axis_size("ctx")
    count = devices // 2
    me = lax.axis_index("ctx").astype(jnp.int32).reshape(1)
    part = functools.partial
    slabs = heads * dk // 8
    cores = [[2 * i + c for i in range(count)] for c in range(2)]

    def to_pair(a):
        return lax.ppermute(a, "ctx", [(i, i ^ 1) for i in range(devices)])

    low = jax.ShapeDtypeStruct

    def given(kinds, *arrays):
        return list(zip(kinds, arrays, strict=True))

    give, turned, column, tile, rows = call(
        part(gates_kernel, heads),
        given(
            "vvvvh", (slabs // 2 + 1, 8, dv), low((heads * dk, n), BF16), (n, 128), (8, 128), (24, n)
        ),
        given("shhmmhhhh", me, w_input.T, w_forget.T, b_input, b_forget, doc_pos, k, x, v),
    )
    pair = to_pair(give)
    (memory,) = call(
        part(products_kernel, heads), given("v", (count, 8, dv)), given("svhv", me, turned, v, column)
    )
    (pay,) = call(
        part(first_kernel, heads),
        given("v", (count, 8, dv + 128)),
        given("svvv", me, memory, tile, pair),
    )
    first = exchange(pay, "ctx", cores)
    even_memory, even_tile, turned, wl, pc, gv, sums = call(
        part(pairs_kernel, heads),
        given(
            "hvvhhhv", (count, 8, dv), (8, 128), low((heads * dk, n), BF16), *[(heads, n, n)] * 3, (16, n)
        ),
        given("svvvhhhhh", me, memory, tile, pair, rows, q, k, v, g),
    )
    give, column, coef, now, coef_later, later, small, tokens = call(
        part(dual_kernel, heads, scale),
        given(
            "vvvvvvhh", (count, 8, dv), (n, 128), (2, count, 128), (16, 128),
            (2, count, 128), (count, 128), (16, 128), (24, n),
        ),
        given("svvhvvh", me, first, even_tile, rows, sums, turned, g),
    )
    pair = to_pair(give)
    (dual,) = call(
        part(products_kernel, heads), given("v", (count, 8, dv)), given("svhv", me, turned, g, column)
    )
    (before,) = call(before_kernel, given("v", (count, 8, dv)), given("vv", first, coef))
    pay, odd_dual = call(
        part(second_kernel, heads),
        given("vh", (count, 8, 2 * dv), (count, 8, dv)),
        given("svvvv", me, before, now, dual, pair),
    )
    second = exchange(pay, "ctx", cores)
    give, mine = call(
        part(halves_kernel, heads),
        given("vv", (count, 8, dv), (count, 8, dv)),
        given("svvv", me, second, even_memory, now),
    )
    pair = to_pair(give)
    after, crossing = call(
        part(mine_kernel, heads),
        given("vv", (count, 2 * dv // 128, 4, 128), (n, 128)),
        given("svvvvv", me, mine, second, coef_later, q, g),
    )
    pay, tile, gt = call(
        part(vector_kernel, heads, scale),
        given("vvv", (count, 2 * dv // 128 + 1, 4, 128), (8, 128), (8, n)),
        given("svvvvvvvv", me, mine, pair, after, crossing, tokens, sums, q, g),
    )
    third = exchange(pay, "ctx", cores)
    states, grad_q, gvalue, gk, row, cold = call(
        part(inner_kernel, heads, scale),
        given("hhhhhh", (slabs, 8, dv), low(q.shape, BF16), v.shape, k.shape, (8, n), (8, n)),
        given("svvvhhhhhhhh", me, mine, pair, gt, tokens, small, wl, pc, gv, q, k, g),
    )
    give, mine, sums = call(
        part(after_kernel, heads),
        given("vvv", (count + 1, 8, dv), (count, 8, dv), (8, 128)),
        given("svvvhva", me, third, later, now, odd_dual, tile, gk),
    )
    pair = to_pair(give)
    (along,) = call(part(along_kernel, heads), given("v", (n, 128)), given("svvv", me, mine, k, v))
    batch, across_x = lax.axis_size("dp"), 4
    tiles = batch * across_x
    at = [[[(z * across_x + i) * 2 + c for i in range(across_x)] for c in range(2)] for z in range(count // across_x)]
    planes = [[i * batch + d for i in row for d in range(batch)] for z in at for row in z]
    lines = [[row[i] for z in at for row in z] for i in range(across_x)]
    chunk = (8, x.shape[1] // tiles)
    following, vector, pay = call(
        part(weights_kernel, heads),
        given("hhv", (slabs, 8, dv), (8, 128), (tiles, *chunk)),
        given(
            "svvvvvvvhhhhv", me, mine, pair, sums, along, now, k, v, states, rows, row, cold, x
        ),
    )
    got = exchange(pay, ("ctx", "dp"), planes)
    grad_k, grad_v = call(
        part(finish_kernel, heads),
        given("hh", low(k.shape, BF16), low(v.shape, BF16)),
        given("hhhhhhhh", following, vector, small, rows, gk, gvalue, k, v),
    )
    (pay,) = call(sum_kernel, given("v", (len(lines[0]), *chunk)), given("va", got, grad_k))
    got = exchange(pay, "ctx", lines)
    (pay,) = call(sum_kernel, given("v", (tiles, *chunk)), given("v", got))
    got = exchange(pay, ("ctx", "dp"), planes)
    first, second = call(
        place_kernel, given("vv", (heads, x.shape[1]), (heads, x.shape[1])), given("v", got)
    )
    return (grad_q[None], grad_k[None], grad_v[None], first.T, second.T)


def solution(mesh):
    split_rows = P("dp", "ctx", None)
    placed = (split_rows,) * 5 + (P("dp", "ctx"),) + (P(),) * 4
    return jax.shard_map(
        local,
        mesh=mesh,
        in_specs=placed,
        out_specs=(split_rows, split_rows, split_rows, P(), P()),
        check_vma=False,
    )
```

```python
import functools

import jax
import jax.numpy as jnp
from jax import lax
from jax.experimental import pallas as pl
from jax.experimental.pallas import tpu as pltpu
from jax.sharding import PartitionSpec as P

NEG = -1e30
BIG = 1e30
F32 = jnp.float32
BF16 = jnp.bfloat16


def dot(a, b, ca, cb):
    return lax.dot_general(a, b, (((ca,), (cb,)), ((), ())), preferred_element_type=F32)


def split(x):
    high = x.astype(BF16)
    return high, (x - high.astype(F32)).astype(BF16)


def dot_left(x, b, ca, cb):
    high, low = split(x)
    return dot(high, b, ca, cb) + dot(low, b, ca, cb)


def dot_right(a, x, ca, cb):
    high, low = split(x)
    return dot(a, high, ca, cb) + dot(a, low, ca, cb)


def thirds(x):
    high = x.astype(BF16).astype(F32)
    middle = (x - high).astype(BF16).astype(F32)
    return [high, middle, x - high - middle]


def times_ones(x, ones):
    parts = dot(jnp.concatenate(thirds(x), axis=0).astype(BF16), ones.astype(F32).astype(BF16), 1, 0)
    return parts[:8] + parts[8:16] + parts[16:24]


def ones_times(ones, x):
    parts = dot(ones.astype(F32).astype(BF16), jnp.concatenate(thirds(x), axis=1).astype(BF16), 1, 0)
    return parts[:, :128] + parts[:, 128:256] + parts[:, 256:]


def iota(shape, dim):
    return lax.broadcasted_iota(jnp.int32, shape, dim)


def column_of(rows):
    r, n = rows.shape
    padded = jnp.concatenate([rows, jnp.zeros((128 - r, n), F32)], axis=0)
    return padded.T


def put(acc, col, h):
    return jnp.where(iota(acc.shape, 1) == h, col, acc)


def down(row, heads):
    return jnp.concatenate([pick(row, h) for h in range(heads)], axis=0)


def across(column):
    row = jnp.zeros((1, 128), F32)
    for h in range(column.shape[0]):
        row = put(row, column[h : h + 1], h)
    return row


def padded(rows):
    return jnp.concatenate([rows, jnp.zeros((8 - rows.shape[0], rows.shape[1]), F32)], axis=0)


def rows_times(rows, b):
    parts = dot(jnp.concatenate(thirds(padded(rows)), axis=0).astype(BF16), b, 1, 0)
    return parts[:8] + parts[8:16] + parts[16:24]


def pick(row, lane):
    return jnp.sum(jnp.where(iota(row.shape, 1) == lane, row, 0.0), axis=1, keepdims=True)


def outer_products(side, heads, turned_ref, rows_ref, columns, out_ref):
    half = heads // 2
    dk, dv = turned_ref.shape[0] // heads, rows_ref.shape[1] // heads
    columns = jnp.where(side == 0, columns, pltpu.roll(columns, 128 - half, 1))
    for i in range(half):
        at = pl.multiple_of((side * half + i) * dv, dv)
        weighted = rows_ref[:, pl.ds(at, dv)].astype(F32) * columns[:, i : i + 1]
        at = pl.multiple_of((side * half + i) * dk, dk)
        product = dot_right(turned_ref[pl.ds(at, dk), :], weighted, 1, 0)
        out_ref[dk // 8 * i : dk // 8 * (i + 1)] = product.reshape(dk // 8, 8, dv)


def products_kernel(heads, me_ref, turned_ref, rows_ref, column_ref, out_ref):
    outer_products(me_ref[0] % 2, heads, turned_ref, rows_ref, column_ref[...], out_ref)


def gates_kernel(
    heads, me_ref, wi_ref, wf_ref, bi_ref, bf_ref, pos_ref, k_ref, x_ref, v_ref,
    give_ref, turned_ref, column_ref, tile_ref, rows_ref,
):
    core = me_ref[0] % 2
    n = x_ref.shape[0]
    dk = k_ref.shape[1] // heads
    dv = v_ref.shape[1] // heads
    weights = [wi_ref[...].astype(F32), wf_ref[...].astype(F32)]
    weights.append(jnp.zeros((16 - 2 * heads, weights[0].shape[1]), F32))
    weights = jnp.concatenate(weights, axis=0).astype(BF16)
    k = k_ref[...]
    turned = k.T
    gates = dot(x_ref[...], weights, 1, 1)
    gates = jnp.concatenate([gates, jnp.zeros((n, 112), F32)], axis=1).T[: 2 * heads]
    row8 = iota(gates.shape, 0)
    for h in range(heads):
        gates = gates + jnp.where(row8 == h, bi_ref[h], 0.0)
        gates = gates + jnp.where(row8 == h + heads, bf_ref[h], 0.0)
    in_gate, forget_pre = gates[:heads], gates[heads:]
    log_forget = jnp.minimum(forget_pre, 0.0) - jnp.log1p(jnp.exp(-jnp.abs(forget_pre)))
    start = (pos_ref[...] == 0).astype(F32)
    stacked = jnp.concatenate([log_forget, start, jnp.zeros((7 - heads, n), F32)], axis=0)
    cum = times_ones(stacked, iota((n, n), 0) <= iota((n, n), 1))
    lc, dc = cum[:heads], cum[heads : heads + 1]
    total, last = lc[:, n - 1 :], dc[:, n - 1 :]
    key_log = jnp.where(dc == last, total - lc + in_gate, NEG)
    rows_ref[...] = jnp.concatenate(
        [in_gate, forget_pre, lc, key_log, dc, jnp.zeros((7, n), F32)], axis=0
    )
    rows_ref.send()
    own_max = jnp.max(key_log, axis=1, keepdims=True)
    weight = jnp.exp(key_log - own_max)
    sums = rows_times(weight, k)
    column = column_of(weight)
    column_ref[...] = column
    turned_ref[...] = turned
    half = give_ref.shape[0] - 1
    outer_products(1 - core, heads, turned_ref, v_ref, column, give_ref)
    cut = jnp.where(last > 0.5, BIG, 0.0)
    tile = jnp.concatenate(
        [sums[h : h + 1, dk * h : dk * (h + 1)] for h in range(heads)]
        + [across(own_max), across(total - cut), across(in_gate[:, :1] - lc[:, :1])]
        + [jnp.broadcast_to(jnp.where(dc[:, :1] < 0.5, 1.0, 0.0), (1, 128))],
        axis=0,
    )
    tile_ref[...] = tile
    give_ref[half] = jnp.concatenate([tile, jnp.zeros((8, dv - 128), F32)], axis=1)


def first_kernel(heads, me_ref, mem_ref, tile_ref, got_ref, out_ref):
    core = me_ref[0] % 2
    half, dv = out_ref.shape[0], mem_ref.shape[2]
    mine, other = tile_ref[...], got_ref[half, :, :128]
    even = jnp.where(core == 0, mine, other)
    odd = jnp.where(core == 0, other, mine)
    chip_max = jnp.maximum(even[4:5] + odd[5:6], odd[4:5])
    keep = jnp.exp(even[4:5] + odd[5:6] - chip_max)
    add = jnp.exp(odd[4:5] - chip_max)
    vectors = [
        keep[:, h : h + 1] * even[h : h + 1] + add[:, h : h + 1] * odd[h : h + 1]
        for h in range(heads)
    ]
    both = jnp.where(iota(even.shape, 1) < heads, even, pltpu.roll(odd, heads, 1))
    tile = jnp.concatenate(vectors + [both[heads:]], axis=0)
    out_ref[:, :, dv:] = jnp.broadcast_to(tile[None], (half, 8, 128))
    weight_mine = jnp.where(core == 0, keep, add)
    weight_other = jnp.where(core == 0, add, keep)
    per_head = half // (heads // 2)
    for i in range(heads // 2):
        at = core * (heads // 2) + i
        slab = slice(i * per_head, (i + 1) * per_head)
        own = mem_ref[slab]
        out_ref[slab, :, :dv] = pick(weight_mine, at) * own + pick(weight_other, at) * got_ref[slab]


def pairs_kernel(
    heads, me_ref, mem_ref, tile_ref, got_ref, rows_ref, q_ref, k_ref, v_ref, g_ref,
    even_ref, even_tile_ref, turned_ref, wl_ref, pc_ref, gv_ref, sums_ref,
):
    core = me_ref[0] % 2
    half = even_ref.shape[0]
    even_ref[...] = jnp.where(core == 0, mem_ref[...], got_ref[:half])
    even_ref.send()
    even_tile_ref[...] = jnp.where(core == 0, tile_ref[...], got_ref[half, :, :128])
    n = q_ref.shape[0]
    dk = k_ref.shape[1] // heads
    dv = v_ref.shape[1] // heads
    rows = rows_ref[...]
    lc = column_of(rows)
    place = 4 * heads
    mask = (iota((n, n), 0) >= iota((n, n), 1)) & (lc[:, place : place + 1] == rows[place : place + 1])
    turned_ref[...] = q_ref[...].T
    sums = jnp.zeros((n, 128), F32)
    for h in range(heads):
        offset = rows[h : h + 1] - rows[2 * heads + h : 2 * heads + h + 1]
        pair_log = jnp.where(mask, lc[:, 2 * heads + h : 2 * heads + h + 1] + offset, NEG)
        row_max = jnp.max(pair_log, axis=1, keepdims=True)
        weight = jnp.exp(pair_log - row_max)
        ks, vs = slice(dk * h, dk * (h + 1)), slice(dv * h, dv * (h + 1))
        coupled = dot(q_ref[:, ks], k_ref[:, ks], 1, 1) * weight
        grad_pair = dot(g_ref[:, vs], v_ref[:, vs], 1, 1)
        wl_ref[h] = weight
        pc_ref[h] = coupled
        gv_ref[h] = grad_pair
        sums = put(sums, row_max, h)
        sums = put(sums, jnp.sum(coupled, axis=1, keepdims=True), heads + h)
        sums = put(sums, jnp.sum(coupled * grad_pair, axis=1, keepdims=True), 2 * heads + h)
    sums_ref[...] = sums.T[: sums_ref.shape[0]]


def shift_down(x, d, fill):
    return jnp.where(iota(x.shape, 0) < d, fill, pltpu.roll(x, d, 0))


def shift_up(x, d, fill):
    size = x.shape[0]
    return jnp.where(iota(x.shape, 0) >= size - d, fill, pltpu.roll(x, size - d, 0))


def dual_kernel(
    heads, scale, me_ref, got_ref, tile_ref, rows_ref, sums_ref, turned_ref, g_ref,
    give_ref, column_ref, coef_ref, now_ref, coef_later_ref, later_ref, small_ref, tokens_ref,
):
    count = got_ref.shape[0]
    n = g_ref.shape[0]
    dk = turned_ref.shape[0] // heads
    dv = g_ref.shape[1] // heads
    me = me_ref[0]
    core, chip = me % 2, me // 2
    max_even, total_even = got_ref[:, heads, dv:], got_ref[:, heads + 1, dv:]
    first_even, valid_even = got_ref[:, heads + 2, dv:], got_ref[:, heads + 3, dv:]
    max_odd, total_odd, first_odd, valid_odd = (
        pltpu.roll(x, 128 - heads, 1) for x in (max_even, total_even, first_even, valid_even)
    )
    row = iota(max_even.shape, 0)
    lane = iota(max_even.shape, 1)
    steps = [1 << i for i in range((count - 1).bit_length())]
    chip_max = jnp.maximum(max_even + total_odd, max_odd)
    total = total_even + total_odd
    t, m = total, chip_max
    for d in steps:
        m = jnp.maximum(shift_down(m, d, NEG) + t, m)
        t = shift_down(t, d, 0.0) + t
    in_even = shift_down(m, 1, NEG)
    in_odd = jnp.maximum(in_even + total_even, max_even)
    dual_even = jnp.where(valid_even > 0.5, -jnp.maximum(in_even, first_even), NEG)
    dual_odd = jnp.where(valid_odd > 0.5, -jnp.maximum(in_odd, first_odd), NEG)
    chip_dual = jnp.maximum(dual_even, total_even + dual_odd)
    t, r = total, chip_dual
    for d in steps:
        r = jnp.maximum(r, t + shift_up(r, d, NEG))
        t = t + shift_up(t, d, 0.0)
    later_odd = shift_up(r, 1, NEG)
    later_even = jnp.maximum(dual_odd, total_odd + later_odd)
    my_head = (heads // 2) * core + chip // (2 * count // heads)
    coefs = (
        jnp.exp(in_even + total - m),
        jnp.exp(chip_max - m),
        jnp.exp(total + later_odd - r),
        jnp.exp(chip_dual - r),
    )
    for i, c in enumerate(coefs):
        mine = jnp.sum(jnp.where(lane == my_head, c, 0.0), axis=1, keepdims=True)
        (coef_ref if i < 2 else coef_later_ref)[i % 2] = jnp.broadcast_to(mine, c.shape)

    def here(x):
        return jnp.sum(jnp.where(row == chip, x, 0.0), axis=0, keepdims=True)

    def mine_of(even, odd):
        return here(jnp.where(core == 0, even, odd))

    in_me, later_me = mine_of(in_even, in_odd), mine_of(later_even, later_odd)
    dual_me, total_me = mine_of(dual_even, dual_odd), mine_of(total_even, total_odd)
    keep = here(jnp.exp(in_even + total_even - in_odd))
    add = here(jnp.exp(max_even - in_odd))
    later_row = iota((count, count), 0) < iota((count, count), 1)
    between = ones_times(later_row, jnp.where(row < chip, total, 0.0))
    weight = jnp.where(
        row < chip, jnp.exp(jnp.minimum(chip_max + between - here(in_even), 0.0)), 0.0
    )
    earlier_row = iota((count, count), 0) > iota((count, count), 1)
    between = ones_times(earlier_row, jnp.where(row > chip, total, 0.0))
    source = jnp.where(core == 0, dual_even, total_even + dual_odd)
    later_ref[...] = jnp.where(
        row > chip, jnp.exp(jnp.minimum(source + between - here(later_odd), 0.0)), 0.0
    )
    even_tile = tile_ref[...]
    vectors = []
    for h in range(heads):
        one = slice(h, h + 1)
        vector = jnp.sum(weight[:, one] * got_ref[:, h, dv:], axis=0, keepdims=True)
        second = keep[:, one] * vector + add[:, one] * even_tile[one]
        vectors.append(jnp.where(core == 0, vector, second))
    small = jnp.concatenate(
        vectors
        + [
            later_me,
            jnp.exp(in_me + total_me + later_me),
            keep,
            add,
            here(jnp.exp(total_odd + later_odd - later_even)),
            here(jnp.exp(dual_odd - later_even)),
            here(jnp.exp(dual_even - chip_dual)),
            here(jnp.exp(total_even + dual_odd - chip_dual)),
            jnp.zeros((8 - heads, 128), F32),
        ],
        axis=0,
    )

    small_ref[...] = small
    small_ref.send()
    now_ref[...] = small
    lc = rows_ref[2 * heads : 3 * heads]
    open_query = rows_ref[4 * heads : 4 * heads + 1] < 0.5
    inner_max = sums_ref[:heads]
    cross_log = jnp.where(open_query, lc + down(in_me, heads), NEG)
    row_max = jnp.maximum(inner_max, cross_log)
    inside = jnp.exp(inner_max - row_max)
    cross = jnp.exp(cross_log - row_max)
    qn = [
        rows_times(small[:heads], turned_ref[dk * h : dk * (h + 1)])[h : h + 1] for h in range(heads)
    ]
    qn = jnp.concatenate(qn, axis=0)
    sums = scale * (sums_ref[heads : 2 * heads] * inside + cross * qn)
    floor = jnp.exp(-row_max)
    size = jnp.abs(sums)
    inverse = 1.0 / jnp.maximum(size, floor)
    active = jnp.where(size > floor, jnp.where(sums > 0.0, 1.0, -1.0), 0.0)
    query_weight = jnp.exp(jnp.minimum(lc - row_max - down(dual_me, heads), 0.0))
    query_weight = jnp.where(open_query, query_weight, 0.0)
    tokens_ref[...] = jnp.concatenate([inside, cross, inverse, active, query_weight, qn], axis=0)
    tokens_ref.send()
    grad_weight = column_of(query_weight * inverse * scale)
    column_ref[...] = grad_weight
    outer_products(1 - core, heads, turned_ref, g_ref, grad_weight, give_ref)


def wide(coef_ref, i, j, reps):
    return jnp.concatenate([coef_ref[i, pl.ds(j, 1), :]] * reps, axis=1)


def before_kernel(got_ref, coef_ref, out_ref):
    count, _, dv = out_ref.shape
    reps = dv // 128

    def forward(j, state):
        out_ref[j] = state
        step = wide(coef_ref, 1, j, reps) * got_ref[j, :, :dv]
        return wide(coef_ref, 0, j, reps) * state + step

    lax.fori_loop(0, count, forward, jnp.zeros((8, dv), F32), unroll=8)


def second_kernel(heads, me_ref, before_ref, small_ref, dual_ref, pair_ref, out_ref, odd_ref):
    core = me_ref[0] % 2
    count, _, dv = dual_ref.shape
    odd_ref[...] = jnp.where(core == 0, pair_ref[...], dual_ref[...])
    odd_ref.send()
    out_ref[:, :, :dv] = before_ref[...]
    even, odd = small_ref[10:11], small_ref[11:12]
    weight_mine = jnp.where(core == 0, even, odd)
    weight_other = jnp.where(core == 0, odd, even)
    per_head = count // (heads // 2)
    for i in range(heads // 2):
        at = core * (heads // 2) + i
        slab = slice(i * per_head, (i + 1) * per_head)
        step = pick(weight_other, at) * pair_ref[slab]
        out_ref[slab, :, dv:] = pick(weight_mine, at) * dual_ref[slab] + step


def halves_kernel(heads, me_ref, got_ref, even_ref, small_ref, give_ref, mine_ref):
    core = me_ref[0] % 2
    count, dv = give_ref.shape[0], give_ref.shape[2]
    per_head = count // (heads // 2)
    even, small = even_ref, small_ref[...]

    def fill(to_even_ref, to_odd_ref):
        for i in range(heads // 2):
            at = core * (heads // 2) + i
            slab = slice(i * per_head, (i + 1) * per_head)
            before = got_ref[slab, :, :dv]
            to_even_ref[slab] = before
            to_odd_ref[slab] = pick(small[6:7], at) * before + pick(small[7:8], at) * even[slab]

    @pl.when(core == 0)
    def _():
        fill(mine_ref, give_ref)

    @pl.when(core == 1)
    def _():
        fill(give_ref, mine_ref)


def crossings(side, heads, memory_ref, q_ref, g_ref):
    half = heads // 2
    n, dk, dv = q_ref.shape[0], q_ref.shape[1] // heads, g_ref.shape[1] // heads
    result = jnp.zeros((n, 128), F32)
    for i in range(half):
        memory = memory_ref[dk // 8 * i : dk // 8 * (i + 1)].reshape(dk, dv)
        at = pl.multiple_of((side * half + i) * dk, dk)
        crossing = dot_right(q_ref[:, pl.ds(at, dk)], memory, 1, 0)
        at = pl.multiple_of((side * half + i) * dv, dv)
        along = g_ref[:, pl.ds(at, dv)].astype(F32) * crossing
        result = put(result, jnp.sum(along, axis=1, keepdims=True), i)
    return result


def merged(core, heads, mine, other):
    half = heads // 2
    first = jnp.where(core == 0, mine, other)
    return first + pltpu.roll(jnp.where(core == 0, other, mine), half, 1)


def mine_kernel(heads, me_ref, mine_ref, got_ref, coef_ref, q_ref, g_ref, out_ref, gc_ref):
    count, dv = mine_ref.shape[0], mine_ref.shape[2]
    reps = dv // 128

    def backward(i, state):
        j = count - 1 - i
        for i in range(2):
            for c in range(reps):
                out_ref[j, i * reps + c] = state[4 * i : 4 * (i + 1), 128 * c : 128 * (c + 1)]
        step = wide(coef_ref, 1, j, reps) * got_ref[j, :, dv:]
        return wide(coef_ref, 0, j, reps) * state + step

    lax.fori_loop(0, count, backward, jnp.zeros((8, dv), F32), unroll=8)
    gc_ref[...] = crossings(me_ref[0] % 2, heads, mine_ref, q_ref, g_ref)


def vector_kernel(
    heads, scale, me_ref, mine_ref, pair_ref, after_ref, crossing_ref, tokens_ref, sums_ref, q_ref, g_ref,
    out_ref, tile_ref, gt_ref,
):
    core = me_ref[0] % 2
    dk = q_ref.shape[1] // heads
    count, pieces = mine_ref.shape[0], after_ref.shape[1]
    out_ref[:, :pieces] = after_ref[...]
    gc = merged(core, heads, crossing_ref[...], crossings(1 - core, heads, pair_ref, q_ref, g_ref))
    inside, cross, inverse, active, query_weight = (
        tokens_ref[heads * i : heads * (i + 1)] for i in range(5)
    )
    gc = gc.T[:heads]
    gt = sums_ref[2 * heads : 3 * heads] * inside + cross * gc
    gt = -scale * gt * inverse * inverse * active
    gt_ref[...] = jnp.concatenate([gt, gc], axis=0)
    vectors = rows_times(query_weight * gt * scale, q_ref[...])
    vectors = [vectors[h : h + 1, dk * h : dk * (h + 1)] for h in range(heads)]
    tile = jnp.concatenate(vectors + [jnp.zeros((8 - heads, 128), F32)], axis=0)
    tile_ref[...] = tile
    out_ref[:, pieces] = jnp.broadcast_to(tile[None, :4], (count, 4, 128))


def inner_kernel(
    heads, scale, me_ref, mine_ref, pair_ref, gt_ref, tokens_ref, small_ref, wl_ref, pc_ref, gv_ref,
    q_ref, k_ref, g_ref,
    mem_ref, gq_ref, gvalue_ref, gk_ref, row_ref, cold_ref,
):
    core, count = me_ref[0] % 2, mine_ref.shape[0]
    mem_ref[pl.ds(core * count, count)] = mine_ref[...]
    mem_ref[pl.ds((1 - core) * count, count)] = pair_ref[...]
    mem_ref.send()
    n = q_ref.shape[0]
    dk = q_ref.shape[1] // heads
    dv = g_ref.shape[1] // heads
    tokens = column_of(jnp.concatenate([tokens_ref[...], gt_ref[...]], axis=0))
    inside, cross, inverse, qn, gt, gc = (unpack(tokens, i, heads) for i in (0, 1, 2, 5, 6, 7))
    row_part = scale * cross * (inverse * gc + gt * qn)
    for h in range(heads):
        ks, vs = slice(dk * h, dk * (h + 1)), slice(dv * h, dv * (h + 1))
        one = slice(h, h + 1)
        q, k, g = q_ref[:, ks], k_ref[:, ks], g_ref[:, vs]
        memory = mem_ref[dk // 8 * h : dk // 8 * (h + 1)].reshape(dk, dv)
        factor = inside[:, one] * (inverse[:, one] * gv_ref[h] + gt[:, one])
        pair_grad = factor * pc_ref[h]
        cold_ref[one, :] = scale * jnp.sum(pair_grad, axis=0, keepdims=True)
        row_part = row_part + put(
            jnp.zeros((n, 128), F32), scale * jnp.sum(pair_grad, axis=1, keepdims=True), h
        )
        score_high, score_low = split(factor * wl_ref[h])
        grad_query = dot(score_high, k, 1, 0) + dot(score_low, k, 1, 0)
        grad_query = grad_query + cross[:, one] * (
            inverse[:, one] * dot_right(g, memory, 1, 1) + gt[:, one] * small_ref[one]
        )
        gq_ref[:, ks] = (scale * grad_query).astype(BF16)
        gk_ref[:, ks] = scale * (dot(score_high, q, 0, 0) + dot(score_low, q, 0, 0))
        coupled = pc_ref[h] * (scale * inside[:, one] * inverse[:, one])
        gvalue_ref[:, vs] = dot_left(coupled, g, 0, 0)
    row_ref[...] = row_part.T[:8]
    cold_ref[heads:, :] = jnp.zeros((8 - heads, n), F32)


def after_kernel(
    heads, me_ref, got_ref, later_ref, small_ref, odd_ref, tile_ref, unused_ref,
    give_ref, mine_ref, sum_ref,
):
    core = me_ref[0] % 2
    count, dv = mine_ref.shape[0], mine_ref.shape[2]
    reps = dv // 128
    per_head = count // (heads // 2)
    vectors = [
        jnp.sum(later_ref[:, h : h + 1] * got_ref[:, 2 * reps, h, :], axis=0, keepdims=True)
        for h in range(heads)
    ]
    tile = jnp.concatenate(vectors + [tile_ref[:heads]], axis=0)
    sum_ref[...] = tile
    give_ref[count] = jnp.concatenate([tile, jnp.zeros((8, dv - 128), F32)], axis=1)
    odd, small = odd_ref.ready(), small_ref[...]

    def fill(to_even_ref, to_odd_ref):
        for i in range(heads // 2):
            at = core * (heads // 2) + i
            slab = slice(i * per_head, (i + 1) * per_head)
            after = [
                jnp.concatenate([got_ref[slab, i * reps + c] for c in range(reps)], axis=2)
                for i in range(2)
            ]
            after = jnp.concatenate(after, axis=1)
            to_odd_ref[slab] = after
            to_even_ref[slab] = pick(small[8:9], at) * after + pick(small[9:10], at) * odd[slab]

    @pl.when(core == 0)
    def _():
        fill(mine_ref, give_ref)

    @pl.when(core == 1)
    def _():
        fill(give_ref, mine_ref)


def alongs(side, heads, after_ref, k_ref, v_ref):
    half = heads // 2
    n, dk, dv = k_ref.shape[0], k_ref.shape[1] // heads, v_ref.shape[1] // heads
    result = jnp.zeros((n, 128), F32)
    for i in range(half):
        following = after_ref[dk // 8 * i : dk // 8 * (i + 1)].reshape(dk, dv)
        at = pl.multiple_of((side * half + i) * dk, dk)
        carried = dot_right(k_ref[:, pl.ds(at, dk)], following, 1, 0)
        at = pl.multiple_of((side * half + i) * dv, dv)
        along = v_ref[:, pl.ds(at, dv)].astype(F32) * carried
        result = put(result, jnp.sum(along, axis=1, keepdims=True), i)
    return result


def of_head(h, heads, core, mine_ref, pair_ref):
    half = heads // 2
    per_head = mine_ref.shape[0] // half
    slab = slice(per_head * (h % half), per_head * (h % half + 1))
    return jnp.where(core == h // half, mine_ref[slab], pair_ref[slab])


def along_kernel(heads, me_ref, mine_ref, k_ref, v_ref, out_ref):
    out_ref[...] = alongs(me_ref[0] % 2, heads, mine_ref, k_ref, v_ref)


def weights_kernel(
    heads, me_ref, mine_ref, pair_ref, sum_ref, along_ref, small_ref, k_ref, v_ref, mem_ref, rows_ref,
    row_ref, cold_ref, x_ref,
    vector_ref, pay_ref,
):
    core = me_ref[0] % 2
    n = k_ref.shape[0]
    dk = k_ref.shape[1] // heads
    dv = v_ref.shape[1] // heads
    count = mine_ref.shape[0]
    mine, other = sum_ref[...], pair_ref[count, :, :128]
    column_cross = merged(
        core, heads, along_ref[...], alongs(1 - core, heads, pair_ref, k_ref, v_ref)
    )
    through = []
    vectors = []
    for h in range(heads):
        ks, one = slice(dk * h, dk * (h + 1)), slice(h, h + 1)
        slab = slice(dk // 8 * h, dk // 8 * (h + 1))
        odd = mine[one] + other[one]
        even = small_ref[8:9, one] * odd + small_ref[9:10, one] * other[heads + h : heads + h + 1]
        vector = jnp.where(core == 0, even, odd)
        vectors.append(vector)
        along = jnp.sum(k_ref[:, ks].astype(F32) * vector, axis=1, keepdims=True)
        column_cross = column_cross + put(jnp.zeros((n, 128), F32), along, h)
        following = of_head(h, heads, core, mine_ref, pair_ref).reshape(dk, dv)
        product = jnp.sum(mem_ref[slab].reshape(dk, dv) * following, axis=0, keepdims=True)
        product = jnp.sum(product, axis=1, keepdims=True)
        product = product + jnp.sum(small_ref[one] * vector, axis=1, keepdims=True)
        through.append(product)
    vector_ref[...] = jnp.concatenate(vectors + [jnp.zeros((8 - heads, 128), F32)], axis=0)
    vector_ref.send()
    passing = padded(jnp.concatenate(through, axis=0) * down(small_ref[heads + 1 : heads + 2], heads))
    key_scale = jnp.exp(rows_ref[3 * heads : 4 * heads] + down(small_ref[heads : heads + 1], heads))
    crossing = padded(column_cross.T[:heads] * key_scale)
    row, inner = row_ref[...], cold_ref[...]
    after = iota((n, n), 0) >= iota((n, n), 1)
    suffix = times_ones(row - inner, after)
    prefix = times_ones(crossing, jnp.logical_not(after))
    grad_log = suffix + prefix + passing
    grad_forget = grad_log[:heads] / (1.0 + jnp.exp(rows_ref[heads : 2 * heads, :]))
    coefs = jnp.concatenate([(inner + crossing)[:heads], grad_forget], axis=0)
    high = coefs.astype(BF16).astype(F32)
    both = jnp.concatenate([high, coefs - high], axis=0).astype(BF16)
    product = dot(both, x_ref[...], 1, 0)
    result = product[: 2 * heads] + product[2 * heads :]
    tiles, _, width = pay_ref.shape
    for c in range(tiles):
        pay_ref[c] = result[:, width * c : width * (c + 1)]


def finish_kernel(
    heads, me_ref, mine_ref, pair_ref, vector_ref, small_ref, rows_ref, gk_ref, gvalue_ref, k_ref, v_ref,
    gkey_ref, out_ref,
):
    dk = gk_ref.shape[1] // heads
    dv = v_ref.shape[1] // heads
    key_scale = jnp.exp(unpack(column_of(rows_ref[...]), 3, heads) + small_ref[heads : heads + 1])
    for h in range(heads):
        ks, vs, one = slice(dk * h, dk * (h + 1)), slice(dv * h, dv * (h + 1)), slice(h, h + 1)
        following = of_head(h, heads, me_ref[0] % 2, mine_ref, pair_ref).reshape(dk, dv)
        high, low = split(following)
        carried = dot(v_ref[:, vs], high, 1, 1) + dot(v_ref[:, vs], low, 1, 1) + vector_ref[one]
        gkey_ref[:, ks] = (gk_ref[:, ks] + key_scale[:, one] * carried).astype(BF16)
        carried = dot(k_ref[:, ks], high, 1, 0) + dot(k_ref[:, ks], low, 1, 0)
        out_ref[:, vs] = (gvalue_ref[:, vs] + key_scale[:, one] * carried).astype(BF16)


def sum_kernel(got_ref, *refs):
    out_ref = refs[-1]
    total = jnp.sum(got_ref[...], axis=0, keepdims=True)
    out_ref[...] = jnp.broadcast_to(total, out_ref.shape)


def place_kernel(got_ref, first_ref, second_ref):
    heads = first_ref.shape[0]
    tiles, _, width = got_ref.shape
    for c in range(tiles):
        first_ref[:, width * c : width * (c + 1)] = got_ref[c, :heads]
        second_ref[:, width * c : width * (c + 1)] = got_ref[c, heads:]


class Fetched:
    def __init__(self, copy, ref):
        self.copy, self.ref, self.waited = copy, ref, False

    def ready(self):
        if not self.waited:
            self.copy.wait()
            self.waited = True
        return self.ref

    @property
    def shape(self):
        return self.ref.shape

    def __getitem__(self, at):
        return self.ready()[at]


class Stored:
    def __init__(self, copy, ref):
        self.copy, self.ref, self.sent = copy, ref, False

    @property
    def shape(self):
        return self.ref.shape

    def send(self):
        if not self.sent:
            self.copy.start()
            self.sent = True

    def __getitem__(self, at):
        return self.ref[at]

    def __setitem__(self, at, value):
        self.ref[at] = value


def call(body, outs, ins, limit=24):
    outs = [(k, o if isinstance(o, jax.ShapeDtypeStruct) else jax.ShapeDtypeStruct(o, F32)) for k, o in outs]
    spaces = {"s": pltpu.SMEM, "v": pltpu.VMEM, "h": pltpu.HBM, "m": pltpu.HBM, "a": pltpu.HBM}
    scratch = [
        (pltpu.SMEM if k == "m" else pltpu.VMEM)(a.shape, a.dtype) for k, a in ins + outs if k in "hm"
    ]
    scratch.append(pltpu.SemaphoreType.DMA((max(len(scratch), 1),)))

    def kernel(*refs):
        given, rest = refs[: len(ins)], refs[len(ins) :]
        results, buffers, sems = rest[: len(outs)], rest[len(outs) : -1], rest[-1]
        taken, made, used = [], [], 0
        for (kind, _), ref in zip(ins, given):
            if kind in "hm":
                copy = pltpu.make_async_copy(ref, buffers[used], sems.at[used])
                copy.start()
                ref = Fetched(copy, buffers[used])
                used += 1
            taken.append(ref)
        for (kind, _), ref in zip(outs, results):
            if kind == "h":
                copy = pltpu.make_async_copy(buffers[used], ref, sems.at[used])
                ref = Stored(copy, buffers[used])
                used += 1
            made.append(ref)
        body(*taken, *made)
        for ref in taken:
            if isinstance(ref, Fetched):
                ref.ready()
        for ref in made:
            if isinstance(ref, Stored):
                ref.send()
        for ref in made:
            if isinstance(ref, Stored):
                ref.copy.wait()

    return pl.pallas_call(
        kernel,
        out_shape=[pltpu.HBM(o.shape, o.dtype) if k == "h" else o for k, o in outs],
        in_specs=[pl.BlockSpec(memory_space=spaces[k]) for k, _ in ins],
        out_specs=[pl.BlockSpec(memory_space=spaces[k]) for k, _ in outs],
        scratch_shapes=scratch,
        compiler_params=pltpu.CompilerParams(vmem_limit_bytes=limit * 1024 * 1024),
    )(*[pltpu.with_memory_space_constraint(a, pltpu.HBM) if k in "hma" else a for k, a in ins])


def unpack(x, i, heads):
    return pltpu.roll(x, 128 - heads * i, 1) if i else x


def exchange(x, axis, groups=None):
    return lax.all_to_all(x, axis, 0, 0, axis_index_groups=groups)


def local(
    layer_input, queries, keys, values, grad_out, doc_pos, w_input, b_input, w_forget, b_forget
):
    x, q, k, v, g = layer_input[0], queries[0], keys[0], values[0], grad_out[0]
    heads = w_input.shape[1]
    n = q.shape[0]
    dk, dv = q.shape[1] // heads, v.shape[1] // heads
    scale = dk ** (-0.5)
    devices = lax.axis_size("ctx")
    count = devices // 2
    me = lax.axis_index("ctx").astype(jnp.int32).reshape(1)
    part = functools.partial
    slabs = heads * dk // 8
    cores = [[2 * i + c for i in range(count)] for c in range(2)]

    def to_pair(a):
        return lax.ppermute(a, "ctx", [(i, i ^ 1) for i in range(devices)])

    low = jax.ShapeDtypeStruct

    def given(kinds, *arrays):
        return list(zip(kinds, arrays, strict=True))

    give, turned, column, tile, rows = call(
        part(gates_kernel, heads),
        given(
            "vvvvh", (slabs // 2 + 1, 8, dv), low((heads * dk, n), BF16), (n, 128), (8, 128), (24, n)
        ),
        given("shhmmhhhh", me, w_input.T, w_forget.T, b_input, b_forget, doc_pos, k, x, v),
    )
    pair = to_pair(give)
    (memory,) = call(
        part(products_kernel, heads), given("v", (count, 8, dv)), given("svhv", me, turned, v, column)
    )
    (pay,) = call(
        part(first_kernel, heads),
        given("v", (count, 8, dv + 128)),
        given("svvv", me, memory, tile, pair),
    )
    first = exchange(pay, "ctx", cores)
    even_memory, even_tile, turned, wl, pc, gv, sums = call(
        part(pairs_kernel, heads),
        given(
            "hvvhhhv", (count, 8, dv), (8, 128), low((heads * dk, n), BF16), *[(heads, n, n)] * 3, (16, n)
        ),
        given("svvvhhhhh", me, memory, tile, pair, rows, q, k, v, g),
    )
    give, column, coef, now, coef_later, later, small, tokens = call(
        part(dual_kernel, heads, scale),
        given(
            "vvvvvvhh", (count, 8, dv), (n, 128), (2, count, 128), (16, 128),
            (2, count, 128), (count, 128), (16, 128), (24, n),
        ),
        given("svvhvvh", me, first, even_tile, rows, sums, turned, g),
    )
    pair = to_pair(give)
    (dual,) = call(
        part(products_kernel, heads), given("v", (count, 8, dv)), given("svhv", me, turned, g, column)
    )
    (before,) = call(before_kernel, given("v", (count, 8, dv)), given("vv", first, coef))
    pay, odd_dual = call(
        part(second_kernel, heads),
        given("vh", (count, 8, 2 * dv), (count, 8, dv)),
        given("svvvv", me, before, now, dual, pair),
    )
    second = exchange(pay, "ctx", cores)
    give, mine = call(
        part(halves_kernel, heads),
        given("vv", (count, 8, dv), (count, 8, dv)),
        given("svvv", me, second, even_memory, now),
    )
    pair = to_pair(give)
    after, crossing = call(
        part(mine_kernel, heads),
        given("vv", (count, 2 * dv // 128, 4, 128), (n, 128)),
        given("svvvvv", me, mine, second, coef_later, q, g),
    )
    pay, tile, gt = call(
        part(vector_kernel, heads, scale),
        given("vvv", (count, 2 * dv // 128 + 1, 4, 128), (8, 128), (8, n)),
        given("svvvvvvvv", me, mine, pair, after, crossing, tokens, sums, q, g),
    )
    third = exchange(pay, "ctx", cores)
    states, grad_q, gvalue, gk, row, cold = call(
        part(inner_kernel, heads, scale),
        given("hhhhhh", (slabs, 8, dv), low(q.shape, BF16), v.shape, k.shape, (8, n), (8, n)),
        given("svvvhhhhhhhh", me, mine, pair, gt, tokens, small, wl, pc, gv, q, k, g),
    )
    give, mine, sums = call(
        part(after_kernel, heads),
        given("vvv", (count + 1, 8, dv), (count, 8, dv), (8, 128)),
        given("svvvhva", me, third, later, now, odd_dual, tile, gk),
    )
    pair = to_pair(give)
    (along,) = call(part(along_kernel, heads), given("v", (n, 128)), given("svvv", me, mine, k, v))
    batch, across_x = lax.axis_size("dp"), 4
    tiles = batch * across_x
    at = [[[(z * across_x + i) * 2 + c for i in range(across_x)] for c in range(2)] for z in range(count // across_x)]
    planes = [[i * batch + d for i in row for d in range(batch)] for z in at for row in z]
    lines = [[row[i] for z in at for row in z] for i in range(across_x)]
    chunk = (8, x.shape[1] // tiles)
    vector, pay = call(
        part(weights_kernel, heads),
        given("hh", (8, 128), (tiles, *chunk)),
        given(
            "svvvvvvvhhhhv", me, mine, pair, sums, along, now, k, v, states, rows, row, cold, x
        ),
    )
    got = exchange(pay, ("ctx", "dp"), planes)
    grad_k, grad_v = call(
        part(finish_kernel, heads),
        given("hh", low(k.shape, BF16), low(v.shape, BF16)),
        given("svvhhhhhhh", me, mine, pair, vector, small, rows, gk, gvalue, k, v),
    )
    (pay,) = call(sum_kernel, given("v", (len(lines[0]), *chunk)), given("va", got, grad_k))
    got = exchange(pay, "ctx", lines)
    (pay,) = call(sum_kernel, given("v", (tiles, *chunk)), given("v", got))
    got = exchange(pay, ("ctx", "dp"), planes)
    first, second = call(
        place_kernel, given("vv", (heads, x.shape[1]), (heads, x.shape[1])), given("v", got)
    )
    return (grad_q[None], grad_k[None], grad_v[None], first.T, second.T)


def solution(mesh):
    split_rows = P("dp", "ctx", None)
    placed = (split_rows,) * 5 + (P("dp", "ctx"),) + (P(),) * 4
    return jax.shard_map(
        local,
        mesh=mesh,
        in_specs=placed,
        out_specs=(split_rows, split_rows, split_rows, P(), P()),
        check_vma=False,
    )
```

```python
import functools

import jax
import jax.numpy as jnp
from jax import lax
from jax.experimental import pallas as pl
from jax.experimental.pallas import tpu as pltpu
from jax.sharding import PartitionSpec as P

NEG = -1e30
BIG = 1e30
F32 = jnp.float32
BF16 = jnp.bfloat16


def dot(a, b, ca, cb):
    return lax.dot_general(a, b, (((ca,), (cb,)), ((), ())), preferred_element_type=F32)


def split(x):
    high = x.astype(BF16)
    return high, (x - high.astype(F32)).astype(BF16)


def dot_left(x, b, ca, cb):
    high, low = split(x)
    return dot(high, b, ca, cb) + dot(low, b, ca, cb)


def dot_right(a, x, ca, cb):
    high, low = split(x)
    return dot(a, high, ca, cb) + dot(a, low, ca, cb)


def thirds(x):
    high = x.astype(BF16).astype(F32)
    middle = (x - high).astype(BF16).astype(F32)
    return [high, middle, x - high - middle]


def times_ones(x, ones):
    parts = dot(jnp.concatenate(thirds(x), axis=0).astype(BF16), ones.astype(F32).astype(BF16), 1, 0)
    return parts[:8] + parts[8:16] + parts[16:24]


def ones_times(ones, x):
    parts = dot(ones.astype(F32).astype(BF16), jnp.concatenate(thirds(x), axis=1).astype(BF16), 1, 0)
    return parts[:, :128] + parts[:, 128:256] + parts[:, 256:]


def iota(shape, dim):
    return lax.broadcasted_iota(jnp.int32, shape, dim)


def column_of(rows):
    r, n = rows.shape
    padded = jnp.concatenate([rows, jnp.zeros((128 - r, n), F32)], axis=0)
    return padded.T


def put(acc, col, h):
    return jnp.where(iota(acc.shape, 1) == h, col, acc)


def down(row, heads):
    return jnp.concatenate([pick(row, h) for h in range(heads)], axis=0)


def across(column):
    row = jnp.zeros((1, 128), F32)
    for h in range(column.shape[0]):
        row = put(row, column[h : h + 1], h)
    return row


def padded(rows):
    return jnp.concatenate([rows, jnp.zeros((8 - rows.shape[0], rows.shape[1]), F32)], axis=0)


def rows_times(rows, b):
    parts = dot(jnp.concatenate(thirds(padded(rows)), axis=0).astype(BF16), b, 1, 0)
    return parts[:8] + parts[8:16] + parts[16:24]


def pick(row, lane):
    return jnp.sum(jnp.where(iota(row.shape, 1) == lane, row, 0.0), axis=1, keepdims=True)


def outer_products(side, heads, turned_ref, rows_ref, columns, out_ref):
    half = heads // 2
    dk, dv = turned_ref.shape[0] // heads, rows_ref.shape[1] // heads
    columns = jnp.where(side == 0, columns, pltpu.roll(columns, 128 - half, 1))
    for i in range(half):
        at = pl.multiple_of((side * half + i) * dv, dv)
        weighted = rows_ref[:, pl.ds(at, dv)].astype(F32) * columns[:, i : i + 1]
        at = pl.multiple_of((side * half + i) * dk, dk)
        product = dot_right(turned_ref[pl.ds(at, dk), :], weighted, 1, 0)
        out_ref[dk // 8 * i : dk // 8 * (i + 1)] = product.reshape(dk // 8, 8, dv)


def products_kernel(heads, me_ref, turned_ref, rows_ref, column_ref, out_ref):
    outer_products(me_ref[0] % 2, heads, turned_ref, rows_ref, column_ref[...], out_ref)


def gates_kernel(
    heads, me_ref, wi_ref, wf_ref, bi_ref, bf_ref, pos_ref, k_ref, x_ref, v_ref,
    give_ref, turned_ref, column_ref, tile_ref, rows_ref,
):
    core = me_ref[0] % 2
    n = x_ref.shape[0]
    dk = k_ref.shape[1] // heads
    dv = v_ref.shape[1] // heads
    weights = [wi_ref[...].astype(F32), wf_ref[...].astype(F32)]
    weights.append(jnp.zeros((16 - 2 * heads, weights[0].shape[1]), F32))
    weights = jnp.concatenate(weights, axis=0).astype(BF16)
    k = k_ref[...]
    turned = k.T
    gates = dot(x_ref[...], weights, 1, 1)
    gates = jnp.concatenate([gates, jnp.zeros((n, 112), F32)], axis=1).T[: 2 * heads]
    row8 = iota(gates.shape, 0)
    for h in range(heads):
        gates = gates + jnp.where(row8 == h, bi_ref[h], 0.0)
        gates = gates + jnp.where(row8 == h + heads, bf_ref[h], 0.0)
    in_gate, forget_pre = gates[:heads], gates[heads:]
    log_forget = jnp.minimum(forget_pre, 0.0) - jnp.log1p(jnp.exp(-jnp.abs(forget_pre)))
    start = (pos_ref[...] == 0).astype(F32)
    stacked = jnp.concatenate([log_forget, start, jnp.zeros((7 - heads, n), F32)], axis=0)
    cum = times_ones(stacked, iota((n, n), 0) <= iota((n, n), 1))
    lc, dc = cum[:heads], cum[heads : heads + 1]
    total, last = lc[:, n - 1 :], dc[:, n - 1 :]
    key_log = jnp.where(dc == last, total - lc + in_gate, NEG)
    rows_ref[...] = jnp.concatenate(
        [in_gate, forget_pre, lc, key_log, dc, jnp.zeros((7, n), F32)], axis=0
    )
    rows_ref.send()
    own_max = jnp.max(key_log, axis=1, keepdims=True)
    weight = jnp.exp(key_log - own_max)
    sums = rows_times(weight, k)
    column = column_of(weight)
    column_ref[...] = column
    turned_ref[...] = turned
    half = give_ref.shape[0] - 1
    outer_products(1 - core, heads, turned_ref, v_ref, column, give_ref)
    cut = jnp.where(last > 0.5, BIG, 0.0)
    tile = jnp.concatenate(
        [sums[h : h + 1, dk * h : dk * (h + 1)] for h in range(heads)]
        + [across(own_max), across(total - cut), across(in_gate[:, :1] - lc[:, :1])]
        + [jnp.broadcast_to(jnp.where(dc[:, :1] < 0.5, 1.0, 0.0), (1, 128))],
        axis=0,
    )
    tile_ref[...] = tile
    give_ref[half] = jnp.concatenate([tile, jnp.zeros((8, dv - 128), F32)], axis=1)


def first_kernel(heads, me_ref, mem_ref, tile_ref, got_ref, out_ref):
    core = me_ref[0] % 2
    half, dv = out_ref.shape[0], mem_ref.shape[2]
    mine, other = tile_ref[...], got_ref[half, :, :128]
    even = jnp.where(core == 0, mine, other)
    odd = jnp.where(core == 0, other, mine)
    chip_max = jnp.maximum(even[4:5] + odd[5:6], odd[4:5])
    keep = jnp.exp(even[4:5] + odd[5:6] - chip_max)
    add = jnp.exp(odd[4:5] - chip_max)
    vectors = [
        keep[:, h : h + 1] * even[h : h + 1] + add[:, h : h + 1] * odd[h : h + 1]
        for h in range(heads)
    ]
    both = jnp.where(iota(even.shape, 1) < heads, even, pltpu.roll(odd, heads, 1))
    tile = jnp.concatenate(vectors + [both[heads:]], axis=0)
    out_ref[:, :, dv:] = jnp.broadcast_to(tile[None], (half, 8, 128))
    weight_mine = jnp.where(core == 0, keep, add)
    weight_other = jnp.where(core == 0, add, keep)
    per_head = half // (heads // 2)
    for i in range(heads // 2):
        at = core * (heads // 2) + i
        slab = slice(i * per_head, (i + 1) * per_head)
        own = mem_ref[slab]
        out_ref[slab, :, :dv] = pick(weight_mine, at) * own + pick(weight_other, at) * got_ref[slab]


def pairs_kernel(
    heads, me_ref, mem_ref, tile_ref, got_ref, rows_ref, q_ref, k_ref, v_ref, g_ref,
    even_ref, even_tile_ref, turned_ref, wl_ref, pc_ref, gv_ref, sums_ref,
):
    core = me_ref[0] % 2
    half = even_ref.shape[0]
    even_ref[...] = jnp.where(core == 0, mem_ref[...], got_ref[:half])
    even_ref.send()
    even_tile_ref[...] = jnp.where(core == 0, tile_ref[...], got_ref[half, :, :128])
    n = q_ref.shape[0]
    dk = k_ref.shape[1] // heads
    dv = v_ref.shape[1] // heads
    rows = rows_ref[...]
    lc = column_of(rows)
    place = 4 * heads
    mask = (iota((n, n), 0) >= iota((n, n), 1)) & (lc[:, place : place + 1] == rows[place : place + 1])
    turned_ref[...] = q_ref[...].T
    sums = jnp.zeros((n, 128), F32)
    for h in range(heads):
        offset = rows[h : h + 1] - rows[2 * heads + h : 2 * heads + h + 1]
        pair_log = jnp.where(mask, lc[:, 2 * heads + h : 2 * heads + h + 1] + offset, NEG)
        row_max = jnp.max(pair_log, axis=1, keepdims=True)
        weight = jnp.exp(pair_log - row_max)
        ks, vs = slice(dk * h, dk * (h + 1)), slice(dv * h, dv * (h + 1))
        coupled = dot(q_ref[:, ks], k_ref[:, ks], 1, 1) * weight
        grad_pair = dot(g_ref[:, vs], v_ref[:, vs], 1, 1)
        wl_ref[h] = weight
        pc_ref[h] = coupled
        gv_ref[h] = grad_pair
        sums = put(sums, row_max, h)
        sums = put(sums, jnp.sum(coupled, axis=1, keepdims=True), heads + h)
        sums = put(sums, jnp.sum(coupled * grad_pair, axis=1, keepdims=True), 2 * heads + h)
    sums_ref[...] = sums.T[: sums_ref.shape[0]]


def shift_down(x, d, fill):
    return jnp.where(iota(x.shape, 0) < d, fill, pltpu.roll(x, d, 0))


def shift_up(x, d, fill):
    size = x.shape[0]
    return jnp.where(iota(x.shape, 0) >= size - d, fill, pltpu.roll(x, size - d, 0))


def dual_kernel(
    heads, scale, me_ref, got_ref, tile_ref, rows_ref, sums_ref, turned_ref, g_ref,
    give_ref, column_ref, coef_ref, now_ref, coef_later_ref, later_ref, small_ref, tokens_ref,
):
    count = got_ref.shape[0]
    n = g_ref.shape[0]
    dk = turned_ref.shape[0] // heads
    dv = g_ref.shape[1] // heads
    me = me_ref[0]
    core, chip = me % 2, me // 2
    max_even, total_even = got_ref[:, heads, dv:], got_ref[:, heads + 1, dv:]
    first_even, valid_even = got_ref[:, heads + 2, dv:], got_ref[:, heads + 3, dv:]
    max_odd, total_odd, first_odd, valid_odd = (
        pltpu.roll(x, 128 - heads, 1) for x in (max_even, total_even, first_even, valid_even)
    )
    row = iota(max_even.shape, 0)
    lane = iota(max_even.shape, 1)
    steps = [1 << i for i in range((count - 1).bit_length())]
    chip_max = jnp.maximum(max_even + total_odd, max_odd)
    total = total_even + total_odd
    t, m = total, chip_max
    for d in steps:
        m = jnp.maximum(shift_down(m, d, NEG) + t, m)
        t = shift_down(t, d, 0.0) + t
    in_even = shift_down(m, 1, NEG)
    in_odd = jnp.maximum(in_even + total_even, max_even)
    dual_even = jnp.where(valid_even > 0.5, -jnp.maximum(in_even, first_even), NEG)
    dual_odd = jnp.where(valid_odd > 0.5, -jnp.maximum(in_odd, first_odd), NEG)
    chip_dual = jnp.maximum(dual_even, total_even + dual_odd)
    t, r = total, chip_dual
    for d in steps:
        r = jnp.maximum(r, t + shift_up(r, d, NEG))
        t = t + shift_up(t, d, 0.0)
    later_odd = shift_up(r, 1, NEG)
    later_even = jnp.maximum(dual_odd, total_odd + later_odd)
    my_head = (heads // 2) * core + chip // (2 * count // heads)
    coefs = (
        jnp.exp(in_even + total - m),
        jnp.exp(chip_max - m),
        jnp.exp(total + later_odd - r),
        jnp.exp(chip_dual - r),
    )
    for i, c in enumerate(coefs):
        mine = jnp.sum(jnp.where(lane == my_head, c, 0.0), axis=1, keepdims=True)
        (coef_ref if i < 2 else coef_later_ref)[i % 2] = jnp.broadcast_to(mine, c.shape)

    def here(x):
        return jnp.sum(jnp.where(row == chip, x, 0.0), axis=0, keepdims=True)

    def mine_of(even, odd):
        return here(jnp.where(core == 0, even, odd))

    in_me, later_me = mine_of(in_even, in_odd), mine_of(later_even, later_odd)
    dual_me, total_me = mine_of(dual_even, dual_odd), mine_of(total_even, total_odd)
    keep = here(jnp.exp(in_even + total_even - in_odd))
    add = here(jnp.exp(max_even - in_odd))
    later_row = iota((count, count), 0) < iota((count, count), 1)
    between = ones_times(later_row, jnp.where(row < chip, total, 0.0))
    weight = jnp.where(
        row < chip, jnp.exp(jnp.minimum(chip_max + between - here(in_even), 0.0)), 0.0
    )
    earlier_row = iota((count, count), 0) > iota((count, count), 1)
    between = ones_times(earlier_row, jnp.where(row > chip, total, 0.0))
    source = jnp.where(core == 0, dual_even, total_even + dual_odd)
    later_ref[...] = jnp.where(
        row > chip, jnp.exp(jnp.minimum(source + between - here(later_odd), 0.0)), 0.0
    )
    even_tile = tile_ref[...]
    vectors = []
    for h in range(heads):
        one = slice(h, h + 1)
        vector = jnp.sum(weight[:, one] * got_ref[:, h, dv:], axis=0, keepdims=True)
        second = keep[:, one] * vector + add[:, one] * even_tile[one]
        vectors.append(jnp.where(core == 0, vector, second))
    small = jnp.concatenate(
        vectors
        + [
            later_me,
            jnp.exp(in_me + total_me + later_me),
            keep,
            add,
            here(jnp.exp(total_odd + later_odd - later_even)),
            here(jnp.exp(dual_odd - later_even)),
            here(jnp.exp(dual_even - chip_dual)),
            here(jnp.exp(total_even + dual_odd - chip_dual)),
            jnp.zeros((8 - heads, 128), F32),
        ],
        axis=0,
    )

    small_ref[...] = small
    small_ref.send()
    now_ref[...] = small
    lc = rows_ref[2 * heads : 3 * heads]
    open_query = rows_ref[4 * heads : 4 * heads + 1] < 0.5
    inner_max = sums_ref[:heads]
    cross_log = jnp.where(open_query, lc + down(in_me, heads), NEG)
    row_max = jnp.maximum(inner_max, cross_log)
    inside = jnp.exp(inner_max - row_max)
    cross = jnp.exp(cross_log - row_max)
    qn = [
        rows_times(small[:heads], turned_ref[dk * h : dk * (h + 1)])[h : h + 1] for h in range(heads)
    ]
    qn = jnp.concatenate(qn, axis=0)
    sums = scale * (sums_ref[heads : 2 * heads] * inside + cross * qn)
    floor = jnp.exp(-row_max)
    size = jnp.abs(sums)
    inverse = 1.0 / jnp.maximum(size, floor)
    active = jnp.where(size > floor, jnp.where(sums > 0.0, 1.0, -1.0), 0.0)
    query_weight = jnp.exp(jnp.minimum(lc - row_max - down(dual_me, heads), 0.0))
    query_weight = jnp.where(open_query, query_weight, 0.0)
    tokens_ref[...] = jnp.concatenate([inside, cross, inverse, active, query_weight, qn], axis=0)
    tokens_ref.send()
    grad_weight = column_of(query_weight * inverse * scale)
    column_ref[...] = grad_weight
    outer_products(1 - core, heads, turned_ref, g_ref, grad_weight, give_ref)


def wide(coef_ref, i, j, reps):
    return jnp.concatenate([coef_ref[i, pl.ds(j, 1), :]] * reps, axis=1)


def before_kernel(got_ref, coef_ref, out_ref):
    count, _, dv = out_ref.shape
    reps = dv // 128

    def forward(j, state):
        out_ref[j] = state
        step = wide(coef_ref, 1, j, reps) * got_ref[j, :, :dv]
        return wide(coef_ref, 0, j, reps) * state + step

    lax.fori_loop(0, count, forward, jnp.zeros((8, dv), F32), unroll=8)


def second_kernel(heads, me_ref, before_ref, small_ref, dual_ref, pair_ref, out_ref, odd_ref):
    core = me_ref[0] % 2
    count, _, dv = dual_ref.shape
    odd_ref[...] = jnp.where(core == 0, pair_ref[...], dual_ref[...])
    odd_ref.send()
    out_ref[:, :, :dv] = before_ref[...]
    even, odd = small_ref[10:11], small_ref[11:12]
    weight_mine = jnp.where(core == 0, even, odd)
    weight_other = jnp.where(core == 0, odd, even)
    per_head = count // (heads // 2)
    for i in range(heads // 2):
        at = core * (heads // 2) + i
        slab = slice(i * per_head, (i + 1) * per_head)
        step = pick(weight_other, at) * pair_ref[slab]
        out_ref[slab, :, dv:] = pick(weight_mine, at) * dual_ref[slab] + step


def halves_kernel(heads, me_ref, got_ref, even_ref, small_ref, give_ref, mine_ref):
    core = me_ref[0] % 2
    count, dv = give_ref.shape[0], give_ref.shape[2]
    per_head = count // (heads // 2)
    even, small = even_ref, small_ref[...]

    def fill(to_even_ref, to_odd_ref):
        for i in range(heads // 2):
            at = core * (heads // 2) + i
            slab = slice(i * per_head, (i + 1) * per_head)
            before = got_ref[slab, :, :dv]
            to_even_ref[slab] = before
            to_odd_ref[slab] = pick(small[6:7], at) * before + pick(small[7:8], at) * even[slab]

    @pl.when(core == 0)
    def _():
        fill(mine_ref, give_ref)

    @pl.when(core == 1)
    def _():
        fill(give_ref, mine_ref)


def crossings(side, heads, memory_ref, q_ref, g_ref):
    half = heads // 2
    n, dk, dv = q_ref.shape[0], q_ref.shape[1] // heads, g_ref.shape[1] // heads
    result = jnp.zeros((n, 128), F32)
    for i in range(half):
        memory = memory_ref[dk // 8 * i : dk // 8 * (i + 1)].reshape(dk, dv)
        at = pl.multiple_of((side * half + i) * dk, dk)
        crossing = dot_right(q_ref[:, pl.ds(at, dk)], memory, 1, 0)
        at = pl.multiple_of((side * half + i) * dv, dv)
        along = g_ref[:, pl.ds(at, dv)].astype(F32) * crossing
        result = put(result, jnp.sum(along, axis=1, keepdims=True), i)
    return result


def merged(core, heads, mine, other):
    half = heads // 2
    first = jnp.where(core == 0, mine, other)
    return first + pltpu.roll(jnp.where(core == 0, other, mine), half, 1)


def mine_kernel(heads, me_ref, mine_ref, got_ref, coef_ref, q_ref, g_ref, out_ref, gc_ref):
    count, dv = mine_ref.shape[0], mine_ref.shape[2]
    reps = dv // 128

    def backward(i, state):
        j = count - 1 - i
        for i in range(2):
            for c in range(reps):
                out_ref[j, i * reps + c] = state[4 * i : 4 * (i + 1), 128 * c : 128 * (c + 1)]
        step = wide(coef_ref, 1, j, reps) * got_ref[j, :, dv:]
        return wide(coef_ref, 0, j, reps) * state + step

    lax.fori_loop(0, count, backward, jnp.zeros((8, dv), F32), unroll=8)
    gc_ref[...] = crossings(me_ref[0] % 2, heads, mine_ref, q_ref, g_ref)


def vector_kernel(
    heads, scale, me_ref, mine_ref, pair_ref, after_ref, crossing_ref, tokens_ref, sums_ref, q_ref, g_ref,
    out_ref, tile_ref, gt_ref,
):
    core = me_ref[0] % 2
    dk = q_ref.shape[1] // heads
    count, pieces = mine_ref.shape[0], after_ref.shape[1]
    out_ref[:, :pieces] = after_ref[...]
    gc = merged(core, heads, crossing_ref[...], crossings(1 - core, heads, pair_ref, q_ref, g_ref))
    inside, cross, inverse, active, query_weight = (
        tokens_ref[heads * i : heads * (i + 1)] for i in range(5)
    )
    gc = gc.T[:heads]
    gt = sums_ref[2 * heads : 3 * heads] * inside + cross * gc
    gt = -scale * gt * inverse * inverse * active
    gt_ref[...] = jnp.concatenate([gt, gc], axis=0)
    vectors = rows_times(query_weight * gt * scale, q_ref[...])
    vectors = [vectors[h : h + 1, dk * h : dk * (h + 1)] for h in range(heads)]
    tile = jnp.concatenate(vectors + [jnp.zeros((8 - heads, 128), F32)], axis=0)
    tile_ref[...] = tile
    out_ref[:, pieces] = jnp.broadcast_to(tile[None, :4], (count, 4, 128))


def inner_kernel(
    heads, scale, me_ref, mine_ref, pair_ref, gt_ref, tokens_ref, small_ref, wl_ref, pc_ref, gv_ref,
    q_ref, k_ref, g_ref,
    mem_ref, gq_ref, gvalue_ref, gk_ref, row_ref, cold_ref,
):
    core, count = me_ref[0] % 2, mine_ref.shape[0]
    mem_ref[pl.ds(core * count, count)] = mine_ref[...]
    mem_ref[pl.ds((1 - core) * count, count)] = pair_ref[...]
    mem_ref.send()
    n = q_ref.shape[0]
    dk = q_ref.shape[1] // heads
    dv = g_ref.shape[1] // heads
    tokens = column_of(jnp.concatenate([tokens_ref[...], gt_ref[...]], axis=0))
    inside, cross, inverse, qn, gt, gc = (unpack(tokens, i, heads) for i in (0, 1, 2, 5, 6, 7))
    row_part = scale * cross * (inverse * gc + gt * qn)
    for h in range(heads):
        ks, vs = slice(dk * h, dk * (h + 1)), slice(dv * h, dv * (h + 1))
        one = slice(h, h + 1)
        q, k, g = q_ref[:, ks], k_ref[:, ks], g_ref[:, vs]
        memory = mem_ref[dk // 8 * h : dk // 8 * (h + 1)].reshape(dk, dv)
        factor = inside[:, one] * (inverse[:, one] * gv_ref[h] + gt[:, one])
        pair_grad = factor * pc_ref[h]
        cold_ref[one, :] = scale * jnp.sum(pair_grad, axis=0, keepdims=True)
        row_part = row_part + put(
            jnp.zeros((n, 128), F32), scale * jnp.sum(pair_grad, axis=1, keepdims=True), h
        )
        score_high, score_low = split(factor * wl_ref[h])
        grad_query = dot(score_high, k, 1, 0) + dot(score_low, k, 1, 0)
        grad_query = grad_query + cross[:, one] * (
            inverse[:, one] * dot_right(g, memory, 1, 1) + gt[:, one] * small_ref[one]
        )
        gq_ref[:, ks] = (scale * grad_query).astype(BF16)
        gk_ref[:, ks] = scale * (dot(score_high, q, 0, 0) + dot(score_low, q, 0, 0))
        coupled = pc_ref[h] * (scale * inside[:, one] * inverse[:, one])
        gvalue_ref[:, vs] = dot_left(coupled, g, 0, 0)
    row_ref[...] = row_part.T[:8]
    cold_ref[heads:, :] = jnp.zeros((8 - heads, n), F32)


def after_kernel(
    heads, me_ref, got_ref, later_ref, small_ref, odd_ref, tile_ref, unused_ref,
    give_ref, mine_ref, sum_ref,
):
    core = me_ref[0] % 2
    count, dv = mine_ref.shape[0], mine_ref.shape[2]
    reps = dv // 128
    per_head = count // (heads // 2)
    vectors = [
        jnp.sum(later_ref[:, h : h + 1] * got_ref[:, 2 * reps, h, :], axis=0, keepdims=True)
        for h in range(heads)
    ]
    tile = jnp.concatenate(vectors + [tile_ref[:heads]], axis=0)
    sum_ref[...] = tile
    give_ref[count] = jnp.concatenate([tile, jnp.zeros((8, dv - 128), F32)], axis=1)
    odd, small = odd_ref.ready(), small_ref[...]

    def fill(to_even_ref, to_odd_ref):
        for i in range(heads // 2):
            at = core * (heads // 2) + i
            slab = slice(i * per_head, (i + 1) * per_head)
            after = [
                jnp.concatenate([got_ref[slab, i * reps + c] for c in range(reps)], axis=2)
                for i in range(2)
            ]
            after = jnp.concatenate(after, axis=1)
            to_odd_ref[slab] = after
            to_even_ref[slab] = pick(small[8:9], at) * after + pick(small[9:10], at) * odd[slab]

    @pl.when(core == 0)
    def _():
        fill(mine_ref, give_ref)

    @pl.when(core == 1)
    def _():
        fill(give_ref, mine_ref)


def alongs(side, heads, after_ref, k_ref, v_ref):
    half = heads // 2
    n, dk, dv = k_ref.shape[0], k_ref.shape[1] // heads, v_ref.shape[1] // heads
    result = jnp.zeros((n, 128), F32)
    for i in range(half):
        following = after_ref[dk // 8 * i : dk // 8 * (i + 1)].reshape(dk, dv)
        at = pl.multiple_of((side * half + i) * dk, dk)
        carried = dot_right(k_ref[:, pl.ds(at, dk)], following, 1, 0)
        at = pl.multiple_of((side * half + i) * dv, dv)
        along = v_ref[:, pl.ds(at, dv)].astype(F32) * carried
        result = put(result, jnp.sum(along, axis=1, keepdims=True), i)
    return result


def of_head(h, heads, core, mine_ref, pair_ref):
    half = heads // 2
    per_head = mine_ref.shape[0] // half
    slab = slice(per_head * (h % half), per_head * (h % half + 1))
    return jnp.where(core == h // half, mine_ref[slab], pair_ref[slab])


def along_kernel(heads, me_ref, mine_ref, k_ref, v_ref, out_ref):
    out_ref[...] = alongs(me_ref[0] % 2, heads, mine_ref, k_ref, v_ref)


def weights_kernel(
    heads, me_ref, mine_ref, pair_ref, sum_ref, along_ref, small_ref, k_ref, v_ref, mem_ref, rows_ref,
    row_ref, cold_ref, x_ref,
    vector_ref, pay_ref,
):
    core = me_ref[0] % 2
    n = k_ref.shape[0]
    dk = k_ref.shape[1] // heads
    dv = v_ref.shape[1] // heads
    count = mine_ref.shape[0]
    mine, other = sum_ref[...], pair_ref[count, :, :128]
    column_cross = merged(
        core, heads, along_ref[...], alongs(1 - core, heads, pair_ref, k_ref, v_ref)
    )
    through = []
    vectors = []
    for h in range(heads):
        ks, one = slice(dk * h, dk * (h + 1)), slice(h, h + 1)
        slab = slice(dk // 8 * h, dk // 8 * (h + 1))
        odd = mine[one] + other[one]
        even = small_ref[8:9, one] * odd + small_ref[9:10, one] * other[heads + h : heads + h + 1]
        vector = jnp.where(core == 0, even, odd)
        vectors.append(vector)
        along = jnp.sum(k_ref[:, ks].astype(F32) * vector, axis=1, keepdims=True)
        column_cross = column_cross + put(jnp.zeros((n, 128), F32), along, h)
        following = of_head(h, heads, core, mine_ref, pair_ref).reshape(dk, dv)
        product = jnp.sum(mem_ref[slab].reshape(dk, dv) * following, axis=0, keepdims=True)
        product = jnp.sum(product, axis=1, keepdims=True)
        product = product + jnp.sum(small_ref[one] * vector, axis=1, keepdims=True)
        through.append(product)
    vector_ref[...] = jnp.concatenate(vectors + [jnp.zeros((8 - heads, 128), F32)], axis=0)
    vector_ref.send()
    passing = padded(jnp.concatenate(through, axis=0) * down(small_ref[heads + 1 : heads + 2], heads))
    key_scale = jnp.exp(rows_ref[3 * heads : 4 * heads] + down(small_ref[heads : heads + 1], heads))
    crossing = padded(column_cross.T[:heads] * key_scale)
    row, inner = row_ref[...], cold_ref[...]
    after = iota((n, n), 0) >= iota((n, n), 1)
    suffix = times_ones(row - inner, after)
    prefix = times_ones(crossing, jnp.logical_not(after))
    grad_log = suffix + prefix + passing
    grad_forget = grad_log[:heads] / (1.0 + jnp.exp(rows_ref[heads : 2 * heads, :]))
    coefs = jnp.concatenate([(inner + crossing)[:heads], grad_forget], axis=0)
    high = coefs.astype(BF16).astype(F32)
    both = jnp.concatenate([high, coefs - high], axis=0).astype(BF16)
    product = dot(both, x_ref[...], 1, 0)
    result = product[: 2 * heads] + product[2 * heads :]
    tiles, _, width = pay_ref.shape
    for c in range(tiles):
        pay_ref[c] = result[:, width * c : width * (c + 1)]


def finish_kernel(
    heads, me_ref, mine_ref, pair_ref, vector_ref, small_ref, rows_ref, gk_ref, gvalue_ref, k_ref, v_ref,
    gkey_ref, out_ref,
):
    dk = gk_ref.shape[1] // heads
    dv = v_ref.shape[1] // heads
    key_scale = jnp.exp(unpack(column_of(rows_ref[...]), 3, heads) + small_ref[heads : heads + 1])
    for h in range(heads):
        ks, vs, one = slice(dk * h, dk * (h + 1)), slice(dv * h, dv * (h + 1)), slice(h, h + 1)
        following = of_head(h, heads, me_ref[0] % 2, mine_ref, pair_ref).reshape(dk, dv)
        high, low = split(following)
        carried = dot(v_ref[:, vs], high, 1, 1) + dot(v_ref[:, vs], low, 1, 1) + vector_ref[one]
        gkey_ref[:, ks] = (gk_ref[:, ks] + key_scale[:, one] * carried).astype(BF16)
        carried = dot(k_ref[:, ks], high, 1, 0) + dot(k_ref[:, ks], low, 1, 0)
        out_ref[:, vs] = (gvalue_ref[:, vs] + key_scale[:, one] * carried).astype(BF16)


def sum_kernel(got_ref, *refs):
    out_ref = refs[-1]
    total = jnp.sum(got_ref[...], axis=0, keepdims=True)
    out_ref[...] = jnp.broadcast_to(total, out_ref.shape)


def place_kernel(got_ref, first_ref, second_ref):
    heads = first_ref.shape[0]
    tiles, _, width = got_ref.shape
    for c in range(tiles):
        first_ref[:, width * c : width * (c + 1)] = got_ref[c, :heads]
        second_ref[:, width * c : width * (c + 1)] = got_ref[c, heads:]


class Fetched:
    def __init__(self, copy, ref):
        self.copy, self.ref, self.waited = copy, ref, False

    def ready(self):
        if not self.waited:
            self.copy.wait()
            self.waited = True
        return self.ref

    @property
    def shape(self):
        return self.ref.shape

    def __getitem__(self, at):
        return self.ready()[at]


class Stored:
    def __init__(self, copy, ref):
        self.copy, self.ref, self.sent = copy, ref, False

    @property
    def shape(self):
        return self.ref.shape

    def send(self):
        if not self.sent:
            self.copy.start()
            self.sent = True

    def __getitem__(self, at):
        return self.ref[at]

    def __setitem__(self, at, value):
        self.ref[at] = value


def call(body, outs, ins, limit=14):
    outs = [(k, o if isinstance(o, jax.ShapeDtypeStruct) else jax.ShapeDtypeStruct(o, F32)) for k, o in outs]
    spaces = {"s": pltpu.SMEM, "v": pltpu.VMEM, "h": pltpu.HBM, "m": pltpu.HBM, "a": pltpu.HBM}
    scratch = [
        (pltpu.SMEM if k == "m" else pltpu.VMEM)(a.shape, a.dtype) for k, a in ins + outs if k in "hm"
    ]
    scratch.append(pltpu.SemaphoreType.DMA((max(len(scratch), 1),)))

    def kernel(*refs):
        given, rest = refs[: len(ins)], refs[len(ins) :]
        results, buffers, sems = rest[: len(outs)], rest[len(outs) : -1], rest[-1]
        taken, made, used = [], [], 0
        for (kind, _), ref in zip(ins, given):
            if kind in "hm":
                copy = pltpu.make_async_copy(ref, buffers[used], sems.at[used])
                copy.start()
                ref = Fetched(copy, buffers[used])
                used += 1
            taken.append(ref)
        for (kind, _), ref in zip(outs, results):
            if kind == "h":
                copy = pltpu.make_async_copy(buffers[used], ref, sems.at[used])
                ref = Stored(copy, buffers[used])
                used += 1
            made.append(ref)
        body(*taken, *made)
        for ref in taken:
            if isinstance(ref, Fetched):
                ref.ready()
        for ref in made:
            if isinstance(ref, Stored):
                ref.send()
        for ref in made:
            if isinstance(ref, Stored):
                ref.copy.wait()

    return pl.pallas_call(
        kernel,
        out_shape=[pltpu.HBM(o.shape, o.dtype) if k == "h" else o for k, o in outs],
        in_specs=[pl.BlockSpec(memory_space=spaces[k]) for k, _ in ins],
        out_specs=[pl.BlockSpec(memory_space=spaces[k]) for k, _ in outs],
        scratch_shapes=scratch,
        compiler_params=pltpu.CompilerParams(vmem_limit_bytes=limit * 1024 * 1024),
    )(*[pltpu.with_memory_space_constraint(a, pltpu.HBM) if k in "hma" else a for k, a in ins])


def unpack(x, i, heads):
    return pltpu.roll(x, 128 - heads * i, 1) if i else x


def exchange(x, axis, groups=None):
    return lax.all_to_all(x, axis, 0, 0, axis_index_groups=groups)


def local(
    layer_input, queries, keys, values, grad_out, doc_pos, w_input, b_input, w_forget, b_forget
):
    x, q, k, v, g = layer_input[0], queries[0], keys[0], values[0], grad_out[0]
    heads = w_input.shape[1]
    n = q.shape[0]
    dk, dv = q.shape[1] // heads, v.shape[1] // heads
    scale = dk ** (-0.5)
    devices = lax.axis_size("ctx")
    count = devices // 2
    me = lax.axis_index("ctx").astype(jnp.int32).reshape(1)
    part = functools.partial
    slabs = heads * dk // 8
    cores = [[2 * i + c for i in range(count)] for c in range(2)]

    def to_pair(a):
        return lax.ppermute(a, "ctx", [(i, i ^ 1) for i in range(devices)])

    low = jax.ShapeDtypeStruct

    def given(kinds, *arrays):
        return list(zip(kinds, arrays, strict=True))

    give, turned, column, tile, rows = call(
        part(gates_kernel, heads),
        given(
            "vvvvh", (slabs // 2 + 1, 8, dv), low((heads * dk, n), BF16), (n, 128), (8, 128), (24, n)
        ),
        given("shhmmhhhh", me, w_input.T, w_forget.T, b_input, b_forget, doc_pos, k, x, v),
    )
    pair = to_pair(give)
    (memory,) = call(
        part(products_kernel, heads), given("v", (count, 8, dv)), given("svhv", me, turned, v, column)
    )
    (pay,) = call(
        part(first_kernel, heads),
        given("v", (count, 8, dv + 128)),
        given("svvv", me, memory, tile, pair),
    )
    first = exchange(pay, "ctx", cores)
    even_memory, even_tile, turned, wl, pc, gv, sums = call(
        part(pairs_kernel, heads),
        given(
            "hvvhhhv", (count, 8, dv), (8, 128), low((heads * dk, n), BF16), *[(heads, n, n)] * 3, (16, n)
        ),
        given("svvvhhhhh", me, memory, tile, pair, rows, q, k, v, g),
    )
    give, column, coef, now, coef_later, later, small, tokens = call(
        part(dual_kernel, heads, scale),
        given(
            "vvvvvvhh", (count, 8, dv), (n, 128), (2, count, 128), (16, 128),
            (2, count, 128), (count, 128), (16, 128), (24, n),
        ),
        given("svvhvvh", me, first, even_tile, rows, sums, turned, g),
    )
    pair = to_pair(give)
    (dual,) = call(
        part(products_kernel, heads), given("v", (count, 8, dv)), given("svhv", me, turned, g, column)
    )
    (before,) = call(before_kernel, given("v", (count, 8, dv)), given("vv", first, coef))
    pay, odd_dual = call(
        part(second_kernel, heads),
        given("vh", (count, 8, 2 * dv), (count, 8, dv)),
        given("svvvv", me, before, now, dual, pair),
    )
    second = exchange(pay, "ctx", cores)
    give, mine = call(
        part(halves_kernel, heads),
        given("vv", (count, 8, dv), (count, 8, dv)),
        given("svvv", me, second, even_memory, now),
    )
    pair = to_pair(give)
    after, crossing = call(
        part(mine_kernel, heads),
        given("vv", (count, 2 * dv // 128, 4, 128), (n, 128)),
        given("svvvvv", me, mine, second, coef_later, q, g),
    )
    pay, tile, gt = call(
        part(vector_kernel, heads, scale),
        given("vvv", (count, 2 * dv // 128 + 1, 4, 128), (8, 128), (8, n)),
        given("svvvvvvvv", me, mine, pair, after, crossing, tokens, sums, q, g),
    )
    third = exchange(pay, "ctx", cores)
    states, grad_q, gvalue, gk, row, cold = call(
        part(inner_kernel, heads, scale),
        given("hhhhhh", (slabs, 8, dv), low(q.shape, BF16), v.shape, k.shape, (8, n), (8, n)),
        given("svvvhhhhhhhh", me, mine, pair, gt, tokens, small, wl, pc, gv, q, k, g),
    )
    give, mine, sums = call(
        part(after_kernel, heads),
        given("vvv", (count + 1, 8, dv), (count, 8, dv), (8, 128)),
        given("svvvhva", me, third, later, now, odd_dual, tile, gk),
    )
    pair = to_pair(give)
    (along,) = call(part(along_kernel, heads), given("v", (n, 128)), given("svvv", me, mine, k, v))
    batch, across_x = lax.axis_size("dp"), 4
    tiles = batch * across_x
    at = [[[(z * across_x + i) * 2 + c for i in range(across_x)] for c in range(2)] for z in range(count // across_x)]
    planes = [[i * batch + d for i in row for d in range(batch)] for z in at for row in z]
    lines = [[row[i] for z in at for row in z] for i in range(across_x)]
    chunk = (8, x.shape[1] // tiles)
    vector, pay = call(
        part(weights_kernel, heads),
        given("hh", (8, 128), (tiles, *chunk)),
        given(
            "svvvvvvvhhhhv", me, mine, pair, sums, along, now, k, v, states, rows, row, cold, x
        ),
    )
    got = exchange(pay, ("ctx", "dp"), planes)
    grad_k, grad_v = call(
        part(finish_kernel, heads),
        given("hh", low(k.shape, BF16), low(v.shape, BF16)),
        given("svvhhhhhhh", me, mine, pair, vector, small, rows, gk, gvalue, k, v),
    )
    (pay,) = call(sum_kernel, given("v", (len(lines[0]), *chunk)), given("va", got, grad_k))
    got = exchange(pay, "ctx", lines)
    (pay,) = call(sum_kernel, given("v", (tiles, *chunk)), given("v", got))
    got = exchange(pay, ("ctx", "dp"), planes)
    first, second = call(
        place_kernel, given("vv", (heads, x.shape[1]), (heads, x.shape[1])), given("v", got)
    )
    return (grad_q[None], grad_k[None], grad_v[None], first.T, second.T)


def solution(mesh):
    split_rows = P("dp", "ctx", None)
    placed = (split_rows,) * 5 + (P("dp", "ctx"),) + (P(),) * 4
    return jax.shard_map(
        local,
        mesh=mesh,
        in_specs=placed,
        out_specs=(split_rows, split_rows, split_rows, P(), P()),
        check_vma=False,
    )
```
